512 devices in a mesh: dp: 16 (over x_lo, y, core), expert: 32 (over x_hi, z).
Axes of the slice: x: 4 (x_hi: 2, x_lo: 2; x = x_hi * 2 + x_lo), y: 4, z: 16, core: 2. Of those that a mesh axis runs over, the one named last changes fastest.
Arguments:
- grad_out: bfloat16 [1024, 7168], P('expert', 'dp'), may hold values from -6 to 6
- routes: int32 [1024, 8], P('expert'), may hold values from 0 to 31, all different within a row; in each aligned block of 32 rows (0 to 31, 32 to 63, ...) at most 12 rows name the same one
- gates: float32 [1024, 8], P('expert'), may hold values from 0.05 to 1
- hidden: bfloat16 [32, 384, 2048], P('expert', None, 'dp'), may hold values from -0.1796875 to 0.1796875
- w_down: bfloat16 [32, 2048, 7168], P('expert', 'dp'), may hold values from -0.125 to 0.125
Outputs:
- d_hidden: bfloat16 [32, 384, 2048], P('expert', None, 'dp')
- d_down: bfloat16 [32, 2048, 7168], P('expert', 'dp')
- d_gate: float32 [1024, 8], P('expert')
The draws below stay inside these ranges and needn't reach their ends.
Inputs may be any that keep to these rules, and one draw needn't show every extreme that they name: `routes`: each row names 8 different experts; within each aligned block of 32 rows (the tokens on one index of the expert axis) no expert is named by more than 12 rows.
All inputs are finite; a program needn't handle non-finite values.
Results may differ from the reference program's by a relative error of at most 0.0049.
Values may be sent and summed in bfloat16 or wider, within the bound.
No kernel may reach another device: no remote copies, remote signals or barrier semaphores. Data moves between devices by JAX's collectives and lax.ppermute only.
A program may use at most 128 MiB of HBM per device.

```python
import math
from functools import partial
import jax
import jax.numpy as jnp
import numpy as np
from jax import lax

D = 7168
F = 2048
TOP = 8
TOK = 32
EXPERTS = 32
CAP = 12
SLOTS = 384
TOKENS = 1024


def block_scale(rng, shape, shards, low, high):
    factor_of, own = 1.0, jax.random.fold_in(rng, 6)
    for position, parts in shards:
        steps = jnp.exp(jax.random.uniform(jax.random.fold_in(own, position), (parts,), jnp.float32, low / len(shards), high / len(shards)))
        factor_of = factor_of * jnp.repeat(steps, shape[position] // parts).reshape([-1 if axis == position else 1 for axis in range(len(shape))])
    return factor_of


def deal_out(rng, own, number, rows, number_of, top, limit, lean):
    sequence = jax.random.permutation(rng, number_of)
    packed, common = portions_of(number_of, rows * top, limit, lean, True), portions_of(number_of, rows * top, limit, lean, False)
    places = jnp.arange(number_of)

    def named(sizes, offset_by):
        used = int((sizes > 0).sum())
        fixed = max(1, used // 4)
        moved = fixed + (places - fixed + offset_by * (used - fixed)) % max(1, number_of - fixed)
        return jnp.zeros((number_of,), jnp.int32).at[sequence[jnp.where(places < fixed, places, moved)]].set(jnp.asarray(sizes, jnp.int32))

    sizes = jnp.where(number % 4 == 0, named(packed, number // 4), named(common, number - number // 4 - 1))
    mixed = jax.random.permutation(jax.random.fold_in(own, 3), number_of)
    giver, receiver = mixed[0:number_of // 2 * 2:2], mixed[1:number_of // 2 * 2:2]
    slack = jnp.minimum(sizes[giver] - 1, limit - sizes[receiver]) // 2
    slack = jnp.where((giver == sequence[0]) | (receiver == sequence[0]) | (sizes[receiver] == 0), 0, jnp.maximum(slack, 0))
    moved = jax.random.randint(jax.random.fold_in(own, 4), (number_of // 2,), 0, 1 << 20) % (slack + 1)
    sizes = sizes.at[giver].add(-moved).at[receiver].add(moved)
    labels = jnp.searchsorted(jnp.cumsum(sizes), jnp.arange(rows * top), side="right").astype(jnp.int32)
    listing = labels.reshape(top, rows).T
    listing = listing[jax.random.permutation(jax.random.fold_in(own, 1), rows)]
    offset_by = jax.random.randint(jax.random.fold_in(own, 2), (rows, 1), 0, top)
    return jnp.take_along_axis(listing, (jnp.arange(top)[None, :] + offset_by) % top, axis=1)


def portions_of(amount, total, reach, lean, full):
    weights = [(1 << 20) // math.isqrt(grade ** lean) + 1 for grade in range(1, amount + 1)]
    largest = reach if full else min(reach, max(-(-total // amount), total * weights[0] // sum(weights)))
    least = 1 if total - largest >= amount - 1 else 0
    given, spare = [largest] + [least] * (amount - 1), total - largest - least * (amount - 1)
    while spare > 0:
        movable = [i for i in range(1, amount) if given[i] < largest] or [i for i in range(1, amount) if given[i] < reach]
        pool, remaining = sum([weights[i] for i in movable]), spare
        for i in movable:
            extra = min(reach - given[i], max(1, remaining * weights[i] // pool), spare)
            given[i] = given[i] + extra
            spare = spare - extra
    return np.array(given)


def gaussian(own_key, shape, width, most, cuts=(), kind=jnp.bfloat16):
    level = block_scale(own_key, shape, cuts, -0.22, 0.18) if cuts else 1.0
    drawn = jax.random.normal(own_key, shape, jnp.float32) * width * level
    return jnp.minimum(jnp.maximum(drawn, -most), most).astype(kind)


def setup_inputs(seed: int = 0) -> dict:
    arg_keys = jax.random.split(jax.random.key(seed), 6)
    grad_out = gaussian(arg_keys[0], (TOKENS, D), 1.0, 6.0, ((0, 32), (1, 16)))
    routes_keys = jax.random.split(jax.random.fold_in(arg_keys[1], 1), TOKENS // TOK)
    routes_turns = jax.random.permutation(jax.random.fold_in(arg_keys[1], 3), TOKENS // TOK)
    routes = jax.vmap(lambda own, number: deal_out(jax.random.fold_in(arg_keys[1], 2), own, number, TOK, EXPERTS, TOP, CAP, 2))(routes_keys, routes_turns).reshape((TOKENS, TOP))
    gates = jnp.clip(jnp.exp(math.log(1.0) - 2.9957323 * jax.random.uniform(arg_keys[2], (TOKENS, TOP), jnp.float32) ** block_scale(arg_keys[2], (TOKENS, TOP), ((0, 32),), -0.2, 0.2)), 0.05, 1.0)
    hidden = gaussian(arg_keys[3], (EXPERTS, SLOTS, F), 0.03, 0.1796875, ((0, 32), (2, 16)))
    w_down = gaussian(arg_keys[4], (EXPERTS, F, D), F ** -0.5, 0.125, ((0, 32), (1, 16)))
    return dict(grad_out=grad_out, routes=routes, gates=gates, hidden=hidden, w_down=w_down)


def route_tables(routes, gates, experts, capacity):
    tokens_here = routes.shape[0]
    expert_ids = lax.broadcasted_iota(jnp.int32, (1, 1, experts), 2)
    chosen = (routes[:, :, None] == expert_ids).astype(jnp.int32)
    present = jnp.sum(chosen, axis=1)
    before = jnp.cumsum(present, axis=0) - present
    route_rank = jnp.sum(chosen * before[:, None, :], axis=2)
    slot_ids = lax.broadcasted_iota(jnp.int32, (1, 1, 1, capacity), 3)
    placed = chosen[:, :, :, None] * (route_rank[:, :, None, None] == slot_ids).astype(jnp.int32)
    tok_index = lax.broadcasted_iota(jnp.int32, (tokens_here, 1, 1, 1), 0)
    slot_token = jnp.sum(placed * tok_index, axis=(0, 1)).astype(jnp.int32)
    slot_gate = jnp.sum(placed.astype(jnp.float32) * gates[:, :, None, None], axis=(0, 1))
    return placed, slot_token, slot_gate


def reference(grad_out, routes, gates, hidden, w_down):
    sources = routes.shape[0] // TOK
    block_routes = routes.reshape(sources, TOK, TOP)
    block_gates = gates.reshape(sources, TOK, TOP)
    tables = jax.vmap(partial(route_tables, experts=EXPERTS, capacity=CAP))
    placed, slot_token, slot_gate = tables(block_routes, block_gates)
    offsets = (jnp.arange(sources, dtype=jnp.int32) * TOK)[:, None, None]
    global_token = (slot_token + offsets).astype(jnp.int32)

    def one_expert(expert):
        token_rows = global_token[:, expert, :].reshape(-1)
        row_gate = slot_gate[:, expert, :].reshape(-1)
        dispatched = (row_gate[:, None] * grad_out[token_rows].astype(jnp.float32)).astype(jnp.bfloat16)
        weight = w_down[expert]
        activations = hidden[expert]
        values = lax.dot_general(dispatched, weight, (((1,), (1,)), ((), ())), preferred_element_type=jnp.float32)
        gate_terms = jnp.sum(activations.astype(jnp.float32) * values, axis=1)
        gradient = lax.dot_general(activations, dispatched, (((0,), (0,)), ((), ())), preferred_element_type=jnp.float32)
        return values.astype(jnp.bfloat16), gradient.astype(jnp.bfloat16), gate_terms

    d_hidden, d_down, gate_terms = lax.map(one_expert, jnp.arange(EXPERTS, dtype=jnp.int32))
    returned = gate_terms.reshape(EXPERTS, sources, CAP).transpose(1, 0, 2)
    matched = jnp.sum(placed.astype(jnp.float32) * returned[:, None, None, :, :], axis=(3, 4))
    d_gate = (matched / block_gates).reshape(-1, TOP)
    return d_hidden, d_down, d_gate
```

```python
import functools

import jax
import jax.numpy as jnp
from jax import lax
from jax.experimental import pallas as pl
from jax.experimental.pallas import tpu as pltpu
from jax.sharding import PartitionSpec as P

F32 = jnp.float32
BF16 = jnp.bfloat16


def ranks(routes, experts):
    tokens, top = routes.shape
    ids = lax.broadcasted_iota(jnp.int32, (tokens, experts), 1)
    named = [routes[:, k : k + 1] == ids for k in range(top)]
    present = functools.reduce(jnp.logical_or, named)
    rows = lax.broadcasted_iota(jnp.int32, (tokens, tokens), 0)
    columns = lax.broadcasted_iota(jnp.int32, (tokens, tokens), 1)
    earlier = (columns < rows).astype(F32)
    before = jnp.dot(earlier, present.astype(F32), preferred_element_type=F32)
    return named, present, before


def pack_kernel(grad_ref, routes_ref, gates_ref, out_ref):
    experts, capacity, _ = out_ref.shape
    named, present, before = ranks(routes_ref[...], experts)
    gates = gates_ref[...]
    gate = jnp.zeros(present.shape, F32)
    for k, here in enumerate(named):
        gate = jnp.where(here, gates[:, k : k + 1], gate)
    grad = grad_ref[...]
    for c in range(capacity):
        placed = jnp.logical_and(present, before == c).astype(F32)
        chosen = placed.T.astype(BF16)
        row_gate = jnp.sum(placed * gate, axis=0, keepdims=True)
        rows = jnp.dot(chosen, grad, preferred_element_type=F32)
        out_ref[:, c, :] = (row_gate.T * rows).astype(BF16)


def values_kernel(steps, disp_ref, weight_ref, hidden_ref, dhid_ref, gate_ref, total):
    step = pl.program_id(0)

    @pl.when(step == 0)
    def _():
        total[...] = jnp.zeros_like(total)

    total[...] += jnp.dot(weight_ref[...], disp_ref[...], preferred_element_type=F32)

    @pl.when(step == steps - 1)
    def _():
        values = total[...].T
        dhid_ref[...] = values.astype(BF16)
        terms = jnp.sum(hidden_ref[...].astype(F32) * values, axis=1, keepdims=True)
        sources, capacity = gate_ref.shape
        slots = values.shape[0]
        slot = lax.broadcasted_iota(jnp.int32, (slots, capacity), 0)
        rank = lax.broadcasted_iota(jnp.int32, (slots, capacity), 1)
        spread = jnp.where(slot % capacity == rank, terms, 0.0)
        owner = lax.broadcasted_iota(jnp.int32, (sources, slots), 0)
        member = lax.broadcasted_iota(jnp.int32, (sources, slots), 1)
        fold = (member // capacity == owner).astype(F32)
        gate_ref[...] = jnp.dot(
            fold, spread, preferred_element_type=F32, precision=lax.Precision.HIGHEST
        )


def down_kernel(disp_ref, hidden_ref, out_ref, flipped):
    @pl.when(pl.program_id(0) == 0)
    def _():
        flipped[...] = hidden_ref[...].astype(F32).T.astype(BF16)

    out_ref[...] = lax.dot_general(
        flipped[...],
        disp_ref[...],
        (((1,), (1,)), ((), ())),
        preferred_element_type=F32,
    ).astype(BF16)


def gate_kernel(parts_ref, routes_ref, gates_ref, out_ref):
    _, experts, capacity = parts_ref.shape
    named, present, before = ranks(routes_ref[...], experts)
    terms = jnp.sum(parts_ref[...], axis=0).T
    matched = jnp.zeros(present.shape, F32)
    for c in range(capacity):
        here = jnp.logical_and(present, before == c)
        matched = jnp.where(here, terms[c : c + 1, :], matched)
    rows = [
        jnp.sum(jnp.where(here, matched, 0.0), axis=1, keepdims=True) for here in named
    ]
    column = lax.broadcasted_iota(jnp.int32, out_ref.shape, 1)
    total = jnp.zeros(out_ref.shape, F32)
    for k, row in enumerate(rows):
        total = jnp.where(column == k, row, total)
    out_ref[...] = total / gates_ref[...]


def whole():
    return pl.BlockSpec(memory_space=pltpu.VMEM)


def on_device(grad_out, routes, gates, hidden, w_down):
    experts, parts = lax.axis_size("expert"), lax.axis_size("dp")
    _, slots, units = hidden.shape
    width = w_down.shape[2]
    capacity = slots // experts
    share = grad_out.shape[1]

    scaled = pl.pallas_call(
        pack_kernel,
        out_shape=jax.ShapeDtypeStruct((experts, capacity, share), BF16),
        in_specs=[whole()] * 3,
        out_specs=whole(),
        name="pack",
    )(grad_out, routes, gates)
    arrived = lax.all_to_all(scaled, "expert", split_axis=0, concat_axis=0, tiled=True)
    flipped = arrived.reshape(slots, share).T
    dispatched = lax.all_gather(flipped, "dp", axis=0, tiled=True)

    depth = 1024
    steps = width // depth
    activations, weight = hidden[0], w_down[0]
    d_hidden, terms = pl.pallas_call(
        functools.partial(values_kernel, steps),
        grid=(steps,),
        out_shape=(
            jax.ShapeDtypeStruct((slots, units), BF16),
            jax.ShapeDtypeStruct((experts, capacity), F32),
        ),
        in_specs=[
            pl.BlockSpec((depth, slots), lambda i: (i, 0)),
            pl.BlockSpec((units, depth), lambda i: (0, i)),
            pl.BlockSpec((slots, units), lambda i: (0, 0)),
        ],
        out_specs=(
            pl.BlockSpec((slots, units), lambda i: (0, 0)),
            pl.BlockSpec((experts, capacity), lambda i: (0, 0)),
        ),
        scratch_shapes=[pltpu.VMEM((units, slots), F32)],
        cost_estimate=pl.CostEstimate(
            flops=2 * slots * units * width, bytes_accessed=7500000, transcendentals=0
        ),
        name="values",
    )(dispatched, weight, activations)
    d_down = pl.pallas_call(
        down_kernel,
        grid=(steps,),
        out_shape=jax.ShapeDtypeStruct((units, width), BF16),
        in_specs=[
            pl.BlockSpec((depth, slots), lambda i: (i, 0)),
            pl.BlockSpec((slots, units), lambda i: (0, 0)),
        ],
        out_specs=pl.BlockSpec((units, depth), lambda i: (0, i)),
        scratch_shapes=[pltpu.VMEM((units, slots), BF16)],
        cost_estimate=pl.CostEstimate(
            flops=2 * slots * units * width, bytes_accessed=7500000, transcendentals=0
        ),
        name="down",
    )(dispatched, activations)

    returned = lax.all_to_all(terms, "expert", split_axis=0, concat_axis=0, tiled=True)
    copies = jnp.broadcast_to(returned[None], (parts, experts, capacity))
    everyone = lax.all_to_all(copies, "dp", split_axis=0, concat_axis=0, tiled=True)
    d_gate = pl.pallas_call(
        gate_kernel,
        out_shape=jax.ShapeDtypeStruct(gates.shape, F32),
        in_specs=[whole()] * 3,
        out_specs=whole(),
        name="match",
    )(everyone, routes, gates)
    return (d_hidden[None], d_down[None], d_gate)


def solution(mesh):
    in_specs = (
        P("expert", "dp"),
        P("expert", None),
        P("expert", None),
        P("expert", None, "dp"),
        P("expert", "dp", None),
    )
    out_specs = (P("expert", None, "dp"), P("expert", "dp", None), P("expert", None))
    return jax.shard_map(
        on_device, mesh=mesh, in_specs=in_specs, out_specs=out_specs, check_vma=False
    )
```

```python
import functools

import jax
import jax.numpy as jnp
from jax import lax
from jax.experimental import pallas as pl
from jax.experimental.pallas import tpu as pltpu
from jax.sharding import Mesh, PartitionSpec as P

F32 = jnp.float32
BF16 = jnp.bfloat16
LANES = 128


def ranks(routes, experts):
    top, tokens = routes.shape
    ids = lax.broadcasted_iota(jnp.int32, (experts, tokens), 0)
    named = [routes[k : k + 1, :] == ids for k in range(top)]
    present = functools.reduce(jnp.logical_or, named)
    rows = lax.broadcasted_iota(jnp.int32, (tokens, tokens), 0)
    columns = lax.broadcasted_iota(jnp.int32, (tokens, tokens), 1)
    earlier = (rows < columns).astype(F32)
    before = jnp.dot(present.astype(F32), earlier, preferred_element_type=F32)
    return named, present, before


def pack_kernel(grad_ref, routes_ref, gates_ref, out_ref):
    experts, rows, _ = out_ref.shape
    share = grad_ref.shape[1]
    pair = 2 * share // LANES
    named, present, before = ranks(routes_ref[...], experts)
    gates = gates_ref[...]
    gate = jnp.zeros(present.shape, F32)
    for k, here in enumerate(named):
        gate = jnp.where(here, gates[k : k + 1, :], gate)
    grad = grad_ref[...]

    def slot(c):
        placed = jnp.logical_and(present, before == c).astype(F32)
        row_gate = jnp.sum(placed * gate, axis=1, keepdims=True)
        return row_gate * jnp.dot(
            placed.astype(BF16), grad, preferred_element_type=F32
        )

    for p in range(rows // pair):
        both = jnp.concatenate([slot(2 * p), slot(2 * p + 1)], axis=1).astype(BF16)
        for i in range(pair):
            out_ref[:, pair * p + i, :] = both[:, LANES * i : LANES * (i + 1)]


def unpack_kernel(in_ref, out_ref):
    sources, rows, _ = in_ref.shape
    share, slots = out_ref.shape
    pair = 2 * share // LANES
    group = LANES // sources
    for g in range(slots // LANES):
        parts = []
        for p in range(g * group // 2, (g + 1) * group // 2):
            both = jnp.concatenate(
                [in_ref[:, pair * p + i, :].astype(F32) for i in range(pair)], axis=1
            )
            parts += [both[:, :share], both[:, share:]]
        block = jnp.concatenate(parts, axis=0)
        out_ref[:, LANES * g : LANES * (g + 1)] = block.T.astype(BF16)


def reorder(slots, sources, rank_slowest_rows):
    capacity = slots // sources
    rows = lax.broadcasted_iota(jnp.int32, (slots, slots), 0)
    columns = lax.broadcasted_iota(jnp.int32, (slots, slots), 1)
    if rank_slowest_rows:
        rows, columns = columns, rows
    matches = (rows % capacity) * sources + rows // capacity == columns
    return matches.astype(F32).astype(BF16)


def split_kernel(sources, core_ref, weight_ref, hidden_ref, keep_ref, send_ref):
    blocks = keep_ref.shape[0] - 1
    share = weight_ref.shape[1] // (2 * blocks)
    slots = hidden_ref.shape[0]
    order = reorder(slots, sources, False)
    flipped = lax.dot_general(
        hidden_ref[...], order, (((0,), (0,)), ((), ())), preferred_element_type=F32
    ).astype(BF16)
    for ref in (keep_ref, send_ref):
        ref[:, :, ref.shape[2] - LANES :] = jnp.zeros((*ref.shape[:2], LANES), BF16)
        ref[blocks, :, :slots] = flipped

    def store(first, second):
        for j in range(blocks):
            both = weight_ref[:, 2 * share * j : 2 * share * (j + 1)]
            first[j, :, :share] = both[:, :share]
            second[j, :, :share] = both[:, share:]

    pl.when(core_ref[0] == 0)(lambda: store(keep_ref, send_ref))
    pl.when(core_ref[0] != 0)(lambda: store(send_ref, keep_ref))


def values_kernel(
    steps,
    disp_ref,
    keep_ref,
    other_ref,
    keep_hidden_ref,
    other_hidden_ref,
    mine_ref,
    theirs_ref,
    gate_ref,
    total,
):
    step = pl.program_id(0)

    @pl.when(step == 0)
    def _():
        total[...] = jnp.zeros_like(total)

    weight = jnp.concatenate([keep_ref[0], other_ref[0]], axis=0)
    share = disp_ref.shape[1]
    total[...] += jnp.dot(weight[:, :share], disp_ref[0], preferred_element_type=F32)

    @pl.when(step == steps - 1)
    def _():
        values = total[...]
        units = values.shape[0] // 2
        slots = values.shape[1]
        mine_ref[...] = values[:units]
        theirs_ref[...] = values[units:]
        hidden = jnp.concatenate([keep_hidden_ref[0], other_hidden_ref[0]], axis=0)
        terms = jnp.sum(
            hidden[:, :slots].astype(F32) * values, axis=0, keepdims=True
        )
        sources, capacity = gate_ref.shape
        owner = lax.broadcasted_iota(jnp.int32, (sources, slots), 0)
        member = lax.broadcasted_iota(jnp.int32, (sources, slots), 1)
        spread = jnp.where(member % sources == owner, terms, 0.0)
        slot = lax.broadcasted_iota(jnp.int32, (slots, capacity), 0)
        rank = lax.broadcasted_iota(jnp.int32, (slots, capacity), 1)
        fold = (slot // sources == rank).astype(F32)
        gate_ref[...] = jnp.dot(
            spread, fold, preferred_element_type=F32, precision=lax.Precision.HIGHEST
        )


def down_kernel(disp_ref, keep_hidden_ref, other_hidden_ref, mine_ref, theirs_ref):
    slots = disp_ref.shape[2]
    hidden = jnp.concatenate([keep_hidden_ref[0], other_hidden_ref[0]], axis=0)
    product = lax.dot_general(
        hidden[:, :slots],
        disp_ref[0],
        (((1,), (1,)), ((), ())),
        preferred_element_type=F32,
    ).astype(BF16)
    units, share = mine_ref.shape[1], product.shape[1]
    for ref, rows in ((mine_ref, product[:units]), (theirs_ref, product[units:])):
        ref[0, :, ref.shape[2] - LANES :] = jnp.zeros((units, LANES), BF16)
        ref[0, :, :share] = rows


def finish_kernel(
    sources, core_ref, mine_ref, got_ref, values_ref, got_values_ref, down_ref, dhid_ref
):
    share = down_ref.shape[1] // 2

    def store(first, second):
        down_ref[:, :share] = first[0, :, :share]
        down_ref[:, share:] = second[0, :, :share]

    pl.when(core_ref[0] == 0)(lambda: store(mine_ref, got_ref))
    pl.when(core_ref[0] != 0)(lambda: store(got_ref, mine_ref))

    @pl.when(pl.program_id(0) == 0)
    def _():
        values = (values_ref[...] + got_values_ref[...]).T.astype(BF16)
        order = reorder(values.shape[0], sources, False)
        dhid_ref[...] = jnp.dot(order, values, preferred_element_type=F32).astype(BF16)


def gate_kernel(capacity, parts_ref, routes_ref, gates_ref, out_ref):
    top, tokens = out_ref.shape
    experts = parts_ref.shape[1] * LANES // capacity
    named, present, before = ranks(routes_ref[...], experts)
    terms = jnp.sum(parts_ref[...], axis=0)
    group = LANES // experts
    matched = jnp.zeros(present.shape, F32)
    for c in range(capacity):
        start = (c % group) * experts
        row = terms[c // group : c // group + 1, start : start + experts]
        spread = jnp.broadcast_to(row, (8, experts)).T[:, :1]
        here = jnp.logical_and(present, before == c)
        matched = jnp.where(here, spread, matched)
    total = [jnp.sum(jnp.where(n, matched, 0.0), axis=0, keepdims=True) for n in named]
    out_ref[...] = jnp.concatenate(total, axis=0) / gates_ref[...]


def whole():
    return pl.BlockSpec(memory_space=pltpu.VMEM)


def scalar():
    return pl.BlockSpec(memory_space=pltpu.SMEM)


def limit(mib):
    return pltpu.CompilerParams(vmem_limit_bytes=mib * 2**20)


def cost(flops, moved):
    return pl.CostEstimate(flops=flops, bytes_accessed=moved, transcendentals=0)


def swap_all(x, axis):
    return lax.all_to_all(x, axis, split_axis=0, concat_axis=0, tiled=True)


def on_device(grad_out, routes, gates, hidden, w_down):
    experts, chips = lax.axis_size("expert"), lax.axis_size("chip")
    _, slots, units = hidden.shape
    width = w_down.shape[2]
    capacity = slots // experts
    share = grad_out.shape[1]
    rows = capacity * share // LANES
    core = lax.axis_index("core").astype(jnp.int32).reshape(1)
    routes, gates = routes.T, gates.T

    def to_other_core(x):
        return lax.ppermute(x, "core", [(0, 1), (1, 0)])

    packed = pl.pallas_call(
        pack_kernel,
        out_shape=jax.ShapeDtypeStruct((experts, rows, LANES), BF16),
        in_specs=[whole()] * 3,
        out_specs=whole(),
        compiler_params=limit(8),
        name="pack",
    )(grad_out, routes, gates)
    arrived = swap_all(packed, "expert")

    padded = -(-share // LANES) * LANES
    half = jax.ShapeDtypeStruct((chips + 1, units, padded), BF16)
    keep, send = pl.pallas_call(
        functools.partial(split_kernel, experts),
        out_shape=(half, half),
        in_specs=[scalar(), whole(), whole()],
        out_specs=(whole(), whole()),
        cost_estimate=cost(2 * units * slots * slots, 2 * 2 * units * width),
        compiler_params=limit(16),
        name="split",
    )(core, w_down[0], hidden[0])
    other = to_other_core(send)

    own = pl.pallas_call(
        unpack_kernel,
        out_shape=jax.ShapeDtypeStruct((share, slots), BF16),
        in_specs=[whole()],
        out_specs=whole(),
        compiler_params=limit(8),
        name="unpack",
    )(arrived)
    dispatched = swap_all(jnp.broadcast_to(own[None], (chips, share, slots)), "chip")

    block = pl.BlockSpec((1, share, slots), lambda i: (i, 0, 0))
    columns = pl.BlockSpec((1, units, padded), lambda i: (i, 0, 0))
    last = pl.BlockSpec((1, units, padded), lambda i: (chips, 0, 0))
    table = pl.BlockSpec((units, slots), lambda i: (0, 0))
    flops = 2 * slots * units * width
    mine, theirs, terms = pl.pallas_call(
        functools.partial(values_kernel, chips),
        grid=(chips,),
        out_shape=(
            jax.ShapeDtypeStruct((units, slots), F32),
            jax.ShapeDtypeStruct((units, slots), F32),
            jax.ShapeDtypeStruct((experts, capacity), F32),
        ),
        in_specs=[block, columns, columns, last, last],
        out_specs=(table, table, pl.BlockSpec((experts, capacity), lambda i: (0, 0))),
        scratch_shapes=[pltpu.VMEM((2 * units, slots), F32)],
        cost_estimate=cost(flops, slots * width + 2 * units * width),
        compiler_params=limit(12),
        name="values",
    )(dispatched, keep, other, keep, other)
    returned = swap_all(terms, "expert")

    part = jax.ShapeDtypeStruct((chips, units, padded), BF16)
    down, down_theirs = pl.pallas_call(
        down_kernel,
        grid=(chips,),
        out_shape=(part, part),
        in_specs=[block, last, last],
        out_specs=(columns, columns),
        cost_estimate=cost(flops, slots * width + 2 * units * width),
        compiler_params=limit(12),
        name="down",
    )(dispatched, keep, other)
    returned, theirs, down_theirs = lax.optimization_barrier(
        (returned, theirs, down_theirs)
    )
    got_down = to_other_core(down_theirs)
    got = to_other_core(theirs)
    d_down, d_hidden = pl.pallas_call(
        functools.partial(finish_kernel, experts),
        grid=(chips,),
        out_shape=(
            jax.ShapeDtypeStruct((units, width), BF16),
            jax.ShapeDtypeStruct((slots, units), BF16),
        ),
        in_specs=[scalar(), columns, columns, table, table],
        out_specs=(
            pl.BlockSpec((units, 2 * share), lambda i: (0, i)),
            pl.BlockSpec((slots, units), lambda i: (0, 0)),
        ),
        cost_estimate=cost(2 * units * slots * slots, 4 * units * width),
        compiler_params=limit(12),
        name="finish",
    )(core, down, got_down, mine, got)

    flat = returned.T.reshape(1, slots // LANES, LANES)
    copies = jnp.broadcast_to(flat, (2 * chips, *flat.shape[1:]))
    everyone = swap_all(copies, ("chip", "core"))
    everyone, _ = lax.optimization_barrier((everyone, d_hidden))
    d_gate = pl.pallas_call(
        functools.partial(gate_kernel, capacity),
        out_shape=jax.ShapeDtypeStruct(gates.shape, F32),
        in_specs=[whole()] * 3,
        out_specs=whole(),
        compiler_params=limit(4),
        name="match",
    )(everyone, routes, gates)
    return (d_hidden[None], d_down[None], d_gate.T)


def solution(mesh):
    parts, experts = mesh.devices.shape
    devices = mesh.devices.reshape(parts // 2, 2, experts)
    finer = Mesh(devices, ("chip", "core", "expert"))
    dp = ("chip", "core")
    in_specs = (
        P("expert", dp),
        P("expert", None),
        P("expert", None),
        P("expert", None, dp),
        P("expert", dp, None),
    )
    out_specs = (P("expert", None, dp), P("expert", dp, None), P("expert", None))
    return jax.shard_map(
        on_device, mesh=finer, in_specs=in_specs, out_specs=out_specs, check_vma=False
    )
```

```python
import functools

import jax
import jax.numpy as jnp
from jax import lax
from jax.experimental import pallas as pl
from jax.experimental.pallas import tpu as pltpu
from jax.sharding import Mesh, PartitionSpec as P

F32 = jnp.float32
BF16 = jnp.bfloat16
LANES = 128


def ranks(routes, experts):
    top, tokens = routes.shape
    ids = lax.broadcasted_iota(jnp.int32, (experts, tokens), 0)
    named = [routes[k : k + 1, :] == ids for k in range(top)]
    present = functools.reduce(jnp.logical_or, named)
    rows = lax.broadcasted_iota(jnp.int32, (tokens, tokens), 0)
    columns = lax.broadcasted_iota(jnp.int32, (tokens, tokens), 1)
    earlier = (rows < columns).astype(F32)
    before = jnp.dot(present.astype(F32), earlier, preferred_element_type=F32)
    return named, present, before


def pack_kernel(grad_ref, routes_ref, gates_ref, out_ref):
    experts, lines, length = out_ref.shape
    grad = grad_ref[...]
    fitting = length // grad.shape[1]
    named, present, before = ranks(routes_ref[...], experts)
    gates = gates_ref[...]
    gate = jnp.zeros(present.shape, F32)
    for k, here in enumerate(named):
        gate = jnp.where(here, gates[k : k + 1, :], gate)

    def slot(c):
        placed = jnp.logical_and(present, before == c).astype(F32)
        row_gate = jnp.sum(placed * gate, axis=1, keepdims=True)
        return row_gate * jnp.dot(
            placed.astype(BF16), grad, preferred_element_type=F32
        )

    for line in range(lines):
        rows = [slot(fitting * line + i) for i in range(fitting)]
        out_ref[:, line, :] = jnp.concatenate(rows, axis=1).astype(BF16)


def unpack_kernel(in_ref, out_ref, flipped, done):
    sources, lines, length = in_ref.shape
    share, slots = flipped.shape
    fitting = length // share
    rows = [in_ref[:, line, :].astype(F32) for line in range(lines)]
    group = LANES // sources
    for g in range(slots // LANES):
        parts = []
        for c in range(g * group, (g + 1) * group):
            start = share * (c % fitting)
            parts.append(rows[c // fitting][:, start : start + share])
        block = jnp.concatenate(parts, axis=0)
        flipped[:, LANES * g : LANES * (g + 1)] = block.T.astype(BF16)
    copies = [
        pltpu.make_async_copy(flipped, out_ref.at[i], done.at[i])
        for i in range(out_ref.shape[0])
    ]
    for copy in copies:
        copy.start()
    for copy in copies:
        copy.wait()


def split_kernel(
    sources, core_ref, weight_ref, hidden_ref, keep_ref, send_ref, order_ref
):
    blocks = keep_ref.shape[0] - 1
    share = weight_ref.shape[1] // (2 * blocks)
    slots = hidden_ref.shape[0]
    capacity = slots // sources
    rows = lax.broadcasted_iota(jnp.int32, (slots, slots), 0)
    columns = lax.broadcasted_iota(jnp.int32, (slots, slots), 1)
    matches = (rows % capacity) * sources + rows // capacity == columns
    order = matches.astype(F32).astype(BF16)
    order_ref[...] = order
    flipped = lax.dot_general(
        hidden_ref[...], order, (((0,), (0,)), ((), ())), preferred_element_type=F32
    ).astype(BF16)
    for ref in (keep_ref, send_ref):
        ref[:, :, ref.shape[2] - LANES :] = jnp.zeros((*ref.shape[:2], LANES), BF16)
        ref[blocks, :, :slots] = flipped

    def store(first, second):
        for j in range(blocks):
            both = weight_ref[:, 2 * share * j : 2 * share * (j + 1)]
            first[j, :, :share] = both[:, :share]
            second[j, :, :share] = both[:, share:]

    pl.when(core_ref[0] == 0)(lambda: store(keep_ref, send_ref))
    pl.when(core_ref[0] != 0)(lambda: store(send_ref, keep_ref))


def values_kernel(
    far, disp_ref, keep_ref, other_ref, mine_ref, theirs_ref, gate_ref, weight, done
):
    blocks, share, slots = disp_ref.shape
    units = mine_ref.shape[0]
    copies = [
        [
            pltpu.make_async_copy(ref.at[j], weight.at[j, half], done.at[j, half])
            for half, ref in enumerate((keep_ref, other_ref))
        ]
        for j in range(blocks + 1)
    ]
    for pair in copies:
        for copy in pair:
            copy.start()
    values = jnp.zeros((2 * units, slots), F32)
    for j in range(blocks):
        for copy in copies[j]:
            copy.wait()
        both = weight[j].reshape(2 * units, weight.shape[3])[:, :share]
        values += jnp.dot(both, disp_ref[j], preferred_element_type=F32)
    for copy in copies[blocks]:
        copy.wait()
    hidden = weight[blocks].reshape(2 * units, weight.shape[3])[:, :slots]
    terms = jnp.sum(hidden.astype(F32) * values, axis=0, keepdims=True)
    mine_ref[...] = values[:units]
    theirs_ref[...] = values[units:]

    near, width = gate_ref.shape
    member = lax.broadcasted_iota(jnp.int32, (near, slots), 1)
    owner = lax.broadcasted_iota(jnp.int32, (near, slots), 0)
    spread = jnp.where(member % near == owner, terms, 0.0)
    slot = lax.broadcasted_iota(jnp.int32, (slots, width), 0) // near
    column = lax.broadcasted_iota(jnp.int32, (slots, width), 1)
    fold = (slot % far) * (width // far) + slot // far == column
    gate_ref[...] = jnp.dot(
        spread,
        fold.astype(F32),
        preferred_element_type=F32,
        precision=lax.Precision.HIGHEST,
    )


def down_kernel(
    disp_ref, keep_hidden_ref, other_hidden_ref, values_ref, mine_ref, theirs_ref
):
    blocks, share, slots = disp_ref.shape
    units = values_ref.shape[0]
    hidden = jnp.concatenate([keep_hidden_ref[0], other_hidden_ref[0]], axis=0)
    hidden = hidden[:, :slots]
    for ref in (mine_ref, theirs_ref):
        ref[:, :, ref.shape[2] - LANES :] = jnp.zeros((*ref.shape[:2], LANES), BF16)
    for j in range(blocks):
        product = lax.dot_general(
            hidden, disp_ref[j], (((1,), (1,)), ((), ())), preferred_element_type=F32
        ).astype(BF16)
        mine_ref[j, :, :share] = product[:units]
        theirs_ref[j, :, :share] = product[units:]
    values = values_ref[...]
    high = values.astype(BF16)
    theirs_ref[blocks, :, :slots] = high
    theirs_ref[blocks + 1, :, :slots] = (values - high.astype(F32)).astype(BF16)


def finish_kernel(
    core_ref,
    mine_ref,
    got_ref,
    values_ref,
    order_ref,
    down_ref,
    dhid_ref,
):
    step, blocks = pl.program_id(0), mine_ref.shape[0]
    last = got_ref.shape[0] - 2
    share = down_ref.shape[1] // (2 * blocks)
    slots = values_ref.shape[1]

    def store(mine_first):
        for j in range(blocks):
            start = 2 * share * j
            both = [mine_ref[j, :, :share], got_ref[step * blocks + j, :, :share]]
            both = both if mine_first else both[::-1]
            down_ref[:, start : start + 2 * share] = jnp.concatenate(both, axis=1)

    pl.when(core_ref[0] == 0)(lambda: store(True))
    pl.when(core_ref[0] != 0)(lambda: store(False))

    @pl.when(step == 0)
    def _():
        high = got_ref[last, :, :slots].astype(F32)
        low = got_ref[last + 1, :, :slots].astype(F32)
        values = (values_ref[...] + (high + low)).T.astype(BF16)
        dhid_ref[...] = jnp.dot(
            order_ref[...], values, preferred_element_type=F32
        ).astype(BF16)


def gate_kernel(near, capacity, parts_ref, routes_ref, gates_ref, out_ref):
    experts = parts_ref.shape[1] * LANES // capacity
    named, present, before = ranks(routes_ref[...], experts)
    terms = jnp.sum(parts_ref[...], axis=0)
    matched = jnp.zeros(present.shape, F32)
    for c in range(capacity):
        pieces = []
        for far in range(experts // near):
            line, lane = divmod((far * capacity + c) * near, LANES)
            pieces.append(terms[line : line + 1, lane : lane + near])
        row = jnp.concatenate(pieces, axis=1)
        spread = jnp.broadcast_to(row, (8, experts)).T[:, :1]
        here = jnp.logical_and(present, before == c)
        matched = jnp.where(here, spread, matched)
    total = [jnp.sum(jnp.where(n, matched, 0.0), axis=0, keepdims=True) for n in named]
    out_ref[...] = jnp.concatenate(total, axis=0) / gates_ref[...]


def whole():
    return pl.BlockSpec(memory_space=pltpu.VMEM)


def scalar():
    return pl.BlockSpec(memory_space=pltpu.SMEM)


def stays():
    return pl.BlockSpec(memory_space=pltpu.HBM)


def in_hbm(x):
    return pltpu.with_memory_space_constraint(x, pltpu.HBM)


def in_vmem(x):
    return pltpu.with_memory_space_constraint(x, pltpu.VMEM)


def limit(mib):
    return pltpu.CompilerParams(vmem_limit_bytes=mib * 2**20)


def cost(flops, moved):
    return pl.CostEstimate(flops=flops, bytes_accessed=moved, transcendentals=0)


def swap_all(x, axis):
    return lax.all_to_all(x, axis, split_axis=0, concat_axis=0, tiled=True)


def on_device(grad_out, routes, gates, hidden, w_down):
    near, far = lax.axis_size("near"), lax.axis_size("far")
    experts, chips = near * far, lax.axis_size("chip")
    _, slots, units = hidden.shape
    width = w_down.shape[2]
    capacity = slots // experts
    share = grad_out.shape[1]
    padded = -(-share // LANES) * LANES
    core = lax.axis_index("core").astype(jnp.int32).reshape(1)
    routes, gates = routes.T, gates.T
    bf16 = functools.partial(pltpu.HBM, dtype=BF16)
    f32 = functools.partial(pltpu.HBM, dtype=F32)

    def to_other_core(x):
        return lax.ppermute(x, "core", [(0, 1), (1, 0)])

    packed = pl.pallas_call(
        pack_kernel,
        out_shape=jax.ShapeDtypeStruct((experts, 2, capacity * share // 2), BF16),
        in_specs=[whole()] * 3,
        out_specs=whole(),
        name="pack",
    )(grad_out, routes, gates)
    arrived = swap_all(packed, ("far", "near"))

    half = bf16((chips + 1, units, padded))
    keep, send, order = pl.pallas_call(
        functools.partial(split_kernel, experts),
        out_shape=(half, half, bf16((slots, slots))),
        in_specs=[scalar(), whole(), whole()],
        out_specs=(whole(),) * 3,
        cost_estimate=cost(2 * units * slots * slots, 2 * 2 * units * width),
        name="split",
    )(core, w_down[0], hidden[0])
    other = in_hbm(to_other_core(send))
    keep, order = in_hbm(keep), in_hbm(order)

    copies = pl.pallas_call(
        unpack_kernel,
        out_shape=bf16((chips, share, slots)),
        in_specs=[whole()],
        out_specs=pl.BlockSpec(memory_space=pl.ANY),
        scratch_shapes=[
            pltpu.VMEM((share, slots), BF16),
            pltpu.SemaphoreType.DMA((chips,)),
        ],
        compiler_params=limit(8),
        name="unpack",
    )(arrived)
    dispatched = in_vmem(swap_all(copies, "chip"))

    flops = 2 * slots * units * width
    mine, theirs, terms = pl.pallas_call(
        functools.partial(values_kernel, far),
        out_shape=(
            f32((units, slots)),
            f32((units, slots)),
            jax.ShapeDtypeStruct((near, far * capacity), F32),
        ),
        in_specs=[whole(), stays(), stays()],
        out_specs=(whole(),) * 3,
        scratch_shapes=[
            pltpu.VMEM((chips + 1, 2, units, padded), BF16),
            pltpu.SemaphoreType.DMA((chips + 1, 2)),
        ],
        compiler_params=limit(16),
        cost_estimate=cost(flops, slots * width + 2 * units * width),
        name="values",
    )(dispatched, keep, other)
    returned = swap_all(terms, "near")
    theirs = in_hbm(theirs)

    last = pl.BlockSpec((1, units, padded), lambda i: (chips, 0, 0))
    table = pl.BlockSpec((units, slots), lambda i: (0, 0))
    down, beside = pl.pallas_call(
        down_kernel,
        grid=(1,),
        out_shape=(
            bf16((chips, units, padded)),
            bf16((chips + 2, units, padded)),
        ),
        in_specs=[whole(), last, last, table],
        out_specs=(whole(), whole()),
        compiler_params=limit(16),
        cost_estimate=cost(flops, slots * width + 2 * units * width),
        name="down",
    )(dispatched, keep, other, theirs)
    returned, beside = lax.optimization_barrier((returned, beside))
    got = in_vmem(to_other_core(beside))
    down, mine = in_hbm(down), in_hbm(mine)

    steps = 4
    some = pl.BlockSpec((chips // steps, units, padded), lambda i: (i, 0, 0))

    d_down, d_hidden = pl.pallas_call(
        finish_kernel,
        grid=(steps,),
        out_shape=(
            jax.ShapeDtypeStruct((units, width), BF16),
            jax.ShapeDtypeStruct((slots, units), BF16),
        ),
        in_specs=[
            scalar(),
            some,
            whole(),
            table,
            pl.BlockSpec((slots, slots), lambda i: (0, 0)),
        ],
        out_specs=(
            pl.BlockSpec((units, width // steps), lambda i: (0, i)),
            pl.BlockSpec((slots, units), lambda i: (0, 0)),
        ),
        compiler_params=limit(16),
        cost_estimate=cost(2 * units * slots * slots, 4 * units * width),
        name="finish",
    )(core, down, got, mine, order)

    returned = returned.reshape(near, far, capacity).transpose(1, 2, 0)
    returned = swap_all(returned.reshape(far, near * capacity), "far")
    flat = returned.reshape(1, slots // LANES, LANES)
    flat = jnp.broadcast_to(flat, (2 * chips, *flat.shape[1:]))
    everyone = swap_all(flat, ("chip", "core"))
    everyone, _ = lax.optimization_barrier((everyone, d_hidden))
    d_gate = pl.pallas_call(
        functools.partial(gate_kernel, near, capacity),
        out_shape=jax.ShapeDtypeStruct(gates.shape, F32),
        in_specs=[whole()] * 3,
        out_specs=whole(),
        compiler_params=limit(4),
        name="match",
    )(everyone, routes, gates)
    return (d_hidden[None], d_down[None], d_gate.T)


def solution(mesh):
    parts, experts = mesh.devices.shape
    devices = mesh.devices.reshape(parts // 2, 2, 2, experts // 2)
    finer = Mesh(devices, ("chip", "core", "far", "near"))
    dp, expert = ("chip", "core"), ("far", "near")
    in_specs = (
        P(expert, dp),
        P(expert, None),
        P(expert, None),
        P(expert, None, dp),
        P(expert, dp, None),
    )
    out_specs = (P(expert, None, dp), P(expert, dp, None), P(expert, None))
    return jax.shard_map(
        on_device, mesh=finer, in_specs=in_specs, out_specs=out_specs, check_vma=False
    )
```

```python
import functools

import jax
import jax.numpy as jnp
from jax import lax
from jax.experimental import pallas as pl
from jax.experimental.pallas import tpu as pltpu
from jax.sharding import Mesh, PartitionSpec as P

F32 = jnp.float32
BF16 = jnp.bfloat16
LANES = 128


def ranks(routes, experts):
    top, tokens = routes.shape
    ids = lax.broadcasted_iota(jnp.int32, (experts, tokens), 0)
    named = [routes[k : k + 1, :] == ids for k in range(top)]
    present = functools.reduce(jnp.logical_or, named)
    rows = lax.broadcasted_iota(jnp.int32, (tokens, tokens), 0)
    columns = lax.broadcasted_iota(jnp.int32, (tokens, tokens), 1)
    earlier = (rows < columns).astype(F32)
    before = jnp.dot(present.astype(F32), earlier, preferred_element_type=F32)
    return named, present, before


def pack_kernel(grad_ref, routes_ref, gates_ref, out_ref):
    experts, lines, length = out_ref.shape
    grad = grad_ref[...]
    fitting = length // grad.shape[1]
    named, present, before = ranks(routes_ref[...], experts)
    gates = gates_ref[...]
    gate = jnp.zeros(present.shape, F32)
    for k, here in enumerate(named):
        gate = jnp.where(here, gates[k : k + 1, :], gate)

    def slot(c):
        placed = jnp.logical_and(present, before == c).astype(F32)
        row_gate = jnp.sum(placed * gate, axis=1, keepdims=True)
        return row_gate * jnp.dot(
            placed.astype(BF16), grad, preferred_element_type=F32
        )

    for line in range(lines):
        rows = [slot(fitting * line + i) for i in range(fitting)]
        out_ref[:, line, :] = jnp.concatenate(rows, axis=1).astype(BF16)


def unpack_kernel(in_ref, out_ref, flipped, done):
    sources, lines, length = in_ref.shape
    share, slots = flipped.shape
    fitting = length // share
    rows = [in_ref[:, line, :].astype(F32) for line in range(lines)]
    group = LANES // sources
    for g in range(slots // LANES):
        parts = []
        for c in range(g * group, (g + 1) * group):
            start = share * (c % fitting)
            parts.append(rows[c // fitting][:, start : start + share])
        block = jnp.concatenate(parts, axis=0)
        flipped[:, LANES * g : LANES * (g + 1)] = block.T.astype(BF16)
    copies = [
        pltpu.make_async_copy(flipped, out_ref.at[i], done.at[i])
        for i in range(out_ref.shape[0])
    ]
    for copy in copies:
        copy.start()
    for copy in copies:
        copy.wait()


def split_kernel(
    sources, core_ref, weight_ref, hidden_ref, keep_ref, send_ref, order_ref
):
    blocks = keep_ref.shape[0] - 1
    share = weight_ref.shape[1] // (2 * blocks)
    slots = hidden_ref.shape[0]
    capacity = slots // sources
    rows = lax.broadcasted_iota(jnp.int32, (slots, slots), 0)
    columns = lax.broadcasted_iota(jnp.int32, (slots, slots), 1)
    matches = (rows % capacity) * sources + rows // capacity == columns
    order = matches.astype(F32).astype(BF16)
    order_ref[...] = order
    flipped = lax.dot_general(
        hidden_ref[...], order, (((0,), (0,)), ((), ())), preferred_element_type=F32
    ).astype(BF16)
    for ref in (keep_ref, send_ref):
        ref[:, :, ref.shape[2] - LANES :] = jnp.zeros((*ref.shape[:2], LANES), BF16)
        ref[blocks, :, :slots] = flipped

    def store(first, second):
        for j in range(blocks):
            both = weight_ref[:, 2 * share * j : 2 * share * (j + 1)]
            first[j, :, :share] = both[:, :share]
            second[j, :, :share] = both[:, share:]

    pl.when(core_ref[0] == 0)(lambda: store(keep_ref, send_ref))
    pl.when(core_ref[0] != 0)(lambda: store(send_ref, keep_ref))


def values_kernel(
    disp_ref, keep_ref, other_ref, mine_ref, theirs_ref, gate_ref, weight, done
):
    blocks, share, slots = disp_ref.shape
    units = mine_ref.shape[0]
    copies = [
        [
            pltpu.make_async_copy(ref.at[j], weight.at[j, half], done.at[j, half])
            for half, ref in enumerate((keep_ref, other_ref))
        ]
        for j in range(blocks + 1)
    ]
    for pair in copies:
        for copy in pair:
            copy.start()
    values = jnp.zeros((2 * units, slots), F32)
    for j in range(blocks):
        for copy in copies[j]:
            copy.wait()
        both = weight[j].reshape(2 * units, weight.shape[3])[:, :share]
        values += jnp.dot(both, disp_ref[j], preferred_element_type=F32)
    for copy in copies[blocks]:
        copy.wait()
    hidden = weight[blocks].reshape(2 * units, weight.shape[3])[:, :slots]
    terms = jnp.sum(hidden.astype(F32) * values, axis=0, keepdims=True)
    mine_ref[...] = values[:units]
    theirs_ref[...] = values[units:]

    lines = [terms[:, i : i + LANES] for i in range(0, slots, LANES)]
    gate_ref[...] = jnp.broadcast_to(jnp.concatenate(lines, axis=0), gate_ref.shape)


def sum_kernel(parts_ref, out_ref):
    sources, capacity = out_ref.shape
    terms = jnp.sum(parts_ref[...], axis=0)
    rows = []
    for c in range(capacity):
        line, lane = divmod(c * sources, LANES)
        rows.append(terms[line : line + 1, lane : lane + sources])
    out_ref[...] = jnp.concatenate(rows, axis=0).T


def down_kernel(
    disp_ref, keep_hidden_ref, other_hidden_ref, values_ref, mine_ref, theirs_ref
):
    blocks, share, slots = disp_ref.shape
    units = values_ref.shape[0]
    hidden = jnp.concatenate([keep_hidden_ref[0], other_hidden_ref[0]], axis=0)
    hidden = hidden[:, :slots]
    for ref in (mine_ref, theirs_ref):
        ref[:, :, ref.shape[2] - LANES :] = jnp.zeros((*ref.shape[:2], LANES), BF16)
    for j in range(blocks):
        product = lax.dot_general(
            hidden, disp_ref[j], (((1,), (1,)), ((), ())), preferred_element_type=F32
        ).astype(BF16)
        mine_ref[j, :, :share] = product[:units]
        theirs_ref[j, :, :share] = product[units:]
    values = values_ref[...]
    high = values.astype(BF16)
    theirs_ref[blocks, :, :slots] = high
    theirs_ref[blocks + 1, :, :slots] = (values - high.astype(F32)).astype(BF16)


def finish_kernel(
    core_ref,
    mine_ref,
    got_ref,
    values_ref,
    order_ref,
    down_ref,
    dhid_ref,
):
    step, blocks = pl.program_id(0), mine_ref.shape[0]
    last = got_ref.shape[0] - 2
    share = down_ref.shape[1] // (2 * blocks)
    slots = values_ref.shape[1]

    def store(mine_first):
        for j in range(blocks):
            start = 2 * share * j
            both = [mine_ref[j, :, :share], got_ref[step * blocks + j, :, :share]]
            both = both if mine_first else both[::-1]
            down_ref[:, start : start + 2 * share] = jnp.concatenate(both, axis=1)

    pl.when(core_ref[0] == 0)(lambda: store(True))
    pl.when(core_ref[0] != 0)(lambda: store(False))

    @pl.when(step == 0)
    def _():
        high = got_ref[last, :, :slots].astype(F32)
        low = got_ref[last + 1, :, :slots].astype(F32)
        values = (values_ref[...] + (high + low)).T.astype(BF16)
        dhid_ref[...] = jnp.dot(
            order_ref[...], values, preferred_element_type=F32
        ).astype(BF16)


def gate_kernel(terms_ref, routes_ref, gates_ref, out_ref):
    experts, capacity = terms_ref.shape
    named, present, before = ranks(routes_ref[...], experts)
    matched = jnp.zeros(present.shape, F32)
    for c in range(capacity):
        here = jnp.logical_and(present, before == c)
        matched = jnp.where(here, terms_ref[:, c : c + 1], matched)
    total = [jnp.sum(jnp.where(n, matched, 0.0), axis=0, keepdims=True) for n in named]
    out_ref[...] = jnp.concatenate(total, axis=0) / gates_ref[...]


def whole():
    return pl.BlockSpec(memory_space=pltpu.VMEM)


def scalar():
    return pl.BlockSpec(memory_space=pltpu.SMEM)


def stays():
    return pl.BlockSpec(memory_space=pltpu.HBM)


def in_hbm(x):
    return pltpu.with_memory_space_constraint(x, pltpu.HBM)


def in_vmem(x):
    return pltpu.with_memory_space_constraint(x, pltpu.VMEM)


def limit(mib):
    return pltpu.CompilerParams(vmem_limit_bytes=mib * 2**20)


def cost(flops, moved):
    return pl.CostEstimate(flops=flops, bytes_accessed=moved, transcendentals=0)


def swap_all(x, axis):
    return lax.all_to_all(x, axis, split_axis=0, concat_axis=0, tiled=True)


def on_device(grad_out, routes, gates, hidden, w_down):
    experts, chips = lax.axis_size("expert"), lax.axis_size("chip")
    _, slots, units = hidden.shape
    width = w_down.shape[2]
    capacity = slots // experts
    share = grad_out.shape[1]
    padded = -(-share // LANES) * LANES
    core = lax.axis_index("core").astype(jnp.int32).reshape(1)
    routes, gates = routes.T, gates.T
    bf16 = functools.partial(pltpu.HBM, dtype=BF16)
    f32 = functools.partial(pltpu.HBM, dtype=F32)

    def to_other_core(x):
        return lax.ppermute(x, "core", [(0, 1), (1, 0)])

    packed = pl.pallas_call(
        pack_kernel,
        out_shape=jax.ShapeDtypeStruct((experts, 2, capacity * share // 2), BF16),
        in_specs=[whole()] * 3,
        out_specs=whole(),
        name="pack",
    )(grad_out, routes, gates)
    arrived = swap_all(packed, "expert")

    half = bf16((chips + 1, units, padded))
    keep, send, order = pl.pallas_call(
        functools.partial(split_kernel, experts),
        out_shape=(half, half, bf16((slots, slots))),
        in_specs=[scalar(), whole(), whole()],
        out_specs=(whole(),) * 3,
        cost_estimate=cost(2 * units * slots * slots, 2 * 2 * units * width),
        name="split",
    )(core, w_down[0], hidden[0])
    other = in_hbm(to_other_core(send))
    keep, order = in_hbm(keep), in_hbm(order)

    copies = pl.pallas_call(
        unpack_kernel,
        out_shape=bf16((chips, share, slots)),
        in_specs=[whole()],
        out_specs=pl.BlockSpec(memory_space=pl.ANY),
        scratch_shapes=[
            pltpu.VMEM((share, slots), BF16),
            pltpu.SemaphoreType.DMA((chips,)),
        ],
        compiler_params=limit(8),
        name="unpack",
    )(arrived)
    dispatched = in_vmem(swap_all(copies, "chip"))

    flops = 2 * slots * units * width
    mine, theirs, terms = pl.pallas_call(
        values_kernel,
        out_shape=(
            f32((units, slots)),
            f32((units, slots)),
            jax.ShapeDtypeStruct((2 * chips, slots // LANES, LANES), F32),
        ),
        in_specs=[whole(), stays(), stays()],
        out_specs=(whole(),) * 3,
        scratch_shapes=[
            pltpu.VMEM((chips + 1, 2, units, padded), BF16),
            pltpu.SemaphoreType.DMA((chips + 1, 2)),
        ],
        compiler_params=limit(16),
        cost_estimate=cost(flops, slots * width + 2 * units * width),
        name="values",
    )(dispatched, keep, other)
    parts = swap_all(terms, ("chip", "core"))
    theirs = in_hbm(theirs)

    last = pl.BlockSpec((1, units, padded), lambda i: (chips, 0, 0))
    table = pl.BlockSpec((units, slots), lambda i: (0, 0))
    down, beside = pl.pallas_call(
        down_kernel,
        grid=(1,),
        out_shape=(
            bf16((chips, units, padded)),
            bf16((chips + 2, units, padded)),
        ),
        in_specs=[whole(), last, last, table],
        out_specs=(whole(), whole()),
        compiler_params=limit(16),
        cost_estimate=cost(flops, slots * width + 2 * units * width),
        name="down",
    )(dispatched, keep, other, theirs)
    parts, beside = lax.optimization_barrier((parts, beside))
    got = in_vmem(to_other_core(beside))
    down, mine = in_hbm(down), in_hbm(mine)

    steps = 4
    some = pl.BlockSpec((chips // steps, units, padded), lambda i: (i, 0, 0))

    d_down, d_hidden = pl.pallas_call(
        finish_kernel,
        grid=(steps,),
        out_shape=(
            jax.ShapeDtypeStruct((units, width), BF16),
            jax.ShapeDtypeStruct((slots, units), BF16),
        ),
        in_specs=[
            scalar(),
            some,
            whole(),
            table,
            pl.BlockSpec((slots, slots), lambda i: (0, 0)),
        ],
        out_specs=(
            pl.BlockSpec((units, width // steps), lambda i: (0, i)),
            pl.BlockSpec((slots, units), lambda i: (0, 0)),
        ),
        compiler_params=limit(16),
        cost_estimate=cost(2 * units * slots * slots, 4 * units * width),
        name="finish",
    )(core, down, got, mine, order)

    sums = pl.pallas_call(
        sum_kernel,
        out_shape=jax.ShapeDtypeStruct((experts, capacity), F32),
        in_specs=[whole()],
        out_specs=whole(),
        compiler_params=limit(4),
        name="sum",
    )(parts)
    returned = swap_all(sums, "expert")
    returned, _ = lax.optimization_barrier((returned, d_hidden))
    d_gate = pl.pallas_call(
        gate_kernel,
        out_shape=jax.ShapeDtypeStruct(gates.shape, F32),
        in_specs=[whole()] * 3,
        out_specs=whole(),
        compiler_params=limit(4),
        name="match",
    )(returned, routes, gates)
    return (d_hidden[None], d_down[None], d_gate.T)


def solution(mesh):
    parts, experts = mesh.devices.shape
    devices = mesh.devices.reshape(parts // 2, 2, experts)
    finer = Mesh(devices, ("chip", "core", "expert"))
    dp = ("chip", "core")
    in_specs = (
        P("expert", dp),
        P("expert", None),
        P("expert", None),
        P("expert", None, dp),
        P("expert", dp, None),
    )
    out_specs = (P("expert", None, dp), P("expert", dp, None), P("expert", None))
    return jax.shard_map(
        on_device, mesh=finer, in_specs=in_specs, out_specs=out_specs, check_vma=False
    )
```

```python
import functools

import jax
import jax.numpy as jnp
from jax import lax
from jax.experimental import pallas as pl
from jax.experimental.pallas import tpu as pltpu
from jax.sharding import Mesh, PartitionSpec as P

F32 = jnp.float32
BF16 = jnp.bfloat16
LANES = 128


def ranks(routes, experts):
    top, tokens = routes.shape
    ids = lax.broadcasted_iota(jnp.int32, (experts, tokens), 0)
    named = [routes[k : k + 1, :] == ids for k in range(top)]
    present = functools.reduce(jnp.logical_or, named)
    rows = lax.broadcasted_iota(jnp.int32, (tokens, tokens), 0)
    columns = lax.broadcasted_iota(jnp.int32, (tokens, tokens), 1)
    earlier = (rows < columns).astype(F32)
    before = jnp.dot(present.astype(F32), earlier, preferred_element_type=F32)
    return named, present, before


def pack_kernel(grad_ref, routes_ref, gates_ref, out_ref):
    experts, lines, length = out_ref.shape
    grad = grad_ref[...]
    fitting = length // grad.shape[1]
    named, present, before = ranks(routes_ref[...], experts)
    gates = gates_ref[...]
    gate = jnp.zeros(present.shape, F32)
    for k, here in enumerate(named):
        gate = jnp.where(here, gates[k : k + 1, :], gate)

    def slot(c):
        placed = jnp.logical_and(present, before == c).astype(F32)
        row_gate = jnp.sum(placed * gate, axis=1, keepdims=True)
        return row_gate * jnp.dot(
            placed.astype(BF16), grad, preferred_element_type=F32
        )

    for line in range(lines):
        rows = [slot(fitting * line + i) for i in range(fitting)]
        out_ref[:, line, :] = jnp.concatenate(rows, axis=1).astype(BF16)


def unpack_kernel(in_ref, out_ref, flipped, done):
    sources, lines, length = in_ref.shape
    share, slots = flipped.shape
    fitting = length // share
    rows = [in_ref[:, line, :].astype(F32) for line in range(lines)]
    group = LANES // sources
    for g in range(slots // LANES):
        parts = []
        for c in range(g * group, (g + 1) * group):
            start = share * (c % fitting)
            parts.append(rows[c // fitting][:, start : start + share])
        block = jnp.concatenate(parts, axis=0)
        flipped[:, LANES * g : LANES * (g + 1)] = block.T.astype(BF16)
    copies = [
        pltpu.make_async_copy(flipped, out_ref.at[i], done.at[i])
        for i in range(out_ref.shape[0])
    ]
    for copy in copies:
        copy.start()
    for copy in copies:
        copy.wait()


def cases(place_ref, body):
    for far in range(2):
        for core in range(2):
            here = jnp.logical_and(place_ref[0] == far, place_ref[1] == core)
            pl.when(here)(functools.partial(body, far, core))


def columns(far, core, y, blocks, share):
    start = ((far * blocks + y) * 2 + core) * share
    return slice(start, start + share)


def split_kernel(sources, place_ref, weight_ref, hidden_ref, keep_ref, far_ref, order_ref):
    slots = hidden_ref.shape[0]
    all_mine = keep_ref.shape[1] - slots
    blocks = 4
    share = all_mine // (2 * blocks)
    capacity = slots // sources
    rows = lax.broadcasted_iota(jnp.int32, (slots, slots), 0)
    cols = lax.broadcasted_iota(jnp.int32, (slots, slots), 1)
    matches = (rows % capacity) * sources + rows // capacity == cols
    order = matches.astype(F32).astype(BF16)
    order_ref[...] = order
    flipped = lax.dot_general(
        hidden_ref[...], order, (((0,), (0,)), ((), ())), preferred_element_type=F32
    ).astype(BF16)

    def store(far, core):
        for ref, f in ((keep_ref, far), (far_ref, 1 - far)):
            for half, c in enumerate((core, 1 - core)):
                pieces = [
                    weight_ref[:, columns(f, c, y, blocks, share)]
                    for y in range(blocks)
                ]
                start = half * blocks * share
                ref[:, start : start + blocks * share] = jnp.concatenate(
                    pieces, axis=1
                )
            ref[:, all_mine:] = flipped

    cases(place_ref, store)


def product(half, disp_ref, keep_ref, far_ref, weight, done):
    blocks, share, slots = disp_ref.shape
    units, wide = keep_ref.shape[0], 2 * share
    copies = []
    for step in range(blocks // 2):
        here = pl.ds((half * blocks // 2 + step) * wide, wide)
        copies.append(
            [
                pltpu.make_async_copy(
                    ref.at[:, here], weight.at[step, k], done.at[step, k]
                )
                for k, ref in enumerate((keep_ref, far_ref))
            ]
        )
    for now in copies:
        for copy in now:
            copy.start()
    values = jnp.zeros((2 * units, slots), F32)
    for step, now in enumerate(copies):
        for copy in now:
            copy.wait()
        rows = weight[step].reshape(2 * units, wide)
        block = disp_ref[2 * step : 2 * step + 2].reshape(wide, slots)
        values += jnp.dot(rows, block, preferred_element_type=F32)
    return values


def first_kernel(disp_ref, keep_ref, far_ref, values_ref, weight, done):
    values_ref[...] = product(0, disp_ref, keep_ref, far_ref, weight, done)


def values_kernel(
    disp_ref,
    keep_ref,
    far_ref,
    first_ref,
    mine_ref,
    theirs_ref,
    gate_ref,
    weight,
    done,
    hidden,
    ready,
):
    units, slots = mine_ref.shape
    after = pl.ds(keep_ref.shape[1] - slots, slots)
    copies = [
        pltpu.make_async_copy(ref.at[:, after], hidden.at[k], ready.at[k])
        for k, ref in enumerate((keep_ref, far_ref))
    ]
    for copy in copies:
        copy.start()
    values = first_ref[...] + product(1, disp_ref, keep_ref, far_ref, weight, done)
    for copy in copies:
        copy.wait()
    left = hidden[...].reshape(2 * units, slots).astype(F32)
    terms = jnp.sum(left * values, axis=0, keepdims=True)
    mine_ref[...] = values[:units]
    theirs_ref[...] = values[units:]
    lines = [terms[:, i : i + LANES] for i in range(0, slots, LANES)]
    gate_ref[...] = jnp.broadcast_to(jnp.concatenate(lines, axis=0), gate_ref.shape)


def down_kernel(
    own_ref, other_ref, keep_ref, far_ref, values_ref, mine_ref, send_ref, hidden, ready
):
    blocks, share, slots = own_ref.shape
    units, wide = hidden.shape[1], 2 * share
    all_mine = mine_ref.shape[1]
    after = pl.ds(all_mine, slots)
    copies = [
        pltpu.make_async_copy(ref.at[:, after], hidden.at[k], ready.at[k])
        for k, ref in enumerate((keep_ref, far_ref))
    ]
    for copy in copies:
        copy.start()
    for copy in copies:
        copy.wait()
    left = hidden[...].reshape(2 * units, slots)
    for half, ref in enumerate((own_ref, other_ref)):
        for step in range(blocks // 2):
            block = ref[2 * step : 2 * step + 2].reshape(wide, slots)
            down = lax.dot_general(
                left, block, (((1,), (1,)), ((), ())), preferred_element_type=F32
            ).astype(BF16)
            start = (half * blocks // 2 + step) * wide
            mine_ref[:, start : start + wide] = down[:units]
            send_ref[:, start : start + wide] = down[units:]
    values = values_ref[...]
    high = values.astype(BF16)
    send_ref[:, all_mine : all_mine + slots] = high
    send_ref[:, all_mine + slots :] = (values - high.astype(F32)).astype(BF16)


def finish_kernel(
    place_ref, mine_ref, got_ref, values_ref, order_ref, down_ref, dhid_ref
):
    slots = values_ref.shape[1]
    all_mine = mine_ref.shape[1]
    blocks = 4
    share = all_mine // (2 * blocks)

    def store(far, core):
        for f in range(2):
            ref = mine_ref if f == far else got_ref
            for y in range(blocks):
                pair = []
                for c in range(2):
                    start = share * ((0 if c == core else blocks) + y)
                    pair.append(ref[:, start : start + share])
                start = 2 * share * (f * blocks + y)
                down_ref[:, start : start + 2 * share] = jnp.concatenate(pair, axis=1)

    cases(place_ref, store)
    high = got_ref[:, all_mine : all_mine + slots].astype(F32)
    low = got_ref[:, all_mine + slots :].astype(F32)
    flipped = (values_ref[...] + (high + low)).T.astype(BF16)
    dhid_ref[...] = jnp.dot(
        order_ref[...], flipped, preferred_element_type=F32
    ).astype(BF16)


def sum_kernel(parts_ref, out_ref):
    sources, capacity = out_ref.shape
    terms = jnp.sum(parts_ref[...], axis=0)
    rows = []
    for c in range(capacity):
        line, lane = divmod(c * sources, LANES)
        rows.append(terms[line : line + 1, lane : lane + sources])
    out_ref[...] = jnp.concatenate(rows, axis=0).T


def gate_kernel(terms_ref, routes_ref, gates_ref, out_ref):
    experts, capacity = terms_ref.shape
    named, present, before = ranks(routes_ref[...], experts)
    matched = jnp.zeros(present.shape, F32)
    for c in range(capacity):
        here = jnp.logical_and(present, before == c)
        matched = jnp.where(here, terms_ref[:, c : c + 1], matched)
    total = [jnp.sum(jnp.where(n, matched, 0.0), axis=0, keepdims=True) for n in named]
    out_ref[...] = jnp.concatenate(total, axis=0) / gates_ref[...]


def whole():
    return pl.BlockSpec(memory_space=pltpu.VMEM)


def scalar():
    return pl.BlockSpec(memory_space=pltpu.SMEM)


def stays():
    return pl.BlockSpec(memory_space=pltpu.HBM)


def in_hbm(x):
    return pltpu.with_memory_space_constraint(x, pltpu.HBM)


def in_vmem(x):
    return pltpu.with_memory_space_constraint(x, pltpu.VMEM)


def limit(mib):
    return pltpu.CompilerParams(vmem_limit_bytes=mib * 2**20)


def cost(flops, moved):
    return pl.CostEstimate(flops=flops, bytes_accessed=moved, transcendentals=0)


def swap_all(x, axis):
    return lax.all_to_all(x, axis, split_axis=0, concat_axis=0, tiled=True)


def on_device(grad_out, routes, gates, hidden, w_down):
    experts, rows_y = lax.axis_size("expert"), lax.axis_size("y")
    _, slots, units = hidden.shape
    width = w_down.shape[2]
    capacity = slots // experts
    share = grad_out.shape[1]
    mine = rows_y * share
    place = jnp.stack([lax.axis_index("x"), lax.axis_index("core")]).astype(jnp.int32)
    routes, gates = routes.T, gates.T
    bf16 = functools.partial(pltpu.HBM, dtype=BF16)
    f32 = functools.partial(pltpu.HBM, dtype=F32)

    def other(x, axis):
        return lax.ppermute(x, axis, [(0, 1), (1, 0)])

    packed = pl.pallas_call(
        pack_kernel,
        out_shape=jax.ShapeDtypeStruct((experts, 2, capacity * share // 2), BF16),
        in_specs=[whole()] * 3,
        out_specs=whole(),
        name="pack",
    )(grad_out, routes, gates)
    arrived = swap_all(packed, "expert")

    all_mine = 2 * mine
    longer = bf16((units, all_mine + slots))
    keep, to_far, order = pl.pallas_call(
        functools.partial(split_kernel, experts),
        out_shape=(longer, longer, bf16((slots, slots))),
        in_specs=[scalar(), whole(), whole()],
        out_specs=(whole(),) * 3,
        cost_estimate=cost(2 * units * slots * slots, 2 * 2 * units * width),
        name="split",
    )(place, w_down[0], hidden[0])
    from_far = other(to_far, "x")
    arrived, from_far = lax.optimization_barrier((arrived, from_far))

    copies = pl.pallas_call(
        unpack_kernel,
        out_shape=bf16((rows_y, share, slots)),
        in_specs=[whole()],
        out_specs=pl.BlockSpec(memory_space=pl.ANY),
        scratch_shapes=[
            pltpu.VMEM((share, slots), BF16),
            pltpu.SemaphoreType.DMA((rows_y,)),
        ],
        compiler_params=limit(8),
        name="unpack",
    )(arrived)
    dispatched = swap_all(copies, "y")
    from_core = in_vmem(other(dispatched, "core"))
    dispatched = in_vmem(dispatched)

    keep, from_far = in_hbm(keep), in_hbm(from_far)
    flops = 2 * slots * units * width
    scratch = [
        pltpu.VMEM((rows_y // 2, 2, units, 2 * share), BF16),
        pltpu.SemaphoreType.DMA((rows_y // 2, 2)),
    ]
    activations = [
        pltpu.VMEM((2, units, slots), BF16),
        pltpu.SemaphoreType.DMA((2,)),
    ]
    first = pl.pallas_call(
        first_kernel,
        out_shape=f32((2 * units, slots)),
        in_specs=[whole(), stays(), stays()],
        out_specs=whole(),
        scratch_shapes=scratch,
        compiler_params=limit(16),
        cost_estimate=cost(flops // 2, slots * width + units * width),
        name="first",
    )(dispatched, keep, from_far)
    mine_values, theirs, terms = pl.pallas_call(
        values_kernel,
        out_shape=(
            f32((units, slots)),
            f32((units, slots)),
            jax.ShapeDtypeStruct((4 * rows_y, slots // LANES, LANES), F32),
        ),
        in_specs=[whole(), stays(), stays(), whole()],
        out_specs=(whole(),) * 3,
        scratch_shapes=scratch + activations,
        compiler_params=limit(16),
        cost_estimate=cost(flops // 2, slots * width + units * width),
        name="values",
    )(from_core, keep, from_far, in_hbm(first))
    parts = swap_all(terms, ("x", "y", "core"))

    down, back = pl.pallas_call(
        down_kernel,
        out_shape=(bf16((units, all_mine)), bf16((units, all_mine + 2 * slots))),
        in_specs=[whole()] * 2 + [stays()] * 2 + [whole()],
        out_specs=(whole(),) * 2,
        scratch_shapes=activations,
        compiler_params=limit(16),
        cost_estimate=cost(flops, slots * width + 2 * units * width),
        name="down",
    )(dispatched, from_core, keep, from_far, in_hbm(theirs))
    parts, back = lax.optimization_barrier((parts, back))
    got = other(back, "x")

    d_down, d_hidden = pl.pallas_call(
        finish_kernel,
        out_shape=(
            jax.ShapeDtypeStruct((units, width), BF16),
            jax.ShapeDtypeStruct((slots, units), BF16),
        ),
        in_specs=[scalar()] + [whole()] * 4,
        out_specs=(whole(),) * 2,
        compiler_params=limit(16),
        cost_estimate=cost(2 * units * slots * slots, 4 * units * width),
        name="finish",
    )(place, in_hbm(down), in_vmem(got), in_hbm(mine_values), in_hbm(order))

    sums = pl.pallas_call(
        sum_kernel,
        out_shape=jax.ShapeDtypeStruct((experts, capacity), F32),
        in_specs=[whole()],
        out_specs=whole(),
        compiler_params=limit(4),
        name="sum",
    )(parts)
    returned = swap_all(sums, "expert")
    returned, _ = lax.optimization_barrier((returned, d_hidden))
    d_gate = pl.pallas_call(
        gate_kernel,
        out_shape=jax.ShapeDtypeStruct(gates.shape, F32),
        in_specs=[whole()] * 3,
        out_specs=whole(),
        compiler_params=limit(4),
        name="match",
    )(returned, routes, gates)
    return (d_hidden[None], d_down[None], d_gate.T)


def solution(mesh):
    parts, experts = mesh.devices.shape
    devices = mesh.devices.reshape(2, parts // 4, 2, experts)
    finer = Mesh(devices, ("x", "y", "core", "expert"))
    dp = ("x", "y", "core")
    in_specs = (
        P("expert", dp),
        P("expert", None),
        P("expert", None),
        P("expert", None, dp),
        P("expert", dp, None),
    )
    out_specs = (P("expert", None, dp), P("expert", dp, None), P("expert", None))
    return jax.shard_map(
        on_device, mesh=finer, in_specs=in_specs, out_specs=out_specs, check_vma=False
    )
```

```python
import functools

import jax
import jax.numpy as jnp
from jax import lax
from jax.experimental import pallas as pl
from jax.experimental.pallas import tpu as pltpu
from jax.sharding import Mesh, PartitionSpec as P

F32 = jnp.float32
BF16 = jnp.bfloat16
LANES = 128


def ranks(routes, experts):
    top, tokens = routes.shape
    ids = lax.broadcasted_iota(jnp.int32, (experts, tokens), 0)
    named = [routes[k : k + 1, :] == ids for k in range(top)]
    present = functools.reduce(jnp.logical_or, named)
    rows = lax.broadcasted_iota(jnp.int32, (tokens, tokens), 0)
    columns = lax.broadcasted_iota(jnp.int32, (tokens, tokens), 1)
    earlier = (rows < columns).astype(F32)
    before = jnp.dot(present.astype(F32), earlier, preferred_element_type=F32)
    return named, present, before


def pack_kernel(grad_ref, routes_ref, gates_ref, out_ref):
    experts, lines, length = out_ref.shape
    grad = grad_ref[...]
    fitting = length // grad.shape[1]
    named, present, before = ranks(routes_ref[...], experts)
    gates = gates_ref[...]
    gate = jnp.zeros(present.shape, F32)
    for k, here in enumerate(named):
        gate = jnp.where(here, gates[k : k + 1, :], gate)

    def slot(c):
        placed = jnp.logical_and(present, before == c).astype(F32)
        row_gate = jnp.sum(placed * gate, axis=1, keepdims=True)
        return row_gate * jnp.dot(
            placed.astype(BF16), grad, preferred_element_type=F32
        )

    for line in range(lines):
        rows = [slot(fitting * line + i) for i in range(fitting)]
        out_ref[:, line, :] = jnp.concatenate(rows, axis=1).astype(BF16)


def unpack_kernel(in_ref, out_ref, flipped, done):
    sources, lines, length = in_ref.shape
    share, slots = flipped.shape
    fitting = length // share
    rows = [in_ref[:, line, :].astype(F32) for line in range(lines)]
    group = LANES // sources
    for g in range(slots // LANES):
        parts = []
        for c in range(g * group, (g + 1) * group):
            start = share * (c % fitting)
            parts.append(rows[c // fitting][:, start : start + share])
        block = jnp.concatenate(parts, axis=0)
        flipped[:, LANES * g : LANES * (g + 1)] = block.T.astype(BF16)
    copies = [
        pltpu.make_async_copy(flipped, out_ref.at[i], done.at[i])
        for i in range(out_ref.shape[0])
    ]
    for copy in copies:
        copy.start()
    for copy in copies:
        copy.wait()


def cases(place_ref, body):
    for far in range(2):
        for core in range(2):
            here = jnp.logical_and(place_ref[0] == far, place_ref[1] == core)
            pl.when(here)(functools.partial(body, far, core))


def columns(far, core, y, blocks, share):
    start = ((far * blocks + y) * 2 + core) * share
    return slice(start, start + share)


def split_kernel(
    sources,
    place_ref,
    weight_ref,
    hidden_ref,
    keep_ref,
    far_ref,
    later_ref,
    order_ref,
):
    slots = hidden_ref.shape[0]
    all_mine = keep_ref.shape[1] - slots
    blocks = 4
    share = all_mine // (2 * blocks)
    capacity = slots // sources
    rows = lax.broadcasted_iota(jnp.int32, (slots, slots), 0)
    cols = lax.broadcasted_iota(jnp.int32, (slots, slots), 1)
    matches = (rows % capacity) * sources + rows // capacity == cols
    order = matches.astype(F32).astype(BF16)
    order_ref[...] = order
    flipped = lax.dot_general(
        hidden_ref[...], order, (((0,), (0,)), ((), ())), preferred_element_type=F32
    ).astype(BF16)

    mine = blocks * share

    def store(far, core):
        def part(f, c):
            pieces = [
                weight_ref[:, columns(f, c, y, blocks, share)] for y in range(blocks)
            ]
            return jnp.concatenate(pieces, axis=1)

        keep_ref[:, :mine] = part(far, core)
        keep_ref[:, mine:all_mine] = part(far, 1 - core)
        keep_ref[:, all_mine:] = flipped
        far_ref[:, :mine] = part(1 - far, core)
        far_ref[:, mine:] = flipped
        later_ref[...] = part(1 - far, 1 - core)

    cases(place_ref, store)


def values_kernel(
    own_ref,
    other_ref,
    keep_ref,
    far_ref,
    later_ref,
    mine_ref,
    theirs_ref,
    gate_ref,
    weight,
    done,
    hidden,
    ready,
):
    blocks, share, slots = own_ref.shape
    units, wide, mine = mine_ref.shape[0], 2 * share, blocks * share
    steps = blocks // 2
    copies = []
    for step in range(2 * steps):
        here = pl.ds(step * wide, wide)
        if step < steps:
            from_far = far_ref.at[:, here]
        else:
            from_far = later_ref.at[:, pl.ds(step * wide - mine, wide)]
        copies.append(
            [
                pltpu.make_async_copy(ref, weight.at[step, k], done.at[step, k])
                for k, ref in enumerate((keep_ref.at[:, here], from_far))
            ]
        )
    last = activations(keep_ref, far_ref, 2 * mine, mine, hidden, ready)
    for now in copies + [last]:
        for copy in now:
            copy.start()
    values = jnp.zeros((2 * units, slots), F32)
    for step, now in enumerate(copies):
        for copy in now:
            copy.wait()
        rows = weight[step].reshape(2 * units, wide)
        ref, first = (own_ref, step) if step < steps else (other_ref, step - steps)
        block = ref[2 * first : 2 * first + 2].reshape(wide, slots)
        values += jnp.dot(rows, block, preferred_element_type=F32)
    for copy in last:
        copy.wait()
    left = hidden[...].reshape(2 * units, slots).astype(F32)
    terms = jnp.sum(left * values, axis=0, keepdims=True)
    mine_ref[...] = values[:units]
    theirs_ref[...] = values[units:]
    lines = [terms[:, i : i + LANES] for i in range(0, slots, LANES)]
    gate_ref[...] = jnp.broadcast_to(jnp.concatenate(lines, axis=0), gate_ref.shape)


def activations(keep_ref, far_ref, keep_start, far_start, hidden, ready):
    slots = hidden.shape[2]
    return [
        pltpu.make_async_copy(ref.at[:, pl.ds(start, slots)], hidden.at[k], ready.at[k])
        for k, (ref, start) in enumerate(((keep_ref, keep_start), (far_ref, far_start)))
    ]


def down_kernel(disp_ref, keep_ref, far_ref, mine_ref, send_ref, hidden, ready):
    blocks, share, slots = disp_ref.shape
    units, wide, mine = hidden.shape[1], 2 * share, blocks * share
    copies = activations(keep_ref, far_ref, 2 * mine, mine, hidden, ready)
    for copy in copies:
        copy.start()
    for copy in copies:
        copy.wait()
    left = hidden[...].reshape(2 * units, slots)
    for step in range(blocks // 2):
        block = disp_ref[2 * step : 2 * step + 2].reshape(wide, slots)
        down = lax.dot_general(
            left, block, (((1,), (1,)), ((), ())), preferred_element_type=F32
        ).astype(BF16)
        mine_ref[:, wide * step : wide * (step + 1)] = down[:units]
        send_ref[:, wide * step : wide * (step + 1)] = down[units:]


def rest_kernel(
    disp_ref, keep_ref, far_ref, values_ref, mine_ref, send_ref, hidden, ready
):
    down_kernel(disp_ref, keep_ref, far_ref, mine_ref, send_ref, hidden, ready)
    mine, slots = mine_ref.shape[1], values_ref.shape[1]
    values = values_ref[...]
    high = values.astype(BF16)
    send_ref[:, mine : mine + slots] = high
    send_ref[:, mine + slots :] = (values - high.astype(F32)).astype(BF16)


def finish_kernel(
    place_ref,
    own_ref,
    other_ref,
    got_own_ref,
    got_other_ref,
    values_ref,
    order_ref,
    down_ref,
    dhid_ref,
):
    slots = values_ref.shape[1]
    mine = own_ref.shape[1]
    blocks = 4
    share = mine // blocks

    def store(far, core):
        for f in range(2):
            refs = (own_ref, other_ref) if f == far else (got_own_ref, got_other_ref)
            refs = refs if core == 0 else refs[::-1]
            for y in range(blocks):
                pair = [ref[:, share * y : share * (y + 1)] for ref in refs]
                start = 2 * share * (f * blocks + y)
                down_ref[:, start : start + 2 * share] = jnp.concatenate(pair, axis=1)

    cases(place_ref, store)
    high = got_other_ref[:, mine : mine + slots].astype(F32)
    low = got_other_ref[:, mine + slots :].astype(F32)
    flipped = (values_ref[...] + (high + low)).T.astype(BF16)
    dhid_ref[...] = jnp.dot(
        order_ref[...], flipped, preferred_element_type=F32
    ).astype(BF16)


def sum_kernel(parts_ref, out_ref):
    sources, capacity = out_ref.shape
    terms = jnp.sum(parts_ref[...], axis=0)
    rows = []
    for c in range(capacity):
        line, lane = divmod(c * sources, LANES)
        rows.append(terms[line : line + 1, lane : lane + sources])
    out_ref[...] = jnp.concatenate(rows, axis=0).T


def gate_kernel(terms_ref, routes_ref, gates_ref, out_ref):
    experts, capacity = terms_ref.shape
    named, present, before = ranks(routes_ref[...], experts)
    matched = jnp.zeros(present.shape, F32)
    for c in range(capacity):
        here = jnp.logical_and(present, before == c)
        matched = jnp.where(here, terms_ref[:, c : c + 1], matched)
    total = [jnp.sum(jnp.where(n, matched, 0.0), axis=0, keepdims=True) for n in named]
    out_ref[...] = jnp.concatenate(total, axis=0) / gates_ref[...]


def whole():
    return pl.BlockSpec(memory_space=pltpu.VMEM)


def scalar():
    return pl.BlockSpec(memory_space=pltpu.SMEM)


def stays():
    return pl.BlockSpec(memory_space=pltpu.HBM)


def in_hbm(x):
    return pltpu.with_memory_space_constraint(x, pltpu.HBM)


def in_vmem(x):
    return pltpu.with_memory_space_constraint(x, pltpu.VMEM)


def limit(mib):
    return pltpu.CompilerParams(vmem_limit_bytes=mib * 2**20)


def cost(flops, moved):
    return pl.CostEstimate(flops=flops, bytes_accessed=moved, transcendentals=0)


def swap_all(x, axis):
    return lax.all_to_all(x, axis, split_axis=0, concat_axis=0, tiled=True)


def on_device(grad_out, routes, gates, hidden, w_down):
    experts, rows_y = lax.axis_size("expert"), lax.axis_size("y")
    _, slots, units = hidden.shape
    width = w_down.shape[2]
    capacity = slots // experts
    share = grad_out.shape[1]
    mine = rows_y * share
    place = jnp.stack([lax.axis_index("x"), lax.axis_index("core")]).astype(jnp.int32)
    routes, gates = routes.T, gates.T
    bf16 = functools.partial(pltpu.HBM, dtype=BF16)
    f32 = functools.partial(pltpu.HBM, dtype=F32)

    def other(x, axis):
        return lax.ppermute(x, axis, [(0, 1), (1, 0)])

    packed = pl.pallas_call(
        pack_kernel,
        out_shape=jax.ShapeDtypeStruct((experts, 2, capacity * share // 2), BF16),
        in_specs=[whole()] * 3,
        out_specs=whole(),
        name="pack",
    )(grad_out, routes, gates)
    arrived = swap_all(packed, "expert")

    keep, to_far, to_far_later, order = pl.pallas_call(
        functools.partial(split_kernel, experts),
        out_shape=(
            bf16((units, 2 * mine + slots)),
            bf16((units, mine + slots)),
            bf16((units, mine)),
            bf16((slots, slots)),
        ),
        in_specs=[scalar(), whole(), whole()],
        out_specs=(whole(),) * 4,
        cost_estimate=cost(2 * units * slots * slots, 2 * 2 * units * width),
        name="split",
    )(place, w_down[0], hidden[0])
    from_far = other(to_far, "x")
    arrived, from_far, to_far_later = lax.optimization_barrier(
        (arrived, from_far, to_far_later)
    )
    later = other(to_far_later, "x")

    copies = pl.pallas_call(
        unpack_kernel,
        out_shape=bf16((rows_y, share, slots)),
        in_specs=[whole()],
        out_specs=pl.BlockSpec(memory_space=pl.ANY),
        scratch_shapes=[
            pltpu.VMEM((share, slots), BF16),
            pltpu.SemaphoreType.DMA((rows_y,)),
        ],
        compiler_params=limit(8),
        name="unpack",
    )(arrived)
    dispatched, later = lax.optimization_barrier((swap_all(copies, "y"), later))
    from_core = other(dispatched, "core")
    dispatched = in_vmem(dispatched)

    keep, from_far, later = in_hbm(keep), in_hbm(from_far), in_vmem(later)
    flops = 2 * slots * units * width
    moved = slots * width + 2 * units * width
    scratch = [
        pltpu.VMEM((2, units, slots), BF16),
        pltpu.SemaphoreType.DMA((2,)),
    ]
    down_own, back_own = pl.pallas_call(
        down_kernel,
        out_shape=(bf16((units, mine)), bf16((units, mine))),
        in_specs=[whole(), stays(), stays()],
        out_specs=(whole(),) * 2,
        scratch_shapes=scratch,
        compiler_params=limit(16),
        cost_estimate=cost(flops // 2, moved // 2),
        name="down",
    )(dispatched, keep, from_far)
    from_core, back_own = lax.optimization_barrier((from_core, back_own))
    got_own = other(back_own, "x")

    mine_values, theirs, terms = pl.pallas_call(
        values_kernel,
        out_shape=(
            f32((units, slots)),
            f32((units, slots)),
            jax.ShapeDtypeStruct((4 * rows_y, slots // LANES, LANES), F32),
        ),
        in_specs=[whole()] * 2 + [stays()] * 2 + [whole()],
        out_specs=(whole(),) * 3,
        scratch_shapes=[
            pltpu.VMEM((rows_y, 2, units, 2 * share), BF16),
            pltpu.SemaphoreType.DMA((rows_y, 2)),
        ]
        + scratch,
        compiler_params=limit(16),
        cost_estimate=cost(flops, moved),
        name="values",
    )(dispatched, in_vmem(from_core), keep, from_far, later)
    parts = swap_all(terms, ("x", "y", "core"))

    down_other, back_other = pl.pallas_call(
        rest_kernel,
        out_shape=(bf16((units, mine)), bf16((units, mine + 2 * slots))),
        in_specs=[whole()] + [stays()] * 2 + [whole()],
        out_specs=(whole(),) * 2,
        scratch_shapes=scratch,
        compiler_params=limit(16),
        cost_estimate=cost(flops // 2, moved // 2),
        name="rest",
    )(in_vmem(from_core), keep, from_far, in_hbm(theirs))
    parts, back_other, got_own = lax.optimization_barrier((parts, back_other, got_own))
    got_other = other(back_other, "x")

    d_down, d_hidden = pl.pallas_call(
        finish_kernel,
        out_shape=(
            jax.ShapeDtypeStruct((units, width), BF16),
            jax.ShapeDtypeStruct((slots, units), BF16),
        ),
        in_specs=[scalar()] + [whole()] * 6,
        out_specs=(whole(),) * 2,
        compiler_params=limit(16),
        cost_estimate=cost(2 * units * slots * slots, 4 * units * width),
        name="finish",
    )(
        place,
        in_hbm(down_own),
        in_hbm(down_other),
        in_vmem(got_own),
        in_vmem(got_other),
        in_hbm(mine_values),
        in_hbm(order),
    )

    sums = pl.pallas_call(
        sum_kernel,
        out_shape=jax.ShapeDtypeStruct((experts, capacity), F32),
        in_specs=[whole()],
        out_specs=whole(),
        compiler_params=limit(4),
        name="sum",
    )(parts)
    returned = swap_all(sums, "expert")
    returned, _ = lax.optimization_barrier((returned, d_hidden))
    d_gate = pl.pallas_call(
        gate_kernel,
        out_shape=jax.ShapeDtypeStruct(gates.shape, F32),
        in_specs=[whole()] * 3,
        out_specs=whole(),
        compiler_params=limit(4),
        name="match",
    )(returned, routes, gates)
    return (d_hidden[None], d_down[None], d_gate.T)


def solution(mesh):
    parts, experts = mesh.devices.shape
    devices = mesh.devices.reshape(2, parts // 4, 2, experts)
    finer = Mesh(devices, ("x", "y", "core", "expert"))
    dp = ("x", "y", "core")
    in_specs = (
        P("expert", dp),
        P("expert", None),
        P("expert", None),
        P("expert", None, dp),
        P("expert", dp, None),
    )
    out_specs = (P("expert", None, dp), P("expert", dp, None), P("expert", None))
    return jax.shard_map(
        on_device, mesh=finer, in_specs=in_specs, out_specs=out_specs, check_vma=False
    )
```

```python
import functools

import jax
import jax.numpy as jnp
from jax import lax
from jax.experimental import pallas as pl
from jax.experimental.pallas import tpu as pltpu
from jax.sharding import Mesh, PartitionSpec as P

F32 = jnp.float32
BF16 = jnp.bfloat16
LANES = 128


def ranks(routes, experts):
    top, tokens = routes.shape
    ids = lax.broadcasted_iota(jnp.int32, (experts, tokens), 0)
    named = [routes[k : k + 1, :] == ids for k in range(top)]
    present = functools.reduce(jnp.logical_or, named)
    rows = lax.broadcasted_iota(jnp.int32, (tokens, tokens), 0)
    columns = lax.broadcasted_iota(jnp.int32, (tokens, tokens), 1)
    earlier = (rows < columns).astype(F32)
    before = jnp.dot(present.astype(F32), earlier, preferred_element_type=F32)
    return named, present, before


def pack_kernel(grad_ref, routes_ref, gates_ref, out_ref):
    experts, lines, length = out_ref.shape
    grad = grad_ref[...]
    fitting = length // grad.shape[1]
    named, present, before = ranks(routes_ref[...], experts)
    gates = gates_ref[...]
    gate = jnp.zeros(present.shape, F32)
    for k, here in enumerate(named):
        gate = jnp.where(here, gates[k : k + 1, :], gate)

    def slot(c):
        placed = jnp.logical_and(present, before == c).astype(F32)
        row_gate = jnp.sum(placed * gate, axis=1, keepdims=True)
        return row_gate * jnp.dot(
            placed.astype(BF16), grad, preferred_element_type=F32
        )

    for line in range(lines):
        rows = [slot(fitting * line + i) for i in range(fitting)]
        out_ref[:, line, :] = jnp.concatenate(rows, axis=1).astype(BF16)


def unpack_kernel(in_ref, out_ref, flipped, done):
    sources, lines, length = in_ref.shape
    share, slots = flipped.shape
    fitting = length // share
    rows = [in_ref[:, line, :].astype(F32) for line in range(lines)]
    group = LANES // sources
    for g in range(slots // LANES):
        parts = []
        for c in range(g * group, (g + 1) * group):
            start = share * (c % fitting)
            parts.append(rows[c // fitting][:, start : start + share])
        block = jnp.concatenate(parts, axis=0)
        flipped[:, LANES * g : LANES * (g + 1)] = block.T.astype(BF16)
    copies = [
        pltpu.make_async_copy(flipped, out_ref.at[i], done.at[i])
        for i in range(out_ref.shape[0])
    ]
    for copy in copies:
        copy.start()
    for copy in copies:
        copy.wait()


def cases(place_ref, body):
    for far in range(2):
        for core in range(2):
            here = jnp.logical_and(place_ref[0] == far, place_ref[1] == core)
            pl.when(here)(functools.partial(body, far, core))


def columns(far, core, y, blocks, share):
    start = ((far * blocks + y) * 2 + core) * share
    return slice(start, start + share)


def split_kernel(
    sources,
    place_ref,
    weight_ref,
    hidden_ref,
    keep_ref,
    far_ref,
    later_ref,
    order_ref,
):
    slots = hidden_ref.shape[0]
    all_mine = keep_ref.shape[1] - slots
    blocks = 4
    share = all_mine // (2 * blocks)
    capacity = slots // sources
    rows = lax.broadcasted_iota(jnp.int32, (slots, slots), 0)
    cols = lax.broadcasted_iota(jnp.int32, (slots, slots), 1)
    matches = (rows % capacity) * sources + rows // capacity == cols
    order = matches.astype(F32).astype(BF16)
    order_ref[...] = order
    flipped = lax.dot_general(
        hidden_ref[...], order, (((0,), (0,)), ((), ())), preferred_element_type=F32
    ).astype(BF16)

    mine = blocks * share

    def store(far, core):
        def part(f, c):
            pieces = [
                weight_ref[:, columns(f, c, y, blocks, share)] for y in range(blocks)
            ]
            return jnp.concatenate(pieces, axis=1)

        keep_ref[:, :mine] = part(far, core)
        keep_ref[:, mine:all_mine] = part(far, 1 - core)
        keep_ref[:, all_mine:] = flipped
        far_ref[...] = part(1 - far, core)
        later_ref[:, :mine] = part(1 - far, 1 - core)
        later_ref[:, mine:] = flipped

    cases(place_ref, store)


def values_kernel(
    own_ref,
    other_ref,
    keep_ref,
    far_ref,
    later_ref,
    mine_ref,
    theirs_ref,
    gate_ref,
    weight,
    done,
    hidden,
    ready,
):
    blocks, share, slots = own_ref.shape
    units, wide, mine = mine_ref.shape[0], 2 * share, blocks * share
    steps = blocks // 2
    copies = []
    for step in range(2 * steps):
        here = pl.ds(step * wide, wide)
        if step < steps:
            from_far = far_ref.at[:, here]
        else:
            from_far = later_ref.at[:, pl.ds(step * wide - mine, wide)]
        copies.append(
            [
                pltpu.make_async_copy(ref, weight.at[step, k], done.at[step, k])
                for k, ref in enumerate((keep_ref.at[:, here], from_far))
            ]
        )
    last = [
        pltpu.make_async_copy(ref.at[:, pl.ds(start, slots)], hidden.at[k], ready.at[k])
        for k, (ref, start) in enumerate(((keep_ref, 2 * mine), (later_ref, mine)))
    ]
    for now in copies + [last]:
        for copy in now:
            copy.start()
    values = jnp.zeros((2 * units, slots), F32)
    for step, now in enumerate(copies):
        for copy in now:
            copy.wait()
        rows = weight[step].reshape(2 * units, wide)
        ref, first = (own_ref, step) if step < steps else (other_ref, step - steps)
        block = ref[2 * first : 2 * first + 2].reshape(wide, slots)
        values += jnp.dot(rows, block, preferred_element_type=F32)
    for copy in last:
        copy.wait()
    left = hidden[...].reshape(2 * units, slots).astype(F32)
    terms = jnp.sum(left * values, axis=0, keepdims=True)
    mine_ref[...] = values[:units]
    theirs = values[units:]
    high = theirs.astype(BF16)
    theirs_ref[:, :slots] = high
    theirs_ref[:, slots:] = (theirs - high.astype(F32)).astype(BF16)
    lines = [terms[:, i : i + LANES] for i in range(0, slots, LANES)]
    gate_ref[...] = jnp.broadcast_to(jnp.concatenate(lines, axis=0), gate_ref.shape)


def down(left, disp_ref, out_ref, first):
    blocks, share, slots = disp_ref.shape
    wide = 2 * share
    for step in range(blocks // 2):
        block = disp_ref[2 * step : 2 * step + 2].reshape(wide, slots)
        part = lax.dot_general(
            left, block, (((1,), (1,)), ((), ())), preferred_element_type=F32
        )
        start = first + wide * step
        out_ref[:, start : start + wide] = part.astype(BF16)


def far_kernel(own_ref, later_ref, out_ref):
    down(later_ref[:, out_ref.shape[1] :], own_ref, out_ref, 0)


def far_rest_kernel(other_ref, later_ref, first_ref, out_ref):
    mine = first_ref.shape[1]
    out_ref[:, :mine] = first_ref[...]
    down(later_ref[:, mine:], other_ref, out_ref, mine)


def own_kernel(own_ref, other_ref, keep_ref, out_ref, hidden, done):
    mine = out_ref.shape[1] // 2
    after = pl.ds(2 * mine, hidden.shape[1])
    copy = pltpu.make_async_copy(keep_ref.at[:, after], hidden, done)
    copy.start()
    copy.wait()
    for half, ref in enumerate((own_ref, other_ref)):
        down(hidden[...], ref, out_ref, half * mine)


def finish_kernel(
    place_ref,
    own_ref,
    far_ref,
    got_values_ref,
    values_ref,
    order_ref,
    down_ref,
    dhid_ref,
):
    slots = values_ref.shape[1]
    mine = own_ref.shape[1] // 2
    blocks = 4
    share = mine // blocks

    def store(far, core):
        for f in range(2):
            ref = own_ref if f == far else far_ref
            for y in range(blocks):
                pair = []
                for c in range(2):
                    start = (0 if c == core else mine) + share * y
                    pair.append(ref[:, start : start + share])
                start = 2 * share * (f * blocks + y)
                down_ref[:, start : start + 2 * share] = jnp.concatenate(pair, axis=1)

    cases(place_ref, store)
    high = got_values_ref[:, :slots].astype(F32)
    low = got_values_ref[:, slots:].astype(F32)
    flipped = (values_ref[...] + (high + low)).T.astype(BF16)
    dhid_ref[...] = jnp.dot(
        order_ref[...], flipped, preferred_element_type=F32
    ).astype(BF16)


def sum_kernel(parts_ref, out_ref):
    sources, capacity = out_ref.shape
    terms = jnp.sum(parts_ref[...], axis=0)
    rows = []
    for c in range(capacity):
        line, lane = divmod(c * sources, LANES)
        rows.append(terms[line : line + 1, lane : lane + sources])
    out_ref[...] = jnp.concatenate(rows, axis=0).T


def gate_kernel(terms_ref, routes_ref, gates_ref, out_ref):
    experts, capacity = terms_ref.shape
    named, present, before = ranks(routes_ref[...], experts)
    matched = jnp.zeros(present.shape, F32)
    for c in range(capacity):
        here = jnp.logical_and(present, before == c)
        matched = jnp.where(here, terms_ref[:, c : c + 1], matched)
    total = [jnp.sum(jnp.where(n, matched, 0.0), axis=0, keepdims=True) for n in named]
    out_ref[...] = jnp.concatenate(total, axis=0) / gates_ref[...]


def whole():
    return pl.BlockSpec(memory_space=pltpu.VMEM)


def scalar():
    return pl.BlockSpec(memory_space=pltpu.SMEM)


def stays():
    return pl.BlockSpec(memory_space=pltpu.HBM)


def in_hbm(x):
    return pltpu.with_memory_space_constraint(x, pltpu.HBM)


def in_vmem(x):
    return pltpu.with_memory_space_constraint(x, pltpu.VMEM)


def limit(mib):
    return pltpu.CompilerParams(vmem_limit_bytes=mib * 2**20)


def cost(flops, moved):
    return pl.CostEstimate(flops=flops, bytes_accessed=moved, transcendentals=0)


def swap_all(x, axis):
    return lax.all_to_all(x, axis, split_axis=0, concat_axis=0, tiled=True)


def on_device(grad_out, routes, gates, hidden, w_down):
    experts, rows_y = lax.axis_size("expert"), lax.axis_size("y")
    _, slots, units = hidden.shape
    width = w_down.shape[2]
    capacity = slots // experts
    share = grad_out.shape[1]
    mine = rows_y * share
    place = jnp.stack([lax.axis_index("x"), lax.axis_index("core")]).astype(jnp.int32)
    routes, gates = routes.T, gates.T
    bf16 = functools.partial(pltpu.HBM, dtype=BF16)
    f32 = functools.partial(pltpu.HBM, dtype=F32)

    def other(x, axis):
        return lax.ppermute(x, axis, [(0, 1), (1, 0)])

    packed = pl.pallas_call(
        pack_kernel,
        out_shape=jax.ShapeDtypeStruct((experts, 2, capacity * share // 2), BF16),
        in_specs=[whole()] * 3,
        out_specs=whole(),
        name="pack",
    )(grad_out, routes, gates)
    arrived = swap_all(packed, "expert")

    keep, to_far, to_far_later, order = pl.pallas_call(
        functools.partial(split_kernel, experts),
        out_shape=(
            bf16((units, 2 * mine + slots)),
            bf16((units, mine)),
            bf16((units, mine + slots)),
            bf16((slots, slots)),
        ),
        in_specs=[scalar(), whole(), whole()],
        out_specs=(whole(),) * 4,
        cost_estimate=cost(2 * units * slots * slots, 2 * 2 * units * width),
        name="split",
    )(place, w_down[0], hidden[0])
    from_far = other(to_far, "x")
    arrived, from_far, to_far_later = lax.optimization_barrier(
        (arrived, from_far, to_far_later)
    )
    later = other(to_far_later, "x")

    copies = pl.pallas_call(
        unpack_kernel,
        out_shape=bf16((rows_y, share, slots)),
        in_specs=[whole()],
        out_specs=pl.BlockSpec(memory_space=pl.ANY),
        scratch_shapes=[
            pltpu.VMEM((share, slots), BF16),
            pltpu.SemaphoreType.DMA((rows_y,)),
        ],
        compiler_params=limit(8),
        name="unpack",
    )(arrived)
    dispatched, later = lax.optimization_barrier((swap_all(copies, "y"), later))
    from_core = other(dispatched, "core")
    dispatched = in_vmem(dispatched)

    keep, from_far, later = in_hbm(keep), in_hbm(from_far), in_vmem(later)
    flops = 2 * slots * units * width
    moved = slots * width + 2 * units * width
    def kernel(body, name, out, *operands):
        return pl.pallas_call(
            body,
            out_shape=out,
            in_specs=[whole()] * len(operands),
            out_specs=whole(),
            compiler_params=limit(16),
            cost_estimate=cost(flops // 4, moved // 4),
            name=name,
        )(*operands)

    far_own = kernel(far_kernel, "far", bf16((units, mine)), dispatched, later)
    from_core, far_own = lax.optimization_barrier((from_core, far_own))
    far_both = kernel(
        far_rest_kernel,
        "far_rest",
        bf16((units, 2 * mine)),
        in_vmem(from_core),
        later,
        in_hbm(far_own),
    )
    from_core, far_both = lax.optimization_barrier((from_core, far_both))
    from_core = in_vmem(from_core)
    got = other(far_both, "x")

    mine_values, theirs, terms = pl.pallas_call(
        values_kernel,
        out_shape=(
            f32((units, slots)),
            bf16((units, 2 * slots)),
            jax.ShapeDtypeStruct((4 * rows_y, slots // LANES, LANES), F32),
        ),
        in_specs=[whole()] * 2 + [stays()] * 2 + [whole()],
        out_specs=(whole(),) * 3,
        scratch_shapes=[
            pltpu.VMEM((rows_y, 2, units, 2 * share), BF16),
            pltpu.SemaphoreType.DMA((rows_y, 2)),
            pltpu.VMEM((2, units, slots), BF16),
            pltpu.SemaphoreType.DMA((2,)),
        ],
        compiler_params=limit(16),
        cost_estimate=cost(flops, moved),
        name="values",
    )(dispatched, from_core, keep, from_far, later)
    parts = swap_all(terms, ("x", "y", "core"))

    down_own = pl.pallas_call(
        own_kernel,
        out_shape=bf16((units, 2 * mine)),
        in_specs=[whole()] * 2 + [stays()],
        out_specs=whole(),
        scratch_shapes=[pltpu.VMEM((units, slots), BF16), pltpu.SemaphoreType.DMA],
        compiler_params=limit(16),
        cost_estimate=cost(flops // 2, moved // 2),
        name="own",
    )(dispatched, from_core, keep)
    parts, down_own, theirs = lax.optimization_barrier((parts, down_own, theirs))
    got_values = other(theirs, "x")

    d_down, d_hidden = pl.pallas_call(
        finish_kernel,
        out_shape=(
            jax.ShapeDtypeStruct((units, width), BF16),
            jax.ShapeDtypeStruct((slots, units), BF16),
        ),
        in_specs=[scalar()] + [whole()] * 5,
        out_specs=(whole(),) * 2,
        compiler_params=limit(16),
        cost_estimate=cost(2 * units * slots * slots, 4 * units * width),
        name="finish",
    )(
        place,
        in_hbm(down_own),
        in_vmem(got),
        in_vmem(got_values),
        in_hbm(mine_values),
        in_hbm(order),
    )

    sums = pl.pallas_call(
        sum_kernel,
        out_shape=jax.ShapeDtypeStruct((experts, capacity), F32),
        in_specs=[whole()],
        out_specs=whole(),
        compiler_params=limit(4),
        name="sum",
    )(parts)
    returned = swap_all(sums, "expert")
    returned, _ = lax.optimization_barrier((returned, d_hidden))
    d_gate = pl.pallas_call(
        gate_kernel,
        out_shape=jax.ShapeDtypeStruct(gates.shape, F32),
        in_specs=[whole()] * 3,
        out_specs=whole(),
        compiler_params=limit(4),
        name="match",
    )(returned, routes, gates)
    return (d_hidden[None], d_down[None], d_gate.T)


def solution(mesh):
    parts, experts = mesh.devices.shape
    devices = mesh.devices.reshape(2, parts // 4, 2, experts)
    finer = Mesh(devices, ("x", "y", "core", "expert"))
    dp = ("x", "y", "core")
    in_specs = (
        P("expert", dp),
        P("expert", None),
        P("expert", None),
        P("expert", None, dp),
        P("expert", dp, None),
    )
    out_specs = (P("expert", None, dp), P("expert", dp, None), P("expert", None))
    return jax.shard_map(
        on_device, mesh=finer, in_specs=in_specs, out_specs=out_specs, check_vma=False
    )
```

```python
import functools

import jax
import jax.numpy as jnp
from jax import lax
from jax.experimental import pallas as pl
from jax.experimental.pallas import tpu as pltpu
from jax.sharding import Mesh, PartitionSpec as P

F32 = jnp.float32
BF16 = jnp.bfloat16
LANES = 128


def ranks(routes, experts):
    top, tokens = routes.shape
    ids = lax.broadcasted_iota(jnp.int32, (experts, tokens), 0)
    named = [routes[k : k + 1, :] == ids for k in range(top)]
    present = functools.reduce(jnp.logical_or, named)
    rows = lax.broadcasted_iota(jnp.int32, (tokens, tokens), 0)
    columns = lax.broadcasted_iota(jnp.int32, (tokens, tokens), 1)
    earlier = (rows < columns).astype(F32)
    before = jnp.dot(present.astype(F32), earlier, preferred_element_type=F32)
    return named, present, before


def pack_kernel(grad_ref, routes_ref, gates_ref, out_ref):
    experts, lines, length = out_ref.shape
    grad = grad_ref[...]
    fitting = length // grad.shape[1]
    named, present, before = ranks(routes_ref[...], experts)
    gates = gates_ref[...]
    gate = jnp.zeros(present.shape, F32)
    for k, here in enumerate(named):
        gate = jnp.where(here, gates[k : k + 1, :], gate)

    def slot(c):
        placed = jnp.logical_and(present, before == c).astype(F32)
        row_gate = jnp.sum(placed * gate, axis=1, keepdims=True)
        return row_gate * jnp.dot(
            placed.astype(BF16), grad, preferred_element_type=F32
        )

    for line in range(lines):
        rows = [slot(fitting * line + i) for i in range(fitting)]
        out_ref[:, line, :] = jnp.concatenate(rows, axis=1).astype(BF16)


def unpack_kernel(in_ref, out_ref, flipped, done):
    sources, lines, length = in_ref.shape
    share, slots = flipped.shape
    fitting = length // share
    rows = [in_ref[:, line, :].astype(F32) for line in range(lines)]
    group = LANES // sources
    for g in range(slots // LANES):
        parts = []
        for c in range(g * group, (g + 1) * group):
            start = share * (c % fitting)
            parts.append(rows[c // fitting][:, start : start + share])
        block = jnp.concatenate(parts, axis=0)
        flipped[:, LANES * g : LANES * (g + 1)] = block.T.astype(BF16)
    copies = [
        pltpu.make_async_copy(flipped, out_ref.at[i], done.at[i])
        for i in range(out_ref.shape[0])
    ]
    for copy in copies:
        copy.start()
    for copy in copies:
        copy.wait()


def cases(place_ref, body):
    for far in range(2):
        for core in range(2):
            here = jnp.logical_and(place_ref[0] == far, place_ref[1] == core)
            pl.when(here)(functools.partial(body, far, core))


def columns(far, core, y, blocks, share):
    start = ((far * blocks + y) * 2 + core) * share
    return slice(start, start + share)


def split_kernel(
    sources,
    place_ref,
    weight_ref,
    hidden_ref,
    keep_ref,
    far_ref,
    later_ref,
    order_ref,
):
    slots = hidden_ref.shape[0]
    all_mine = keep_ref.shape[1] - slots
    blocks = 4
    share = all_mine // (2 * blocks)
    capacity = slots // sources
    rows = lax.broadcasted_iota(jnp.int32, (slots, slots), 0)
    cols = lax.broadcasted_iota(jnp.int32, (slots, slots), 1)
    matches = (rows % capacity) * sources + rows // capacity == cols
    order = matches.astype(F32).astype(BF16)
    order_ref[...] = order
    flipped = lax.dot_general(
        hidden_ref[...], order, (((0,), (0,)), ((), ())), preferred_element_type=F32
    ).astype(BF16)

    mine = blocks * share

    def store(far, core):
        def part(f, c):
            pieces = [
                weight_ref[:, columns(f, c, y, blocks, share)] for y in range(blocks)
            ]
            return jnp.concatenate(pieces, axis=1)

        keep_ref[:, :mine] = part(far, core)
        keep_ref[:, mine:all_mine] = part(far, 1 - core)
        keep_ref[:, all_mine:] = flipped
        far_ref[...] = part(1 - far, core)
        later_ref[:, :mine] = part(1 - far, 1 - core)
        later_ref[:, mine:] = flipped

    cases(place_ref, store)


def values_kernel(
    own_ref,
    other_ref,
    keep_ref,
    far_ref,
    later_ref,
    mine_ref,
    theirs_ref,
    gate_ref,
    weight,
    done,
    hidden,
    ready,
):
    blocks, share, slots = own_ref.shape
    units, wide, mine = mine_ref.shape[0], 2 * share, blocks * share
    steps = blocks // 2
    copies = []
    for step in range(2 * steps):
        here = pl.ds(step * wide, wide)
        if step < steps:
            from_far = far_ref.at[:, here]
        else:
            from_far = later_ref.at[:, pl.ds(step * wide - mine, wide)]
        copies.append(
            [
                pltpu.make_async_copy(ref, weight.at[step, k], done.at[step, k])
                for k, ref in enumerate((keep_ref.at[:, here], from_far))
            ]
        )
    last = activations(keep_ref, later_ref, 2 * mine, mine, hidden, ready)
    for now in copies + [last]:
        for copy in now:
            copy.start()
    values = jnp.zeros((2 * units, slots), F32)
    for step, now in enumerate(copies):
        for copy in now:
            copy.wait()
        rows = weight[step].reshape(2 * units, wide)
        ref, first = (own_ref, step) if step < steps else (other_ref, step - steps)
        block = ref[2 * first : 2 * first + 2].reshape(wide, slots)
        values += jnp.dot(rows, block, preferred_element_type=F32)
    for copy in last:
        copy.wait()
    left = hidden[...].reshape(2 * units, slots).astype(F32)
    terms = jnp.sum(left * values, axis=0, keepdims=True)
    mine_ref[...] = values[:units]
    theirs_ref[...] = values[units:]
    lines = [terms[:, i : i + LANES] for i in range(0, slots, LANES)]
    gate_ref[...] = jnp.broadcast_to(jnp.concatenate(lines, axis=0), gate_ref.shape)


def activations(keep_ref, far_ref, keep_start, far_start, hidden, ready):
    slots = hidden.shape[2]
    return [
        pltpu.make_async_copy(ref.at[:, pl.ds(start, slots)], hidden.at[k], ready.at[k])
        for k, (ref, start) in enumerate(((keep_ref, keep_start), (far_ref, far_start)))
    ]


def down_kernel(disp_ref, keep_ref, far_ref, mine_ref, send_ref, hidden, ready):
    blocks, share, slots = disp_ref.shape
    units, wide, mine = hidden.shape[1], 2 * share, blocks * share
    copies = activations(keep_ref, far_ref, 2 * mine, mine, hidden, ready)
    for copy in copies:
        copy.start()
    for copy in copies:
        copy.wait()
    left = hidden[...].reshape(2 * units, slots)
    for step in range(blocks // 2):
        block = disp_ref[2 * step : 2 * step + 2].reshape(wide, slots)
        down = lax.dot_general(
            left, block, (((1,), (1,)), ((), ())), preferred_element_type=F32
        ).astype(BF16)
        mine_ref[:, wide * step : wide * (step + 1)] = down[:units]
        send_ref[:, wide * step : wide * (step + 1)] = down[units:]


def rest_kernel(
    disp_ref, keep_ref, far_ref, values_ref, mine_ref, send_ref, hidden, ready
):
    down_kernel(disp_ref, keep_ref, far_ref, mine_ref, send_ref, hidden, ready)
    mine, slots = mine_ref.shape[1], values_ref.shape[1]
    values = values_ref[...]
    high = values.astype(BF16)
    send_ref[:, mine : mine + slots] = high
    send_ref[:, mine + slots :] = (values - high.astype(F32)).astype(BF16)


def finish_kernel(
    place_ref,
    own_ref,
    other_ref,
    got_own_ref,
    got_other_ref,
    values_ref,
    order_ref,
    down_ref,
    dhid_ref,
):
    slots = values_ref.shape[1]
    mine = own_ref.shape[1]
    blocks = 4
    share = mine // blocks

    def store(far, core):
        for f in range(2):
            refs = (own_ref, other_ref) if f == far else (got_own_ref, got_other_ref)
            refs = refs if core == 0 else refs[::-1]
            for y in range(blocks):
                pair = [ref[:, share * y : share * (y + 1)] for ref in refs]
                start = 2 * share * (f * blocks + y)
                down_ref[:, start : start + 2 * share] = jnp.concatenate(pair, axis=1)

    cases(place_ref, store)
    high = got_other_ref[:, mine : mine + slots].astype(F32)
    low = got_other_ref[:, mine + slots :].astype(F32)
    flipped = (values_ref[...] + (high + low)).T.astype(BF16)
    dhid_ref[...] = jnp.dot(
        order_ref[...], flipped, preferred_element_type=F32
    ).astype(BF16)


def sum_kernel(far, parts_ref, out_ref):
    near, width = out_ref.shape
    terms = jnp.sum(parts_ref[...], axis=0)
    capacity = width // far
    rows = []
    for f in range(far):
        for c in range(capacity):
            line, lane = divmod((c * far + f) * near, LANES)
            rows.append(terms[line : line + 1, lane : lane + near])
    out_ref[...] = jnp.concatenate(rows, axis=0).T


def gate_kernel(near, terms_ref, routes_ref, gates_ref, out_ref):
    far, _, length = terms_ref.shape
    named, present, before = ranks(routes_ref[...], far * near)
    matched = jnp.zeros(present.shape, F32)
    for c in range(length // near):
        pieces = [terms_ref[f, :, near * c : near * (c + 1)] for f in range(far)]
        row = jnp.concatenate(pieces, axis=1)
        spread = jnp.broadcast_to(row, (8, far * near)).T[:, :1]
        here = jnp.logical_and(present, before == c)
        matched = jnp.where(here, spread, matched)
    total = [jnp.sum(jnp.where(n, matched, 0.0), axis=0, keepdims=True) for n in named]
    out_ref[...] = jnp.concatenate(total, axis=0) / gates_ref[...]


def whole():
    return pl.BlockSpec(memory_space=pltpu.VMEM)


def scalar():
    return pl.BlockSpec(memory_space=pltpu.SMEM)


def stays():
    return pl.BlockSpec(memory_space=pltpu.HBM)


def in_hbm(x):
    return pltpu.with_memory_space_constraint(x, pltpu.HBM)


def in_vmem(x):
    return pltpu.with_memory_space_constraint(x, pltpu.VMEM)


def limit(mib):
    return pltpu.CompilerParams(vmem_limit_bytes=mib * 2**20)


def cost(flops, moved):
    return pl.CostEstimate(flops=flops, bytes_accessed=moved, transcendentals=0)


def swap_all(x, axis):
    return lax.all_to_all(x, axis, split_axis=0, concat_axis=0, tiled=True)


def on_device(grad_out, routes, gates, hidden, w_down):
    near, far = lax.axis_size("near"), lax.axis_size("far")
    experts, rows_y = near * far, lax.axis_size("y")
    _, slots, units = hidden.shape
    width = w_down.shape[2]
    capacity = slots // experts
    share = grad_out.shape[1]
    mine = rows_y * share
    place = jnp.stack([lax.axis_index("x"), lax.axis_index("core")]).astype(jnp.int32)
    routes, gates = routes.T, gates.T
    bf16 = functools.partial(pltpu.HBM, dtype=BF16)
    f32 = functools.partial(pltpu.HBM, dtype=F32)

    def other(x, axis):
        return lax.ppermute(x, axis, [(0, 1), (1, 0)])

    packed = pl.pallas_call(
        pack_kernel,
        out_shape=jax.ShapeDtypeStruct((experts, 2, capacity * share // 2), BF16),
        in_specs=[whole()] * 3,
        out_specs=whole(),
        name="pack",
    )(grad_out, routes, gates)
    arrived = swap_all(packed, ("far", "near"))

    keep, to_far, to_far_later, order = pl.pallas_call(
        functools.partial(split_kernel, experts),
        out_shape=(
            bf16((units, 2 * mine + slots)),
            bf16((units, mine)),
            bf16((units, mine + slots)),
            bf16((slots, slots)),
        ),
        in_specs=[scalar(), whole(), whole()],
        out_specs=(whole(),) * 4,
        cost_estimate=cost(2 * units * slots * slots, 2 * 2 * units * width),
        name="split",
    )(place, w_down[0], hidden[0])
    from_far = other(to_far, "x")
    arrived, from_far, to_far_later = lax.optimization_barrier(
        (arrived, from_far, to_far_later)
    )
    later = other(to_far_later, "x")

    copies = pl.pallas_call(
        unpack_kernel,
        out_shape=bf16((rows_y, share, slots)),
        in_specs=[whole()],
        out_specs=pl.BlockSpec(memory_space=pl.ANY),
        scratch_shapes=[
            pltpu.VMEM((share, slots), BF16),
            pltpu.SemaphoreType.DMA((rows_y,)),
        ],
        compiler_params=limit(8),
        name="unpack",
    )(arrived)
    dispatched, later = lax.optimization_barrier((swap_all(copies, "y"), later))
    from_core = other(dispatched, "core")
    dispatched = in_vmem(dispatched)

    keep, from_far, later = in_hbm(keep), in_hbm(from_far), in_vmem(later)
    flops = 2 * slots * units * width
    moved = slots * width + 2 * units * width
    scratch = [
        pltpu.VMEM((2, units, slots), BF16),
        pltpu.SemaphoreType.DMA((2,)),
    ]
    down_own, back_own = pl.pallas_call(
        down_kernel,
        out_shape=(bf16((units, mine)), bf16((units, mine))),
        in_specs=[whole(), stays(), whole()],
        out_specs=(whole(),) * 2,
        scratch_shapes=scratch,
        compiler_params=limit(16),
        cost_estimate=cost(flops // 2, moved // 2),
        name="down",
    )(dispatched, keep, later)
    from_core, back_own = lax.optimization_barrier((from_core, back_own))
    got_own = other(back_own, "x")

    mine_values, theirs, terms = pl.pallas_call(
        values_kernel,
        out_shape=(
            f32((units, slots)),
            f32((units, slots)),
            jax.ShapeDtypeStruct((4 * rows_y, slots // LANES, LANES), F32),
        ),
        in_specs=[whole()] * 2 + [stays()] * 2 + [whole()],
        out_specs=(whole(),) * 3,
        scratch_shapes=[
            pltpu.VMEM((rows_y, 2, units, 2 * share), BF16),
            pltpu.SemaphoreType.DMA((rows_y, 2)),
        ]
        + scratch,
        compiler_params=limit(16),
        cost_estimate=cost(flops, moved),
        name="values",
    )(dispatched, in_vmem(from_core), keep, from_far, later)
    parts = swap_all(terms, ("x", "y", "core"))

    down_other, back_other = pl.pallas_call(
        rest_kernel,
        out_shape=(bf16((units, mine)), bf16((units, mine + 2 * slots))),
        in_specs=[whole(), stays(), whole(), whole()],
        out_specs=(whole(),) * 2,
        scratch_shapes=scratch,
        compiler_params=limit(16),
        cost_estimate=cost(flops // 2, moved // 2),
        name="rest",
    )(in_vmem(from_core), keep, later, in_hbm(theirs))
    parts, back_other, got_own = lax.optimization_barrier((parts, back_other, got_own))
    got_other = other(back_other, "x")

    d_down, d_hidden = pl.pallas_call(
        finish_kernel,
        out_shape=(
            jax.ShapeDtypeStruct((units, width), BF16),
            jax.ShapeDtypeStruct((slots, units), BF16),
        ),
        in_specs=[scalar()] + [whole()] * 6,
        out_specs=(whole(),) * 2,
        compiler_params=limit(16),
        cost_estimate=cost(2 * units * slots * slots, 4 * units * width),
        name="finish",
    )(
        place,
        in_hbm(down_own),
        in_hbm(down_other),
        in_vmem(got_own),
        in_vmem(got_other),
        in_hbm(mine_values),
        in_hbm(order),
    )

    sums = pl.pallas_call(
        functools.partial(sum_kernel, far),
        out_shape=jax.ShapeDtypeStruct((near, far * capacity), F32),
        in_specs=[whole()],
        out_specs=whole(),
        compiler_params=limit(4),
        name="sum",
    )(parts)
    returned = swap_all(sums, "near")
    returned = returned.reshape(near, far, capacity).transpose(1, 2, 0)
    returned = swap_all(returned.reshape(far, 1, capacity * near), "far")
    returned, _ = lax.optimization_barrier((returned, d_hidden))
    d_gate = pl.pallas_call(
        functools.partial(gate_kernel, near),
        out_shape=jax.ShapeDtypeStruct(gates.shape, F32),
        in_specs=[whole()] * 3,
        out_specs=whole(),
        compiler_params=limit(4),
        name="match",
    )(returned, routes, gates)
    return (d_hidden[None], d_down[None], d_gate.T)


def solution(mesh):
    parts, experts = mesh.devices.shape
    devices = mesh.devices.reshape(2, parts // 4, 2, 2, experts // 2)
    finer = Mesh(devices, ("x", "y", "core", "far", "near"))
    dp, expert = ("x", "y", "core"), ("far", "near")
    in_specs = (
        P(expert, dp),
        P(expert, None),
        P(expert, None),
        P(expert, None, dp),
        P(expert, dp, None),
    )
    out_specs = (P(expert, None, dp), P(expert, dp, None), P(expert, None))
    return jax.shard_map(
        on_device, mesh=finer, in_specs=in_specs, out_specs=out_specs, check_vma=False
    )
```

```python
import functools

import jax
import jax.numpy as jnp
from jax import lax
from jax.experimental import pallas as pl
from jax.experimental.pallas import tpu as pltpu
from jax.sharding import Mesh, PartitionSpec as P

F32 = jnp.float32
BF16 = jnp.bfloat16
LANES = 128


def ranks(routes, experts):
    top, tokens = routes.shape
    ids = lax.broadcasted_iota(jnp.int32, (experts, tokens), 0)
    named = [routes[k : k + 1, :] == ids for k in range(top)]
    present = functools.reduce(jnp.logical_or, named)
    rows = lax.broadcasted_iota(jnp.int32, (tokens, tokens), 0)
    columns = lax.broadcasted_iota(jnp.int32, (tokens, tokens), 1)
    earlier = (rows < columns).astype(F32)
    before = jnp.dot(present.astype(F32), earlier, preferred_element_type=F32)
    return named, present, before


def pack_kernel(grad_ref, routes_ref, gates_ref, out_ref):
    experts, lines, length = out_ref.shape
    grad = grad_ref[...]
    fitting = length // grad.shape[1]
    named, present, before = ranks(routes_ref[...], experts)
    gates = gates_ref[...]
    gate = jnp.zeros(present.shape, F32)
    for k, here in enumerate(named):
        gate = jnp.where(here, gates[k : k + 1, :], gate)

    def slot(c):
        placed = jnp.logical_and(present, before == c).astype(F32)
        row_gate = jnp.sum(placed * gate, axis=1, keepdims=True)
        return row_gate * jnp.dot(
            placed.astype(BF16), grad, preferred_element_type=F32
        )

    for line in range(lines):
        rows = [slot(fitting * line + i) for i in range(fitting)]
        out_ref[:, line, :] = jnp.concatenate(rows, axis=1).astype(BF16)


def unpack_kernel(in_ref, out_ref, flipped, done):
    sources, lines, length = in_ref.shape
    share, slots = flipped.shape
    fitting = length // share
    rows = [in_ref[:, line, :].astype(F32) for line in range(lines)]
    group = LANES // sources
    for g in range(slots // LANES):
        parts = []
        for c in range(g * group, (g + 1) * group):
            start = share * (c % fitting)
            parts.append(rows[c // fitting][:, start : start + share])
        block = jnp.concatenate(parts, axis=0)
        flipped[:, LANES * g : LANES * (g + 1)] = block.T.astype(BF16)
    copies = [
        pltpu.make_async_copy(flipped, out_ref.at[i], done.at[i])
        for i in range(out_ref.shape[0])
    ]
    for copy in copies:
        copy.start()
    for copy in copies:
        copy.wait()


def cases(place_ref, body):
    for far in range(2):
        for core in range(2):
            here = jnp.logical_and(place_ref[0] == far, place_ref[1] == core)
            pl.when(here)(functools.partial(body, far, core))


def columns(far, core, y, blocks, share):
    start = ((far * blocks + y) * 2 + core) * share
    return slice(start, start + share)


def split_kernel(
    sources,
    place_ref,
    weight_ref,
    hidden_ref,
    keep_ref,
    far_ref,
    later_ref,
    order_ref,
):
    slots = hidden_ref.shape[0]
    all_mine = keep_ref.shape[1] - slots
    blocks = 4
    share = all_mine // (2 * blocks)
    capacity = slots // sources
    rows = lax.broadcasted_iota(jnp.int32, (slots, slots), 0)
    cols = lax.broadcasted_iota(jnp.int32, (slots, slots), 1)
    matches = (rows % capacity) * sources + rows // capacity == cols
    order = matches.astype(F32).astype(BF16)
    order_ref[...] = order
    flipped = lax.dot_general(
        hidden_ref[...], order, (((0,), (0,)), ((), ())), preferred_element_type=F32
    ).astype(BF16)

    mine = blocks * share

    def store(far, core):
        def part(f, c):
            pieces = [
                weight_ref[:, columns(f, c, y, blocks, share)] for y in range(blocks)
            ]
            return jnp.concatenate(pieces, axis=1)

        keep_ref[:, :mine] = part(far, core)
        keep_ref[:, mine:all_mine] = part(far, 1 - core)
        keep_ref[:, all_mine:] = flipped
        far_ref[...] = part(1 - far, core)
        later_ref[:, :mine] = part(1 - far, 1 - core)
        later_ref[:, mine:] = flipped

    cases(place_ref, store)


def values_kernel(
    far,
    capacity,
    own_ref,
    other_ref,
    keep_ref,
    far_ref,
    later_ref,
    mine_ref,
    theirs_ref,
    gate_ref,
    weight,
    done,
    hidden,
    ready,
):
    blocks, share, slots = own_ref.shape
    units, wide, mine = mine_ref.shape[0], 2 * share, blocks * share
    steps = blocks // 2
    copies = []
    for step in range(2 * steps):
        here = pl.ds(step * wide, wide)
        if step < steps:
            from_far = far_ref.at[:, here]
        else:
            from_far = later_ref.at[:, pl.ds(step * wide - mine, wide)]
        copies.append(
            [
                pltpu.make_async_copy(ref, weight.at[step, k], done.at[step, k])
                for k, ref in enumerate((keep_ref.at[:, here], from_far))
            ]
        )
    last = activations(keep_ref, later_ref, 2 * mine, mine, hidden, ready)
    for now in copies + [last]:
        for copy in now:
            copy.start()
    values = jnp.zeros((2 * units, slots), F32)
    for step, now in enumerate(copies):
        for copy in now:
            copy.wait()
        rows = weight[step].reshape(2 * units, wide)
        ref, first = (own_ref, step) if step < steps else (other_ref, step - steps)
        block = ref[2 * first : 2 * first + 2].reshape(wide, slots)
        values += jnp.dot(rows, block, preferred_element_type=F32)
    for copy in last:
        copy.wait()
    left = hidden[...].reshape(2 * units, slots).astype(F32)
    terms = jnp.sum(left * values, axis=0, keepdims=True)
    mine_ref[...] = values[:units]
    theirs_ref[...] = values[units:]
    copies, near = gate_ref.shape[0] // far, gate_ref.shape[2] // capacity
    for f in range(far):
        starts = [(c * far + f) * near for c in range(capacity)]
        row = jnp.concatenate([terms[:, i : i + near] for i in starts], axis=1)
        gate_ref[f * copies : (f + 1) * copies] = jnp.broadcast_to(
            row[None], (copies, *row.shape)
        )


def activations(keep_ref, far_ref, keep_start, far_start, hidden, ready):
    slots = hidden.shape[2]
    return [
        pltpu.make_async_copy(ref.at[:, pl.ds(start, slots)], hidden.at[k], ready.at[k])
        for k, (ref, start) in enumerate(((keep_ref, keep_start), (far_ref, far_start)))
    ]


def down_kernel(disp_ref, keep_ref, far_ref, mine_ref, send_ref, hidden, ready):
    blocks, share, slots = disp_ref.shape
    units, wide, mine = hidden.shape[1], 2 * share, blocks * share
    copies = activations(keep_ref, far_ref, 2 * mine, mine, hidden, ready)
    for copy in copies:
        copy.start()
    for copy in copies:
        copy.wait()
    left = hidden[...].reshape(2 * units, slots)
    for step in range(blocks // 2):
        block = disp_ref[2 * step : 2 * step + 2].reshape(wide, slots)
        down = lax.dot_general(
            left, block, (((1,), (1,)), ((), ())), preferred_element_type=F32
        ).astype(BF16)
        mine_ref[:, wide * step : wide * (step + 1)] = down[:units]
        send_ref[:, wide * step : wide * (step + 1)] = down[units:]


def rest_kernel(
    disp_ref, keep_ref, far_ref, values_ref, mine_ref, send_ref, hidden, ready
):
    down_kernel(disp_ref, keep_ref, far_ref, mine_ref, send_ref, hidden, ready)
    mine, slots = mine_ref.shape[1], values_ref.shape[1]
    values = values_ref[...]
    high = values.astype(BF16)
    send_ref[:, mine : mine + slots] = high
    send_ref[:, mine + slots :] = (values - high.astype(F32)).astype(BF16)


def finish_kernel(
    place_ref,
    own_ref,
    other_ref,
    got_own_ref,
    got_other_ref,
    values_ref,
    order_ref,
    down_ref,
    dhid_ref,
):
    slots = values_ref.shape[1]
    mine = own_ref.shape[1]
    blocks = 4
    share = mine // blocks

    def store(far, core):
        for f in range(2):
            refs = (own_ref, other_ref) if f == far else (got_own_ref, got_other_ref)
            refs = refs if core == 0 else refs[::-1]
            for y in range(blocks):
                pair = [ref[:, share * y : share * (y + 1)] for ref in refs]
                start = 2 * share * (f * blocks + y)
                down_ref[:, start : start + 2 * share] = jnp.concatenate(pair, axis=1)

    cases(place_ref, store)
    high = got_other_ref[:, mine : mine + slots].astype(F32)
    low = got_other_ref[:, mine + slots :].astype(F32)
    flipped = (values_ref[...] + (high + low)).T.astype(BF16)
    dhid_ref[...] = jnp.dot(
        order_ref[...], flipped, preferred_element_type=F32
    ).astype(BF16)


def sum_kernel(far, parts_ref, out_ref):
    near, width = out_ref.shape
    copies = parts_ref.shape[0] // far
    rows = []
    for f in range(far):
        terms = jnp.sum(parts_ref[f * copies : (f + 1) * copies], axis=0)
        for c in range(width // far):
            rows.append(terms[:, near * c : near * (c + 1)])
    out_ref[...] = jnp.concatenate(rows, axis=0).T


def gate_kernel(far, terms_ref, routes_ref, gates_ref, out_ref):
    near, width = terms_ref.shape
    capacity = width // far
    named, present, before = ranks(routes_ref[...], far * near)
    matched = jnp.zeros(present.shape, F32)
    for c in range(capacity):
        columns = [
            terms_ref[:, f * capacity + c : f * capacity + c + 1] for f in range(far)
        ]
        here = jnp.logical_and(present, before == c)
        matched = jnp.where(here, jnp.concatenate(columns, axis=0), matched)
    total = [jnp.sum(jnp.where(n, matched, 0.0), axis=0, keepdims=True) for n in named]
    out_ref[...] = jnp.concatenate(total, axis=0) / gates_ref[...]


def whole():
    return pl.BlockSpec(memory_space=pltpu.VMEM)


def scalar():
    return pl.BlockSpec(memory_space=pltpu.SMEM)


def stays():
    return pl.BlockSpec(memory_space=pltpu.HBM)


def in_hbm(x):
    return pltpu.with_memory_space_constraint(x, pltpu.HBM)


def in_vmem(x):
    return pltpu.with_memory_space_constraint(x, pltpu.VMEM)


def limit(mib):
    return pltpu.CompilerParams(vmem_limit_bytes=mib * 2**20)


def cost(flops, moved):
    return pl.CostEstimate(flops=flops, bytes_accessed=moved, transcendentals=0)


def swap_all(x, axis):
    return lax.all_to_all(x, axis, split_axis=0, concat_axis=0, tiled=True)


def on_device(grad_out, routes, gates, hidden, w_down):
    near, far = lax.axis_size("near"), lax.axis_size("far")
    experts, rows_y = near * far, lax.axis_size("y")
    _, slots, units = hidden.shape
    width = w_down.shape[2]
    capacity = slots // experts
    share = grad_out.shape[1]
    mine = rows_y * share
    place = jnp.stack([lax.axis_index("x"), lax.axis_index("core")]).astype(jnp.int32)
    routes, gates = routes.T, gates.T
    bf16 = functools.partial(pltpu.HBM, dtype=BF16)
    f32 = functools.partial(pltpu.HBM, dtype=F32)

    def other(x, axis):
        return lax.ppermute(x, axis, [(0, 1), (1, 0)])

    packed = pl.pallas_call(
        pack_kernel,
        out_shape=jax.ShapeDtypeStruct((experts, 2, capacity * share // 2), BF16),
        in_specs=[whole()] * 3,
        out_specs=whole(),
        name="pack",
    )(grad_out, routes, gates)
    arrived = swap_all(packed, ("far", "near"))

    keep, to_far, to_far_later, order = pl.pallas_call(
        functools.partial(split_kernel, experts),
        out_shape=(
            bf16((units, 2 * mine + slots)),
            bf16((units, mine)),
            bf16((units, mine + slots)),
            bf16((slots, slots)),
        ),
        in_specs=[scalar(), whole(), whole()],
        out_specs=(whole(),) * 4,
        cost_estimate=cost(2 * units * slots * slots, 2 * 2 * units * width),
        name="split",
    )(place, w_down[0], hidden[0])
    from_far = other(to_far, "x")
    arrived, from_far, to_far_later = lax.optimization_barrier(
        (arrived, from_far, to_far_later)
    )
    later = other(to_far_later, "x")

    copies = pl.pallas_call(
        unpack_kernel,
        out_shape=bf16((rows_y, share, slots)),
        in_specs=[whole()],
        out_specs=pl.BlockSpec(memory_space=pl.ANY),
        scratch_shapes=[
            pltpu.VMEM((share, slots), BF16),
            pltpu.SemaphoreType.DMA((rows_y,)),
        ],
        compiler_params=limit(8),
        name="unpack",
    )(arrived)
    dispatched, later = lax.optimization_barrier((swap_all(copies, "y"), later))
    from_core = other(dispatched, "core")
    dispatched = in_vmem(dispatched)

    keep, from_far, later = in_hbm(keep), in_hbm(from_far), in_vmem(later)
    flops = 2 * slots * units * width
    moved = slots * width + 2 * units * width
    scratch = [
        pltpu.VMEM((2, units, slots), BF16),
        pltpu.SemaphoreType.DMA((2,)),
    ]
    down_own, back_own = pl.pallas_call(
        down_kernel,
        out_shape=(bf16((units, mine)), bf16((units, mine))),
        in_specs=[whole(), stays(), whole()],
        out_specs=(whole(),) * 2,
        scratch_shapes=scratch,
        compiler_params=limit(16),
        cost_estimate=cost(flops // 2, moved // 2),
        name="down",
    )(dispatched, keep, later)
    from_core, back_own = lax.optimization_barrier((from_core, back_own))
    got_own = other(back_own, "x")

    mine_values, theirs, terms = pl.pallas_call(
        functools.partial(values_kernel, far, capacity),
        out_shape=(
            f32((units, slots)),
            f32((units, slots)),
            jax.ShapeDtypeStruct((far * 4 * rows_y, 1, capacity * near), F32),
        ),
        in_specs=[whole()] * 2 + [stays()] * 2 + [whole()],
        out_specs=(whole(),) * 3,
        scratch_shapes=[
            pltpu.VMEM((rows_y, 2, units, 2 * share), BF16),
            pltpu.SemaphoreType.DMA((rows_y, 2)),
        ]
        + scratch,
        compiler_params=limit(16),
        cost_estimate=cost(flops, moved),
        name="values",
    )(dispatched, in_vmem(from_core), keep, from_far, later)
    parts = swap_all(terms, ("far", "x", "y", "core"))

    down_other, back_other = pl.pallas_call(
        rest_kernel,
        out_shape=(bf16((units, mine)), bf16((units, mine + 2 * slots))),
        in_specs=[whole(), stays(), whole(), whole()],
        out_specs=(whole(),) * 2,
        scratch_shapes=scratch,
        compiler_params=limit(16),
        cost_estimate=cost(flops // 2, moved // 2),
        name="rest",
    )(in_vmem(from_core), keep, later, in_hbm(theirs))
    parts, back_other, got_own = lax.optimization_barrier((parts, back_other, got_own))
    got_other = other(back_other, "x")

    d_down, d_hidden = pl.pallas_call(
        finish_kernel,
        out_shape=(
            jax.ShapeDtypeStruct((units, width), BF16),
            jax.ShapeDtypeStruct((slots, units), BF16),
        ),
        in_specs=[scalar()] + [whole()] * 6,
        out_specs=(whole(),) * 2,
        compiler_params=limit(16),
        cost_estimate=cost(2 * units * slots * slots, 4 * units * width),
        name="finish",
    )(
        place,
        in_hbm(down_own),
        in_hbm(down_other),
        in_vmem(got_own),
        in_vmem(got_other),
        in_hbm(mine_values),
        in_hbm(order),
    )

    sums = pl.pallas_call(
        functools.partial(sum_kernel, far),
        out_shape=jax.ShapeDtypeStruct((near, far * capacity), F32),
        in_specs=[whole()],
        out_specs=whole(),
        compiler_params=limit(4),
        name="sum",
    )(parts)
    returned = swap_all(sums, "near")
    returned, _ = lax.optimization_barrier((returned, d_hidden))
    d_gate = pl.pallas_call(
        functools.partial(gate_kernel, far),
        out_shape=jax.ShapeDtypeStruct(gates.shape, F32),
        in_specs=[whole()] * 3,
        out_specs=whole(),
        compiler_params=limit(4),
        name="match",
    )(returned, routes, gates)
    return (d_hidden[None], d_down[None], d_gate.T)


def solution(mesh):
    parts, experts = mesh.devices.shape
    devices = mesh.devices.reshape(2, parts // 4, 2, 2, experts // 2)
    finer = Mesh(devices, ("x", "y", "core", "far", "near"))
    dp, expert = ("x", "y", "core"), ("far", "near")
    in_specs = (
        P(expert, dp),
        P(expert, None),
        P(expert, None),
        P(expert, None, dp),
        P(expert, dp, None),
    )
    out_specs = (P(expert, None, dp), P(expert, dp, None), P(expert, None))
    return jax.shard_map(
        on_device, mesh=finer, in_specs=in_specs, out_specs=out_specs, check_vma=False
    )
```

```python
import functools

import jax
import jax.numpy as jnp
from jax import lax
from jax.experimental import pallas as pl
from jax.experimental.pallas import tpu as pltpu
from jax.sharding import Mesh, PartitionSpec as P

F32 = jnp.float32
BF16 = jnp.bfloat16
LANES = 128


def ranks(routes, experts):
    top, tokens = routes.shape
    ids = lax.broadcasted_iota(jnp.int32, (experts, tokens), 0)
    named = [routes[k : k + 1, :] == ids for k in range(top)]
    present = functools.reduce(jnp.logical_or, named)
    rows = lax.broadcasted_iota(jnp.int32, (tokens, tokens), 0)
    columns = lax.broadcasted_iota(jnp.int32, (tokens, tokens), 1)
    earlier = (rows < columns).astype(F32)
    before = jnp.dot(present.astype(F32), earlier, preferred_element_type=F32)
    return named, present, before


def pack_kernel(grad_ref, routes_ref, gates_ref, out_ref):
    experts, lines, length = out_ref.shape
    grad = grad_ref[...]
    fitting = length // grad.shape[1]
    named, present, before = ranks(routes_ref[...], experts)
    gates = gates_ref[...]
    gate = jnp.zeros(present.shape, F32)
    for k, here in enumerate(named):
        gate = jnp.where(here, gates[k : k + 1, :], gate)

    def slot(c):
        placed = jnp.logical_and(present, before == c).astype(F32)
        row_gate = jnp.sum(placed * gate, axis=1, keepdims=True)
        return row_gate * jnp.dot(
            placed.astype(BF16), grad, preferred_element_type=F32
        )

    for line in range(lines):
        rows = [slot(fitting * line + i) for i in range(fitting)]
        out_ref[:, line, :] = jnp.concatenate(rows, axis=1).astype(BF16)


def unpack_kernel(in_ref, out_ref, flipped, done):
    sources, lines, length = in_ref.shape
    share, slots = flipped.shape
    fitting = length // share
    rows = [in_ref[:, line, :].astype(F32) for line in range(lines)]
    group = LANES // sources
    for g in range(slots // LANES):
        parts = []
        for c in range(g * group, (g + 1) * group):
            start = share * (c % fitting)
            parts.append(rows[c // fitting][:, start : start + share])
        block = jnp.concatenate(parts, axis=0)
        flipped[:, LANES * g : LANES * (g + 1)] = block.T.astype(BF16)
    copies = [
        pltpu.make_async_copy(flipped, out_ref.at[i], done.at[i])
        for i in range(out_ref.shape[0])
    ]
    for copy in copies:
        copy.start()
    for copy in copies:
        copy.wait()


def cases(place_ref, body):
    for far in range(2):
        for core in range(2):
            here = jnp.logical_and(place_ref[0] == far, place_ref[1] == core)
            pl.when(here)(functools.partial(body, far, core))


def columns(far, core, y, blocks, share):
    start = ((far * blocks + y) * 2 + core) * share
    return slice(start, start + share)


def split_kernel(
    sources,
    place_ref,
    weight_ref,
    hidden_ref,
    keep_ref,
    far_ref,
    later_ref,
    order_ref,
):
    slots = hidden_ref.shape[0]
    all_mine = keep_ref.shape[1] - slots
    blocks = 4
    share = all_mine // (2 * blocks)
    capacity = slots // sources
    rows = lax.broadcasted_iota(jnp.int32, (slots, slots), 0)
    cols = lax.broadcasted_iota(jnp.int32, (slots, slots), 1)
    matches = (rows % capacity) * sources + rows // capacity == cols
    order = matches.astype(F32).astype(BF16)
    order_ref[...] = order
    flipped = lax.dot_general(
        hidden_ref[...], order, (((0,), (0,)), ((), ())), preferred_element_type=F32
    ).astype(BF16)

    mine = blocks * share

    def store(far, core):
        def part(f, c):
            pieces = [
                weight_ref[:, columns(f, c, y, blocks, share)] for y in range(blocks)
            ]
            return jnp.concatenate(pieces, axis=1)

        keep_ref[:, :mine] = part(far, core)
        keep_ref[:, mine:all_mine] = part(far, 1 - core)
        keep_ref[:, all_mine:] = flipped
        far_ref[...] = part(1 - far, core)
        later_ref[:, :mine] = part(1 - far, 1 - core)
        later_ref[:, mine:] = flipped

    cases(place_ref, store)


def values_kernel(
    far,
    capacity,
    own_ref,
    other_ref,
    keep_ref,
    far_ref,
    later_ref,
    mine_ref,
    theirs_ref,
    gate_ref,
    weight,
    done,
    hidden,
    ready,
):
    blocks, share, slots = own_ref.shape
    units, wide, mine = mine_ref.shape[0], 2 * share, blocks * share
    steps = blocks // 2
    copies = []
    for step in range(2 * steps):
        here = pl.ds(step * wide, wide)
        if step < steps:
            from_far = far_ref.at[:, here]
        else:
            from_far = later_ref.at[:, pl.ds(step * wide - mine, wide)]
        copies.append(
            [
                pltpu.make_async_copy(ref, weight.at[step, k], done.at[step, k])
                for k, ref in enumerate((keep_ref.at[:, here], from_far))
            ]
        )
    last = activations(keep_ref, later_ref, 2 * mine, mine, hidden, ready)
    for now in copies + [last]:
        for copy in now:
            copy.start()
    values = jnp.zeros((2 * units, slots), F32)
    for step, now in enumerate(copies):
        for copy in now:
            copy.wait()
        rows = weight[step].reshape(2 * units, wide)
        ref, first = (own_ref, step) if step < steps else (other_ref, step - steps)
        block = ref[2 * first : 2 * first + 2].reshape(wide, slots)
        values += jnp.dot(rows, block, preferred_element_type=F32)
    for copy in last:
        copy.wait()
    left = hidden[...].reshape(2 * units, slots).astype(F32)
    terms = jnp.sum(left * values, axis=0, keepdims=True)
    mine_ref[...] = values[:units]
    theirs_ref[...] = values[units:]
    copies, near = gate_ref.shape[0] // far, gate_ref.shape[2] // capacity
    for f in range(far):
        starts = [(c * far + f) * near for c in range(capacity)]
        row = jnp.concatenate([terms[:, i : i + near] for i in starts], axis=1)
        gate_ref[f * copies : (f + 1) * copies] = jnp.broadcast_to(
            row[None], (copies, *row.shape)
        )


def activations(keep_ref, far_ref, keep_start, far_start, hidden, ready):
    slots = hidden.shape[2]
    return [
        pltpu.make_async_copy(ref.at[:, pl.ds(start, slots)], hidden.at[k], ready.at[k])
        for k, (ref, start) in enumerate(((keep_ref, keep_start), (far_ref, far_start)))
    ]


def down(left, disp_ref, out_ref, first):
    blocks, share, slots = disp_ref.shape
    wide = 2 * share
    for step in range(blocks // 2):
        block = disp_ref[2 * step : 2 * step + 2].reshape(wide, slots)
        part = lax.dot_general(
            left, block, (((1,), (1,)), ((), ())), preferred_element_type=F32
        )
        start = first + wide * step
        out_ref[:, start : start + wide] = part.astype(BF16)


def far_kernel(own_ref, later_ref, out_ref):
    down(later_ref[:, out_ref.shape[1] :], own_ref, out_ref, 0)


def rest_kernel(
    own_ref, other_ref, keep_ref, later_ref, values_ref, mine_ref, send_ref, hidden, done
):
    mine, slots = mine_ref.shape[1] // 2, values_ref.shape[1]
    after = pl.ds(2 * mine, slots)
    copy = pltpu.make_async_copy(keep_ref.at[:, after], hidden, done)
    copy.start()
    down(later_ref[:, mine:], other_ref, send_ref, 0)
    values = values_ref[...]
    high = values.astype(BF16)
    send_ref[:, mine : mine + slots] = high
    send_ref[:, mine + slots :] = (values - high.astype(F32)).astype(BF16)
    copy.wait()
    for half, ref in enumerate((own_ref, other_ref)):
        down(hidden[...], ref, mine_ref, half * mine)


def finish_kernel(
    place_ref,
    own_ref,
    got_own_ref,
    got_other_ref,
    values_ref,
    order_ref,
    down_ref,
    dhid_ref,
):
    slots = values_ref.shape[1]
    mine = got_own_ref.shape[1]
    blocks = 4
    share = mine // blocks

    def store(far, core):
        for f in range(2):
            refs = ((own_ref, 0), (own_ref, mine))
            if f != far:
                refs = ((got_own_ref, 0), (got_other_ref, 0))
            refs = refs if core == 0 else refs[::-1]
            for y in range(blocks):
                starts = [(ref, first + share * y) for ref, first in refs]
                pair = [ref[:, start : start + share] for ref, start in starts]
                start = 2 * share * (f * blocks + y)
                down_ref[:, start : start + 2 * share] = jnp.concatenate(pair, axis=1)

    cases(place_ref, store)
    high = got_other_ref[:, mine : mine + slots].astype(F32)
    low = got_other_ref[:, mine + slots :].astype(F32)
    flipped = (values_ref[...] + (high + low)).T.astype(BF16)
    dhid_ref[...] = jnp.dot(
        order_ref[...], flipped, preferred_element_type=F32
    ).astype(BF16)


def sum_kernel(far, parts_ref, out_ref):
    near, width = out_ref.shape
    copies = parts_ref.shape[0] // far
    rows = []
    for f in range(far):
        terms = jnp.sum(parts_ref[f * copies : (f + 1) * copies], axis=0)
        for c in range(width // far):
            rows.append(terms[:, near * c : near * (c + 1)])
    out_ref[...] = jnp.concatenate(rows, axis=0).T


def gate_kernel(far, terms_ref, routes_ref, gates_ref, out_ref):
    near, width = terms_ref.shape
    capacity = width // far
    named, present, before = ranks(routes_ref[...], far * near)
    matched = jnp.zeros(present.shape, F32)
    for c in range(capacity):
        columns = [
            terms_ref[:, f * capacity + c : f * capacity + c + 1] for f in range(far)
        ]
        here = jnp.logical_and(present, before == c)
        matched = jnp.where(here, jnp.concatenate(columns, axis=0), matched)
    total = [jnp.sum(jnp.where(n, matched, 0.0), axis=0, keepdims=True) for n in named]
    out_ref[...] = jnp.concatenate(total, axis=0) / gates_ref[...]


def whole():
    return pl.BlockSpec(memory_space=pltpu.VMEM)


def scalar():
    return pl.BlockSpec(memory_space=pltpu.SMEM)


def stays():
    return pl.BlockSpec(memory_space=pltpu.HBM)


def in_hbm(x):
    return pltpu.with_memory_space_constraint(x, pltpu.HBM)


def in_vmem(x):
    return pltpu.with_memory_space_constraint(x, pltpu.VMEM)


def limit(mib):
    return pltpu.CompilerParams(vmem_limit_bytes=mib * 2**20)


def cost(flops, moved):
    return pl.CostEstimate(flops=flops, bytes_accessed=moved, transcendentals=0)


def swap_all(x, axis):
    return lax.all_to_all(x, axis, split_axis=0, concat_axis=0, tiled=True)


def on_device(grad_out, routes, gates, hidden, w_down):
    near, far = lax.axis_size("near"), lax.axis_size("far")
    experts, rows_y = near * far, lax.axis_size("y")
    _, slots, units = hidden.shape
    width = w_down.shape[2]
    capacity = slots // experts
    share = grad_out.shape[1]
    mine = rows_y * share
    place = jnp.stack([lax.axis_index("x"), lax.axis_index("core")]).astype(jnp.int32)
    routes, gates = routes.T, gates.T
    bf16 = functools.partial(pltpu.HBM, dtype=BF16)
    f32 = functools.partial(pltpu.HBM, dtype=F32)

    def other(x, axis):
        return lax.ppermute(x, axis, [(0, 1), (1, 0)])

    packed = pl.pallas_call(
        pack_kernel,
        out_shape=jax.ShapeDtypeStruct((experts, 2, capacity * share // 2), BF16),
        in_specs=[whole()] * 3,
        out_specs=whole(),
        name="pack",
    )(grad_out, routes, gates)
    arrived = swap_all(packed, ("far", "near"))

    keep, to_far, to_far_later, order = pl.pallas_call(
        functools.partial(split_kernel, experts),
        out_shape=(
            bf16((units, 2 * mine + slots)),
            bf16((units, mine)),
            bf16((units, mine + slots)),
            bf16((slots, slots)),
        ),
        in_specs=[scalar(), whole(), whole()],
        out_specs=(whole(),) * 4,
        cost_estimate=cost(2 * units * slots * slots, 2 * 2 * units * width),
        name="split",
    )(place, w_down[0], hidden[0])
    from_far = other(to_far, "x")
    arrived, from_far, to_far_later = lax.optimization_barrier(
        (arrived, from_far, to_far_later)
    )
    later = other(to_far_later, "x")

    copies = pl.pallas_call(
        unpack_kernel,
        out_shape=bf16((rows_y, share, slots)),
        in_specs=[whole()],
        out_specs=pl.BlockSpec(memory_space=pl.ANY),
        scratch_shapes=[
            pltpu.VMEM((share, slots), BF16),
            pltpu.SemaphoreType.DMA((rows_y,)),
        ],
        compiler_params=limit(8),
        name="unpack",
    )(arrived)
    dispatched, later = lax.optimization_barrier((swap_all(copies, "y"), later))
    from_core = other(dispatched, "core")
    dispatched = in_vmem(dispatched)

    keep, from_far, later = in_hbm(keep), in_hbm(from_far), in_vmem(later)
    flops = 2 * slots * units * width
    moved = slots * width + 2 * units * width
    scratch = [
        pltpu.VMEM((2, units, slots), BF16),
        pltpu.SemaphoreType.DMA((2,)),
    ]
    back_own = pl.pallas_call(
        far_kernel,
        out_shape=bf16((units, mine)),
        in_specs=[whole()] * 2,
        out_specs=whole(),
        compiler_params=limit(16),
        cost_estimate=cost(flops // 4, moved // 4),
        name="far",
    )(dispatched, later)
    from_core, _ = lax.optimization_barrier((from_core, back_own))
    got_own = other(back_own, "x")

    mine_values, theirs, terms = pl.pallas_call(
        functools.partial(values_kernel, far, capacity),
        out_shape=(
            f32((units, slots)),
            f32((units, slots)),
            jax.ShapeDtypeStruct((far * 4 * rows_y, 1, capacity * near), F32),
        ),
        in_specs=[whole()] * 2 + [stays()] * 2 + [whole()],
        out_specs=(whole(),) * 3,
        scratch_shapes=[
            pltpu.VMEM((rows_y, 2, units, 2 * share), BF16),
            pltpu.SemaphoreType.DMA((rows_y, 2)),
        ]
        + scratch,
        compiler_params=limit(16),
        cost_estimate=cost(flops, moved),
        name="values",
    )(dispatched, in_vmem(from_core), keep, from_far, later)
    parts = swap_all(terms, ("far", "x", "y", "core"))

    down_mine, back_other = pl.pallas_call(
        rest_kernel,
        out_shape=(bf16((units, 2 * mine)), bf16((units, mine + 2 * slots))),
        in_specs=[whole()] * 2 + [stays()] + [whole()] * 2,
        out_specs=(whole(),) * 2,
        scratch_shapes=[pltpu.VMEM((units, slots), BF16), pltpu.SemaphoreType.DMA],
        compiler_params=limit(16),
        cost_estimate=cost(3 * flops // 4, moved // 2),
        name="rest",
    )(dispatched, in_vmem(from_core), keep, later, in_hbm(theirs))
    parts, back_other, got_own = lax.optimization_barrier((parts, back_other, got_own))
    got_other = other(back_other, "x")

    d_down, d_hidden = pl.pallas_call(
        finish_kernel,
        out_shape=(
            jax.ShapeDtypeStruct((units, width), BF16),
            jax.ShapeDtypeStruct((slots, units), BF16),
        ),
        in_specs=[scalar()] + [whole()] * 5,
        out_specs=(whole(),) * 2,
        compiler_params=limit(16),
        cost_estimate=cost(2 * units * slots * slots, 4 * units * width),
        name="finish",
    )(
        place,
        in_hbm(down_mine),
        in_vmem(got_own),
        in_vmem(got_other),
        in_hbm(mine_values),
        in_hbm(order),
    )

    sums = pl.pallas_call(
        functools.partial(sum_kernel, far),
        out_shape=jax.ShapeDtypeStruct((near, far * capacity), F32),
        in_specs=[whole()],
        out_specs=whole(),
        compiler_params=limit(4),
        name="sum",
    )(parts)
    returned = swap_all(sums, "near")
    returned, _ = lax.optimization_barrier((returned, d_hidden))
    d_gate = pl.pallas_call(
        functools.partial(gate_kernel, far),
        out_shape=jax.ShapeDtypeStruct(gates.shape, F32),
        in_specs=[whole()] * 3,
        out_specs=whole(),
        compiler_params=limit(4),
        name="match",
    )(returned, routes, gates)
    return (d_hidden[None], d_down[None], d_gate.T)


def solution(mesh):
    parts, experts = mesh.devices.shape
    devices = mesh.devices.reshape(2, parts // 4, 2, 2, experts // 2)
    finer = Mesh(devices, ("x", "y", "core", "far", "near"))
    dp, expert = ("x", "y", "core"), ("far", "near")
    in_specs = (
        P(expert, dp),
        P(expert, None),
        P(expert, None),
        P(expert, None, dp),
        P(expert, dp, None),
    )
    out_specs = (P(expert, None, dp), P(expert, dp, None), P(expert, None))
    return jax.shard_map(
        on_device, mesh=finer, in_specs=in_specs, out_specs=out_specs, check_vma=False
    )
```

```python
import functools

import jax
import jax.numpy as jnp
from jax import lax
from jax.experimental import pallas as pl
from jax.experimental.pallas import tpu as pltpu
from jax.sharding import Mesh, PartitionSpec as P

F32 = jnp.float32
BF16 = jnp.bfloat16
LANES = 128


def ranks(routes, experts):
    top, tokens = routes.shape
    ids = lax.broadcasted_iota(jnp.int32, (experts, tokens), 0)
    named = [routes[k : k + 1, :] == ids for k in range(top)]
    present = functools.reduce(jnp.logical_or, named)
    rows = lax.broadcasted_iota(jnp.int32, (tokens, tokens), 0)
    columns = lax.broadcasted_iota(jnp.int32, (tokens, tokens), 1)
    earlier = (rows < columns).astype(F32)
    before = jnp.dot(present.astype(F32), earlier, preferred_element_type=F32)
    return named, present, before


def pack_kernel(grad_ref, routes_ref, gates_ref, out_ref):
    experts, lines, length = out_ref.shape
    grad = grad_ref[...]
    fitting = length // grad.shape[1]
    named, present, before = ranks(routes_ref[...], experts)
    gates = gates_ref[...]
    gate = jnp.zeros(present.shape, F32)
    for k, here in enumerate(named):
        gate = jnp.where(here, gates[k : k + 1, :], gate)

    def slot(c):
        placed = jnp.logical_and(present, before == c).astype(F32)
        row_gate = jnp.sum(placed * gate, axis=1, keepdims=True)
        return row_gate * jnp.dot(
            placed.astype(BF16), grad, preferred_element_type=F32
        )

    for line in range(lines):
        rows = [slot(fitting * line + i) for i in range(fitting)]
        out_ref[:, line, :] = jnp.concatenate(rows, axis=1).astype(BF16)


def unpack_kernel(in_ref, out_ref, flipped, done):
    sources, lines, length = in_ref.shape
    share, slots = flipped.shape
    fitting = length // share
    rows = [in_ref[:, line, :].astype(F32) for line in range(lines)]
    group = LANES // sources
    for g in range(slots // LANES):
        parts = []
        for c in range(g * group, (g + 1) * group):
            start = share * (c % fitting)
            parts.append(rows[c // fitting][:, start : start + share])
        block = jnp.concatenate(parts, axis=0)
        flipped[:, LANES * g : LANES * (g + 1)] = block.T.astype(BF16)
    copies = [
        pltpu.make_async_copy(flipped, out_ref.at[i], done.at[i])
        for i in range(out_ref.shape[0])
    ]
    for copy in copies:
        copy.start()
    for copy in copies:
        copy.wait()


def cases(place_ref, body):
    for far in range(2):
        for core in range(2):
            here = jnp.logical_and(place_ref[0] == far, place_ref[1] == core)
            pl.when(here)(functools.partial(body, far, core))


def columns(far, core, y, blocks, share):
    start = ((far * blocks + y) * 2 + core) * share
    return slice(start, start + share)


def split_kernel(
    sources,
    place_ref,
    weight_ref,
    hidden_ref,
    keep_ref,
    far_ref,
    later_ref,
    order_ref,
):
    slots = hidden_ref.shape[0]
    all_mine = keep_ref.shape[1] - slots
    blocks = 4
    share = all_mine // (2 * blocks)
    capacity = slots // sources
    rows = lax.broadcasted_iota(jnp.int32, (slots, slots), 0)
    cols = lax.broadcasted_iota(jnp.int32, (slots, slots), 1)
    matches = (rows % capacity) * sources + rows // capacity == cols
    order = matches.astype(F32).astype(BF16)
    order_ref[...] = order
    flipped = lax.dot_general(
        hidden_ref[...], order, (((0,), (0,)), ((), ())), preferred_element_type=F32
    ).astype(BF16)

    mine = blocks * share

    def store(far, core):
        def part(f, c):
            pieces = [
                weight_ref[:, columns(f, c, y, blocks, share)] for y in range(blocks)
            ]
            return jnp.concatenate(pieces, axis=1)

        keep_ref[:, :mine] = part(far, core)
        keep_ref[:, mine:all_mine] = part(far, 1 - core)
        keep_ref[:, all_mine:] = flipped
        far_ref[...] = part(1 - far, core)
        later_ref[:, :mine] = part(1 - far, 1 - core)
        later_ref[:, mine:] = flipped

    cases(place_ref, store)


def values_kernel(
    far,
    capacity,
    own_ref,
    other_ref,
    keep_ref,
    far_ref,
    later_ref,
    mine_ref,
    theirs_ref,
    gate_ref,
    weight,
    done,
):
    blocks, share, slots = own_ref.shape
    units, mine = mine_ref.shape[0], blocks * share
    copy = pltpu.make_async_copy(far_ref, weight, done)
    copy.start()
    values = []
    for first, second, start in ((keep_ref, keep_ref, mine), (weight, later_ref, 0)):
        if first is weight:
            copy.wait()
        values.append(
            jnp.dot(
                first[:, :mine],
                own_ref[...].reshape(mine, slots),
                preferred_element_type=F32,
            )
            + jnp.dot(
                second[:, start : start + mine],
                other_ref[...].reshape(mine, slots),
                preferred_element_type=F32,
            )
        )
    values = jnp.concatenate(values, axis=0)
    left = [keep_ref[:, 2 * mine :], later_ref[:, mine:]]
    left = jnp.concatenate(left, axis=0).astype(F32)
    terms = jnp.sum(left * values, axis=0, keepdims=True)
    mine_ref[...] = values[:units]
    theirs_ref[...] = values[units:]
    copies, near = gate_ref.shape[0] // far, gate_ref.shape[2] // capacity
    for f in range(far):
        starts = [(c * far + f) * near for c in range(capacity)]
        row = jnp.concatenate([terms[:, i : i + near] for i in starts], axis=1)
        gate_ref[f * copies : (f + 1) * copies] = jnp.broadcast_to(
            row[None], (copies, *row.shape)
        )


def down(left, disp_ref, out_ref, first):
    blocks, share, slots = disp_ref.shape
    wide = 2 * share
    for step in range(blocks // 2):
        block = disp_ref[2 * step : 2 * step + 2].reshape(wide, slots)
        part = lax.dot_general(
            left, block, (((1,), (1,)), ((), ())), preferred_element_type=F32
        )
        start = first + wide * step
        out_ref[:, start : start + wide] = part.astype(BF16)


def far_kernel(own_ref, later_ref, out_ref):
    down(later_ref[:, out_ref.shape[1] :], own_ref, out_ref, 0)


def rest_kernel(
    own_ref, other_ref, keep_ref, later_ref, values_ref, mine_ref, send_ref
):
    mine, slots = mine_ref.shape[1] // 2, values_ref.shape[1]
    down(later_ref[:, mine:], other_ref, send_ref, 0)
    values = values_ref[...]
    high = values.astype(BF16)
    send_ref[:, mine : mine + slots] = high
    send_ref[:, mine + slots :] = (values - high.astype(F32)).astype(BF16)
    for half, ref in enumerate((own_ref, other_ref)):
        down(keep_ref[:, 2 * mine :], ref, mine_ref, half * mine)


def finish_kernel(
    place_ref,
    own_ref,
    got_own_ref,
    got_other_ref,
    values_ref,
    order_ref,
    down_ref,
    dhid_ref,
):
    slots = values_ref.shape[1]
    mine = got_own_ref.shape[1]
    blocks = 4
    share = mine // blocks

    def store(far, core):
        for f in range(2):
            refs = ((own_ref, 0), (own_ref, mine))
            if f != far:
                refs = ((got_own_ref, 0), (got_other_ref, 0))
            refs = refs if core == 0 else refs[::-1]
            for y in range(blocks):
                starts = [(ref, first + share * y) for ref, first in refs]
                pair = [ref[:, start : start + share] for ref, start in starts]
                start = 2 * share * (f * blocks + y)
                down_ref[:, start : start + 2 * share] = jnp.concatenate(pair, axis=1)

    cases(place_ref, store)
    high = got_other_ref[:, mine : mine + slots].astype(F32)
    low = got_other_ref[:, mine + slots :].astype(F32)
    flipped = (values_ref[...] + (high + low)).T.astype(BF16)
    dhid_ref[...] = jnp.dot(
        order_ref[...], flipped, preferred_element_type=F32
    ).astype(BF16)


def sum_kernel(far, parts_ref, out_ref):
    near, width = out_ref.shape
    copies = parts_ref.shape[0] // far
    rows = []
    for f in range(far):
        terms = jnp.sum(parts_ref[f * copies : (f + 1) * copies], axis=0)
        for c in range(width // far):
            rows.append(terms[:, near * c : near * (c + 1)])
    out_ref[...] = jnp.concatenate(rows, axis=0).T


def gate_kernel(far, terms_ref, routes_ref, gates_ref, out_ref):
    near, width = terms_ref.shape
    capacity = width // far
    named, present, before = ranks(routes_ref[...], far * near)
    matched = jnp.zeros(present.shape, F32)
    for c in range(capacity):
        columns = [
            terms_ref[:, f * capacity + c : f * capacity + c + 1] for f in range(far)
        ]
        here = jnp.logical_and(present, before == c)
        matched = jnp.where(here, jnp.concatenate(columns, axis=0), matched)
    total = [jnp.sum(jnp.where(n, matched, 0.0), axis=0, keepdims=True) for n in named]
    out_ref[...] = jnp.concatenate(total, axis=0) / gates_ref[...]


def whole():
    return pl.BlockSpec(memory_space=pltpu.VMEM)


def scalar():
    return pl.BlockSpec(memory_space=pltpu.SMEM)


def stays():
    return pl.BlockSpec(memory_space=pltpu.HBM)


def in_hbm(x):
    return pltpu.with_memory_space_constraint(x, pltpu.HBM)


def in_vmem(x):
    return pltpu.with_memory_space_constraint(x, pltpu.VMEM)


def limit(mib):
    return pltpu.CompilerParams(vmem_limit_bytes=mib * 2**20)


def cost(flops, moved):
    return pl.CostEstimate(flops=flops, bytes_accessed=moved, transcendentals=0)


def swap_all(x, axis):
    return lax.all_to_all(x, axis, split_axis=0, concat_axis=0, tiled=True)


def on_device(grad_out, routes, gates, hidden, w_down):
    near, far = lax.axis_size("near"), lax.axis_size("far")
    experts, rows_y = near * far, lax.axis_size("y")
    _, slots, units = hidden.shape
    width = w_down.shape[2]
    capacity = slots // experts
    share = grad_out.shape[1]
    mine = rows_y * share
    place = jnp.stack([lax.axis_index("x"), lax.axis_index("core")]).astype(jnp.int32)
    routes, gates = routes.T, gates.T
    bf16 = functools.partial(pltpu.HBM, dtype=BF16)
    f32 = functools.partial(pltpu.HBM, dtype=F32)

    def other(x, axis):
        return lax.ppermute(x, axis, [(0, 1), (1, 0)])

    packed = pl.pallas_call(
        pack_kernel,
        out_shape=jax.ShapeDtypeStruct((experts, 2, capacity * share // 2), BF16),
        in_specs=[whole()] * 3,
        out_specs=whole(),
        name="pack",
    )(grad_out, routes, gates)
    arrived = swap_all(packed, ("far", "near"))

    keep, to_far, to_far_later, order = pl.pallas_call(
        functools.partial(split_kernel, experts),
        out_shape=(
            pltpu.VMEM((units, 2 * mine + slots), BF16),
            bf16((units, mine)),
            bf16((units, mine + slots)),
            bf16((slots, slots)),
        ),
        in_specs=[scalar(), whole(), whole()],
        out_specs=(whole(),) * 4,
        cost_estimate=cost(2 * units * slots * slots, 2 * 2 * units * width),
        name="split",
    )(place, w_down[0], hidden[0])
    from_far = other(to_far, "x")
    arrived, from_far, to_far_later = lax.optimization_barrier(
        (arrived, from_far, to_far_later)
    )
    later = other(to_far_later, "x")

    copies = pl.pallas_call(
        unpack_kernel,
        out_shape=bf16((rows_y, share, slots)),
        in_specs=[whole()],
        out_specs=pl.BlockSpec(memory_space=pl.ANY),
        scratch_shapes=[
            pltpu.VMEM((share, slots), BF16),
            pltpu.SemaphoreType.DMA((rows_y,)),
        ],
        compiler_params=limit(8),
        name="unpack",
    )(arrived)
    dispatched, later = lax.optimization_barrier((swap_all(copies, "y"), later))
    from_core = other(dispatched, "core")
    dispatched = in_vmem(dispatched)

    keep, from_far, later = in_vmem(keep), in_hbm(from_far), in_vmem(later)
    flops = 2 * slots * units * width
    moved = slots * width + 2 * units * width
    back_own = pl.pallas_call(
        far_kernel,
        out_shape=bf16((units, mine)),
        in_specs=[whole()] * 2,
        out_specs=whole(),
        compiler_params=limit(16),
        cost_estimate=cost(flops // 4, moved // 4),
        name="far",
    )(dispatched, later)
    from_core, _ = lax.optimization_barrier((from_core, back_own))
    got_own = other(back_own, "x")

    mine_values, theirs, terms = pl.pallas_call(
        functools.partial(values_kernel, far, capacity),
        out_shape=(
            f32((units, slots)),
            f32((units, slots)),
            jax.ShapeDtypeStruct((far * 4 * rows_y, 1, capacity * near), F32),
        ),
        in_specs=[whole()] * 3 + [stays(), whole()],
        out_specs=(whole(),) * 3,
        scratch_shapes=[pltpu.VMEM((units, mine), BF16), pltpu.SemaphoreType.DMA],
        compiler_params=limit(16),
        cost_estimate=cost(flops, moved),
        name="values",
    )(dispatched, in_vmem(from_core), keep, from_far, later)
    parts = swap_all(terms, ("far", "x", "y", "core"))

    down_mine, back_other = pl.pallas_call(
        rest_kernel,
        out_shape=(bf16((units, 2 * mine)), bf16((units, mine + 2 * slots))),
        in_specs=[whole()] * 5,
        out_specs=(whole(),) * 2,
        compiler_params=limit(16),
        cost_estimate=cost(3 * flops // 4, moved // 2),
        name="rest",
    )(dispatched, in_vmem(from_core), keep, later, in_hbm(theirs))
    parts, back_other, got_own = lax.optimization_barrier((parts, back_other, got_own))
    got_other = other(back_other, "x")

    d_down, d_hidden = pl.pallas_call(
        finish_kernel,
        out_shape=(
            jax.ShapeDtypeStruct((units, width), BF16),
            jax.ShapeDtypeStruct((slots, units), BF16),
        ),
        in_specs=[scalar()] + [whole()] * 5,
        out_specs=(whole(),) * 2,
        compiler_params=limit(16),
        cost_estimate=cost(2 * units * slots * slots, 4 * units * width),
        name="finish",
    )(
        place,
        in_hbm(down_mine),
        in_vmem(got_own),
        in_vmem(got_other),
        in_hbm(mine_values),
        in_hbm(order),
    )

    sums = pl.pallas_call(
        functools.partial(sum_kernel, far),
        out_shape=jax.ShapeDtypeStruct((near, far * capacity), F32),
        in_specs=[whole()],
        out_specs=whole(),
        compiler_params=limit(4),
        name="sum",
    )(parts)
    returned = swap_all(sums, "near")
    returned, _ = lax.optimization_barrier((returned, d_hidden))
    d_gate = pl.pallas_call(
        functools.partial(gate_kernel, far),
        out_shape=jax.ShapeDtypeStruct(gates.shape, F32),
        in_specs=[whole()] * 3,
        out_specs=whole(),
        compiler_params=limit(4),
        name="match",
    )(returned, routes, gates)
    return (d_hidden[None], d_down[None], d_gate.T)


def solution(mesh):
    parts, experts = mesh.devices.shape
    devices = mesh.devices.reshape(2, parts // 4, 2, 2, experts // 2)
    finer = Mesh(devices, ("x", "y", "core", "far", "near"))
    dp, expert = ("x", "y", "core"), ("far", "near")
    in_specs = (
        P(expert, dp),
        P(expert, None),
        P(expert, None),
        P(expert, None, dp),
        P(expert, dp, None),
    )
    out_specs = (P(expert, None, dp), P(expert, dp, None), P(expert, None))
    return jax.shard_map(
        on_device, mesh=finer, in_specs=in_specs, out_specs=out_specs, check_vma=False
    )
```

```python
import functools

import jax
import jax.numpy as jnp
from jax import lax
from jax.experimental import pallas as pl
from jax.experimental.pallas import tpu as pltpu
from jax.sharding import Mesh, PartitionSpec as P

F32 = jnp.float32
BF16 = jnp.bfloat16
LANES = 128


def ranks(routes, experts):
    top, tokens = routes.shape
    ids = lax.broadcasted_iota(jnp.int32, (experts, tokens), 0)
    named = [routes[k : k + 1, :] == ids for k in range(top)]
    present = functools.reduce(jnp.logical_or, named)
    rows = lax.broadcasted_iota(jnp.int32, (tokens, tokens), 0)
    columns = lax.broadcasted_iota(jnp.int32, (tokens, tokens), 1)
    earlier = (rows < columns).astype(F32)
    before = jnp.dot(present.astype(F32), earlier, preferred_element_type=F32)
    return named, present, before


def pack_kernel(grad_ref, routes_ref, gates_ref, out_ref):
    experts, lines, length = out_ref.shape
    grad = grad_ref[...]
    fitting = length // grad.shape[1]
    named, present, before = ranks(routes_ref[...], experts)
    gates = gates_ref[...]
    gate = jnp.zeros(present.shape, F32)
    for k, here in enumerate(named):
        gate = jnp.where(here, gates[k : k + 1, :], gate)

    def slot(c):
        placed = jnp.logical_and(present, before == c).astype(F32)
        row_gate = jnp.sum(placed * gate, axis=1, keepdims=True)
        return row_gate * jnp.dot(
            placed.astype(BF16), grad, preferred_element_type=F32
        )

    for line in range(lines):
        rows = [slot(fitting * line + i) for i in range(fitting)]
        out_ref[:, line, :] = jnp.concatenate(rows, axis=1).astype(BF16)


def unpack_kernel(in_ref, out_ref, flipped, done):
    sources, lines, length = in_ref.shape
    share, slots = flipped.shape
    fitting = length // share
    rows = [in_ref[:, line, :].astype(F32) for line in range(lines)]
    group = LANES // sources
    for g in range(slots // LANES):
        parts = []
        for c in range(g * group, (g + 1) * group):
            start = share * (c % fitting)
            parts.append(rows[c // fitting][:, start : start + share])
        block = jnp.concatenate(parts, axis=0)
        flipped[:, LANES * g : LANES * (g + 1)] = block.T.astype(BF16)
    copies = [
        pltpu.make_async_copy(flipped, out_ref.at[i], done.at[i])
        for i in range(out_ref.shape[0])
    ]
    for copy in copies:
        copy.start()
    for copy in copies:
        copy.wait()


def cases(place_ref, body):
    for far in range(2):
        for core in range(2):
            here = jnp.logical_and(place_ref[0] == far, place_ref[1] == core)
            pl.when(here)(functools.partial(body, far, core))


def columns(far, core, y, blocks, share):
    start = ((far * blocks + y) * 2 + core) * share
    return slice(start, start + share)


def split_kernel(
    sources,
    place_ref,
    weight_ref,
    hidden_ref,
    keep_ref,
    far_ref,
    later_ref,
    order_ref,
):
    slots = hidden_ref.shape[0]
    all_mine = keep_ref.shape[1] - slots
    blocks = 4
    share = all_mine // (2 * blocks)
    capacity = slots // sources
    rows = lax.broadcasted_iota(jnp.int32, (slots, slots), 0)
    cols = lax.broadcasted_iota(jnp.int32, (slots, slots), 1)
    matches = (rows % capacity) * sources + rows // capacity == cols
    order = matches.astype(F32).astype(BF16)
    order_ref[...] = order
    flipped = lax.dot_general(
        hidden_ref[...], order, (((0,), (0,)), ((), ())), preferred_element_type=F32
    ).astype(BF16)

    mine = blocks * share

    def store(far, core):
        def part(f, c):
            pieces = [
                weight_ref[:, columns(f, c, y, blocks, share)] for y in range(blocks)
            ]
            return jnp.concatenate(pieces, axis=1)

        keep_ref[:, :mine] = part(far, core)
        keep_ref[:, mine:all_mine] = part(far, 1 - core)
        keep_ref[:, all_mine:] = flipped
        far_ref[...] = part(1 - far, core)[:, : far_ref.shape[1]]
        later_ref[:, :mine] = part(1 - far, 1 - core)
        later_ref[:, mine : mine + slots] = flipped
        behind = mine + slots
        later_ref[:, later_ref.shape[1] - LANES :] = jnp.zeros(
            (later_ref.shape[0], LANES), BF16
        )
        later_ref[:, behind : behind + share] = part(1 - far, core)[:, mine - share :]

    cases(place_ref, store)


def values_kernel(
    far,
    capacity,
    own_ref,
    other_ref,
    keep_ref,
    far_ref,
    later_ref,
    mine_ref,
    theirs_ref,
    gate_ref,
    weight,
    done,
):
    blocks, share, slots = own_ref.shape
    units, mine = mine_ref.shape[0], blocks * share
    copy = pltpu.make_async_copy(far_ref, weight, done)
    copy.start()

    def times(rows, ref):
        return jnp.dot(
            rows,
            ref.reshape(ref.shape[0] * share, slots),
            preferred_element_type=F32,
        )

    values = [
        times(keep_ref[:, :mine], own_ref[...])
        + times(keep_ref[:, mine : 2 * mine], other_ref[...])
    ]
    behind = times(later_ref[:, :mine], other_ref[...])
    after = mine + slots
    behind += times(later_ref[:, after : after + share], own_ref[blocks - 1 :])
    copy.wait()
    values.append(times(weight[:, : mine - share], own_ref[: blocks - 1]) + behind)
    values = jnp.concatenate(values, axis=0)
    left = [keep_ref[:, 2 * mine :], later_ref[:, mine : mine + slots]]
    left = jnp.concatenate(left, axis=0).astype(F32)
    terms = jnp.sum(left * values, axis=0, keepdims=True)
    mine_ref[...] = values[:units]
    theirs_ref[...] = values[units:]
    copies, near = gate_ref.shape[0] // far, gate_ref.shape[2] // capacity
    for f in range(far):
        starts = [(c * far + f) * near for c in range(capacity)]
        row = jnp.concatenate([terms[:, i : i + near] for i in starts], axis=1)
        gate_ref[f * copies : (f + 1) * copies] = jnp.broadcast_to(
            row[None], (copies, *row.shape)
        )


def down(left, disp_ref, out_ref, first):
    blocks, share, slots = disp_ref.shape
    wide = 2 * share
    for step in range(blocks // 2):
        block = disp_ref[2 * step : 2 * step + 2].reshape(wide, slots)
        part = lax.dot_general(
            left, block, (((1,), (1,)), ((), ())), preferred_element_type=F32
        )
        start = first + wide * step
        out_ref[:, start : start + wide] = part.astype(BF16)


def far_kernel(own_ref, later_ref, out_ref):
    mine, slots = out_ref.shape[1], own_ref.shape[2]
    down(later_ref[:, mine : mine + slots], own_ref, out_ref, 0)


def rest_kernel(
    own_ref, other_ref, keep_ref, later_ref, values_ref, mine_ref, send_ref
):
    mine, slots = mine_ref.shape[1] // 2, values_ref.shape[1]
    down(later_ref[:, mine : mine + slots], other_ref, send_ref, 0)
    values = values_ref[...]
    high = values.astype(BF16)
    send_ref[:, mine : mine + slots] = high
    send_ref[:, mine + slots :] = (values - high.astype(F32)).astype(BF16)
    for half, ref in enumerate((own_ref, other_ref)):
        down(keep_ref[:, 2 * mine :], ref, mine_ref, half * mine)


def finish_kernel(
    place_ref,
    own_ref,
    got_own_ref,
    got_other_ref,
    values_ref,
    order_ref,
    down_ref,
    dhid_ref,
):
    slots = values_ref.shape[1]
    mine = got_own_ref.shape[1]
    blocks = 4
    share = mine // blocks

    def store(far, core):
        for f in range(2):
            refs = ((own_ref, 0), (own_ref, mine))
            if f != far:
                refs = ((got_own_ref, 0), (got_other_ref, 0))
            refs = refs if core == 0 else refs[::-1]
            for y in range(blocks):
                starts = [(ref, first + share * y) for ref, first in refs]
                pair = [ref[:, start : start + share] for ref, start in starts]
                start = 2 * share * (f * blocks + y)
                down_ref[:, start : start + 2 * share] = jnp.concatenate(pair, axis=1)

    cases(place_ref, store)
    high = got_other_ref[:, mine : mine + slots].astype(F32)
    low = got_other_ref[:, mine + slots :].astype(F32)
    flipped = (values_ref[...] + (high + low)).T.astype(BF16)
    dhid_ref[...] = jnp.dot(
        order_ref[...], flipped, preferred_element_type=F32
    ).astype(BF16)


def sum_kernel(far, parts_ref, out_ref):
    near, width = out_ref.shape
    copies = parts_ref.shape[0] // far
    rows = []
    for f in range(far):
        terms = jnp.sum(parts_ref[f * copies : (f + 1) * copies], axis=0)
        for c in range(width // far):
            rows.append(terms[:, near * c : near * (c + 1)])
    out_ref[...] = jnp.concatenate(rows, axis=0).T


def gate_kernel(far, terms_ref, routes_ref, gates_ref, out_ref):
    near, width = terms_ref.shape
    capacity = width // far
    named, present, before = ranks(routes_ref[...], far * near)
    matched = jnp.zeros(present.shape, F32)
    for c in range(capacity):
        columns = [
            terms_ref[:, f * capacity + c : f * capacity + c + 1] for f in range(far)
        ]
        here = jnp.logical_and(present, before == c)
        matched = jnp.where(here, jnp.concatenate(columns, axis=0), matched)
    total = [jnp.sum(jnp.where(n, matched, 0.0), axis=0, keepdims=True) for n in named]
    out_ref[...] = jnp.concatenate(total, axis=0) / gates_ref[...]


def whole():
    return pl.BlockSpec(memory_space=pltpu.VMEM)


def scalar():
    return pl.BlockSpec(memory_space=pltpu.SMEM)


def stays():
    return pl.BlockSpec(memory_space=pltpu.HBM)


def lanes(width):
    return -(-width // LANES) * LANES


def in_hbm(x):
    return pltpu.with_memory_space_constraint(x, pltpu.HBM)


def in_vmem(x):
    return pltpu.with_memory_space_constraint(x, pltpu.VMEM)


def limit(mib):
    return pltpu.CompilerParams(vmem_limit_bytes=mib * 2**20)


def cost(flops, moved):
    return pl.CostEstimate(flops=flops, bytes_accessed=moved, transcendentals=0)


def swap_all(x, axis):
    return lax.all_to_all(x, axis, split_axis=0, concat_axis=0, tiled=True)


def on_device(grad_out, routes, gates, hidden, w_down):
    near, far = lax.axis_size("near"), lax.axis_size("far")
    experts, rows_y = near * far, lax.axis_size("y")
    _, slots, units = hidden.shape
    width = w_down.shape[2]
    capacity = slots // experts
    share = grad_out.shape[1]
    mine = rows_y * share
    place = jnp.stack([lax.axis_index("x"), lax.axis_index("core")]).astype(jnp.int32)
    routes, gates = routes.T, gates.T
    bf16 = functools.partial(pltpu.HBM, dtype=BF16)
    f32 = functools.partial(pltpu.HBM, dtype=F32)

    def other(x, axis):
        return lax.ppermute(x, axis, [(0, 1), (1, 0)])

    packed = pl.pallas_call(
        pack_kernel,
        out_shape=jax.ShapeDtypeStruct((experts, 2, capacity * share // 2), BF16),
        in_specs=[whole()] * 3,
        out_specs=whole(),
        name="pack",
    )(grad_out, routes, gates)
    arrived = swap_all(packed, ("far", "near"))

    keep, to_far, to_far_later, order = pl.pallas_call(
        functools.partial(split_kernel, experts),
        out_shape=(
            pltpu.VMEM((units, 2 * mine + slots), BF16),
            bf16((units, lanes(mine - share))),
            bf16((units, mine + slots + lanes(share))),
            bf16((slots, slots)),
        ),
        in_specs=[scalar(), whole(), whole()],
        out_specs=(whole(),) * 4,
        cost_estimate=cost(2 * units * slots * slots, 2 * 2 * units * width),
        name="split",
    )(place, w_down[0], hidden[0])
    from_far = other(to_far, "x")
    arrived, from_far, to_far_later = lax.optimization_barrier(
        (arrived, from_far, to_far_later)
    )
    later = other(to_far_later, "x")

    copies = pl.pallas_call(
        unpack_kernel,
        out_shape=bf16((rows_y, share, slots)),
        in_specs=[whole()],
        out_specs=pl.BlockSpec(memory_space=pl.ANY),
        scratch_shapes=[
            pltpu.VMEM((share, slots), BF16),
            pltpu.SemaphoreType.DMA((rows_y,)),
        ],
        compiler_params=limit(8),
        name="unpack",
    )(arrived)
    dispatched, later = lax.optimization_barrier((swap_all(copies, "y"), later))
    from_core = other(dispatched, "core")
    dispatched = in_vmem(dispatched)

    keep, from_far, later = in_vmem(keep), in_hbm(from_far), in_vmem(later)
    flops = 2 * slots * units * width
    moved = slots * width + 2 * units * width
    back_own = pl.pallas_call(
        far_kernel,
        out_shape=bf16((units, mine)),
        in_specs=[whole()] * 2,
        out_specs=whole(),
        compiler_params=limit(16),
        cost_estimate=cost(flops // 4, moved // 4),
        name="far",
    )(dispatched, later)
    from_core, _ = lax.optimization_barrier((from_core, back_own))
    got_own = other(back_own, "x")

    mine_values, theirs, terms = pl.pallas_call(
        functools.partial(values_kernel, far, capacity),
        out_shape=(
            f32((units, slots)),
            f32((units, slots)),
            jax.ShapeDtypeStruct((far * 4 * rows_y, 1, capacity * near), F32),
        ),
        in_specs=[whole()] * 3 + [stays(), whole()],
        out_specs=(whole(),) * 3,
        scratch_shapes=[
            pltpu.VMEM((units, lanes(mine - share)), BF16),
            pltpu.SemaphoreType.DMA,
        ],
        compiler_params=limit(16),
        cost_estimate=cost(flops, moved),
        name="values",
    )(dispatched, in_vmem(from_core), keep, from_far, later)
    parts = swap_all(terms, ("far", "x", "y", "core"))

    down_mine, back_other = pl.pallas_call(
        rest_kernel,
        out_shape=(bf16((units, 2 * mine)), bf16((units, mine + 2 * slots))),
        in_specs=[whole()] * 5,
        out_specs=(whole(),) * 2,
        compiler_params=limit(16),
        cost_estimate=cost(3 * flops // 4, moved // 2),
        name="rest",
    )(dispatched, in_vmem(from_core), keep, later, in_hbm(theirs))
    parts, back_other, got_own = lax.optimization_barrier((parts, back_other, got_own))
    got_other = other(back_other, "x")

    d_down, d_hidden = pl.pallas_call(
        finish_kernel,
        out_shape=(
            jax.ShapeDtypeStruct((units, width), BF16),
            jax.ShapeDtypeStruct((slots, units), BF16),
        ),
        in_specs=[scalar()] + [whole()] * 5,
        out_specs=(whole(),) * 2,
        compiler_params=limit(16),
        cost_estimate=cost(2 * units * slots * slots, 4 * units * width),
        name="finish",
    )(
        place,
        in_hbm(down_mine),
        in_vmem(got_own),
        in_vmem(got_other),
        in_hbm(mine_values),
        in_hbm(order),
    )

    sums = pl.pallas_call(
        functools.partial(sum_kernel, far),
        out_shape=jax.ShapeDtypeStruct((near, far * capacity), F32),
        in_specs=[whole()],
        out_specs=whole(),
        compiler_params=limit(4),
        name="sum",
    )(parts)
    returned = swap_all(sums, "near")
    returned, _ = lax.optimization_barrier((returned, d_hidden))
    d_gate = pl.pallas_call(
        functools.partial(gate_kernel, far),
        out_shape=jax.ShapeDtypeStruct(gates.shape, F32),
        in_specs=[whole()] * 3,
        out_specs=whole(),
        compiler_params=limit(4),
        name="match",
    )(returned, routes, gates)
    return (d_hidden[None], d_down[None], d_gate.T)


def solution(mesh):
    parts, experts = mesh.devices.shape
    devices = mesh.devices.reshape(2, parts // 4, 2, 2, experts // 2)
    finer = Mesh(devices, ("x", "y", "core", "far", "near"))
    dp, expert = ("x", "y", "core"), ("far", "near")
    in_specs = (
        P(expert, dp),
        P(expert, None),
        P(expert, None),
        P(expert, None, dp),
        P(expert, dp, None),
    )
    out_specs = (P(expert, None, dp), P(expert, dp, None), P(expert, None))
    return jax.shard_map(
        on_device, mesh=finer, in_specs=in_specs, out_specs=out_specs, check_vma=False
    )
```

```python
import functools

import jax
import jax.numpy as jnp
from jax import lax
from jax.experimental import pallas as pl
from jax.experimental.pallas import tpu as pltpu
from jax.sharding import Mesh, PartitionSpec as P

F32 = jnp.float32
BF16 = jnp.bfloat16
LANES = 128


def ranks(routes, experts):
    top, tokens = routes.shape
    ids = lax.broadcasted_iota(jnp.int32, (experts, tokens), 0)
    named = [routes[k : k + 1, :] == ids for k in range(top)]
    present = functools.reduce(jnp.logical_or, named)
    rows = lax.broadcasted_iota(jnp.int32, (tokens, tokens), 0)
    columns = lax.broadcasted_iota(jnp.int32, (tokens, tokens), 1)
    earlier = (rows < columns).astype(F32)
    before = jnp.dot(present.astype(F32), earlier, preferred_element_type=F32)
    return named, present, before


def pack_kernel(grad_ref, routes_ref, gates_ref, out_ref):
    experts, lines, length = out_ref.shape
    grad = grad_ref[...]
    fitting = length // grad.shape[1]
    named, present, before = ranks(routes_ref[...], experts)
    gates = gates_ref[...]
    gate = jnp.zeros(present.shape, F32)
    for k, here in enumerate(named):
        gate = jnp.where(here, gates[k : k + 1, :], gate)

    capacity = lines * fitting
    placed = [jnp.logical_and(present, before == c).astype(F32) for c in range(capacity)]
    placed = jnp.concatenate(placed, axis=0)
    row_gate = jnp.sum(
        placed * jnp.concatenate([gate] * capacity, axis=0), axis=1, keepdims=True
    )
    scaled = row_gate * jnp.dot(
        placed.astype(BF16), grad, preferred_element_type=F32
    )
    for line in range(lines):
        rows = [
            scaled[experts * c : experts * (c + 1)]
            for c in range(fitting * line, fitting * (line + 1))
        ]
        out_ref[:, line, :] = jnp.concatenate(rows, axis=1).astype(BF16)


def unpack_kernel(in_ref, out_ref, flipped, done):
    sources, lines, length = in_ref.shape
    share, slots = flipped.shape
    fitting = length // share
    rows = [in_ref[:, line, :].astype(F32) for line in range(lines)]
    group = LANES // sources
    for g in range(slots // LANES):
        parts = []
        for c in range(g * group, (g + 1) * group):
            start = share * (c % fitting)
            parts.append(rows[c // fitting][:, start : start + share])
        block = jnp.concatenate(parts, axis=0)
        flipped[:, LANES * g : LANES * (g + 1)] = block.T.astype(BF16)
    copies = [
        pltpu.make_async_copy(flipped, out_ref.at[i], done.at[i])
        for i in range(out_ref.shape[0])
    ]
    for copy in copies:
        copy.start()
    for copy in copies:
        copy.wait()


def cases(place_ref, body):
    for far in range(2):
        for core in range(2):
            here = jnp.logical_and(place_ref[0] == far, place_ref[1] == core)
            pl.when(here)(functools.partial(body, far, core))


def columns(far, core, y, blocks, share):
    start = ((far * blocks + y) * 2 + core) * share
    return slice(start, start + share)


def split_kernel(
    sources,
    place_ref,
    weight_ref,
    hidden_ref,
    keep_ref,
    far_ref,
    later_ref,
    order_ref,
):
    slots = hidden_ref.shape[0]
    all_mine = keep_ref.shape[1] - slots
    blocks = 4
    share = all_mine // (2 * blocks)
    capacity = slots // sources
    rows = lax.broadcasted_iota(jnp.int32, (slots, slots), 0)
    cols = lax.broadcasted_iota(jnp.int32, (slots, slots), 1)
    matches = (rows % capacity) * sources + rows // capacity == cols
    order = matches.astype(F32).astype(BF16)
    order_ref[...] = order
    flipped = lax.dot_general(
        hidden_ref[...], order, (((0,), (0,)), ((), ())), preferred_element_type=F32
    ).astype(BF16)

    mine = blocks * share

    def store(far, core):
        def part(f, c):
            pieces = [
                weight_ref[:, columns(f, c, y, blocks, share)] for y in range(blocks)
            ]
            return jnp.concatenate(pieces, axis=1)

        keep_ref[:, :mine] = part(far, core)
        keep_ref[:, mine:all_mine] = part(far, 1 - core)
        keep_ref[:, all_mine:] = flipped
        far_ref[...] = part(1 - far, core)
        later_ref[:, :mine] = part(1 - far, 1 - core)
        later_ref[:, mine:] = flipped

    cases(place_ref, store)


def values_kernel(
    far,
    capacity,
    own_ref,
    other_ref,
    keep_ref,
    far_ref,
    later_ref,
    mine_ref,
    theirs_ref,
    gate_ref,
    weight,
    done,
):
    blocks, share, slots = own_ref.shape
    units, mine = mine_ref.shape[0], blocks * share
    copy = pltpu.make_async_copy(far_ref, weight, done)
    copy.start()
    values = []
    for first, second, start in ((keep_ref, keep_ref, mine), (weight, later_ref, 0)):
        if first is weight:
            copy.wait()
        values.append(
            jnp.dot(
                first[:, :mine],
                own_ref[...].reshape(mine, slots),
                preferred_element_type=F32,
            )
            + jnp.dot(
                second[:, start : start + mine],
                other_ref[...].reshape(mine, slots),
                preferred_element_type=F32,
            )
        )
    values = jnp.concatenate(values, axis=0)
    left = [keep_ref[:, 2 * mine :], later_ref[:, mine:]]
    left = jnp.concatenate(left, axis=0).astype(F32)
    terms = jnp.sum(left * values, axis=0, keepdims=True)
    mine_ref[...] = values[:units]
    theirs_ref[...] = values[units:]
    copies, near = gate_ref.shape[0] // far, gate_ref.shape[2] // capacity
    for f in range(far):
        starts = [(c * far + f) * near for c in range(capacity)]
        row = jnp.concatenate([terms[:, i : i + near] for i in starts], axis=1)
        gate_ref[f * copies : (f + 1) * copies] = jnp.broadcast_to(
            row[None], (copies, *row.shape)
        )


def down(left, disp_ref, out_ref, first):
    blocks, share, slots = disp_ref.shape
    wide = 2 * share
    for step in range(blocks // 2):
        block = disp_ref[2 * step : 2 * step + 2].reshape(wide, slots)
        part = lax.dot_general(
            left, block, (((1,), (1,)), ((), ())), preferred_element_type=F32
        )
        start = first + wide * step
        out_ref[:, start : start + wide] = part.astype(BF16)


def far_kernel(own_ref, later_ref, out_ref):
    down(later_ref[:, out_ref.shape[1] :], own_ref, out_ref, 0)


def rest_kernel(
    own_ref, other_ref, keep_ref, later_ref, values_ref, mine_ref, send_ref
):
    mine, slots = mine_ref.shape[1] // 2, values_ref.shape[1]
    down(later_ref[:, mine:], other_ref, send_ref, 0)
    values = values_ref[...]
    high = values.astype(BF16)
    send_ref[:, mine : mine + slots] = high
    send_ref[:, mine + slots :] = (values - high.astype(F32)).astype(BF16)
    for half, ref in enumerate((own_ref, other_ref)):
        down(keep_ref[:, 2 * mine :], ref, mine_ref, half * mine)


def finish_kernel(
    place_ref,
    own_ref,
    got_own_ref,
    got_other_ref,
    values_ref,
    order_ref,
    down_ref,
    dhid_ref,
):
    slots = values_ref.shape[1]
    mine = got_own_ref.shape[1]
    blocks = 4
    share = mine // blocks

    def store(far, core):
        for f in range(2):
            refs = ((own_ref, 0), (own_ref, mine))
            if f != far:
                refs = ((got_own_ref, 0), (got_other_ref, 0))
            refs = refs if core == 0 else refs[::-1]
            for y in range(blocks):
                starts = [(ref, first + share * y) for ref, first in refs]
                pair = [ref[:, start : start + share] for ref, start in starts]
                start = 2 * share * (f * blocks + y)
                down_ref[:, start : start + 2 * share] = jnp.concatenate(pair, axis=1)

    cases(place_ref, store)
    high = got_other_ref[:, mine : mine + slots].astype(F32)
    low = got_other_ref[:, mine + slots :].astype(F32)
    flipped = (values_ref[...] + (high + low)).T.astype(BF16)
    dhid_ref[...] = jnp.dot(
        order_ref[...], flipped, preferred_element_type=F32
    ).astype(BF16)


def sum_kernel(far, parts_ref, out_ref):
    near, width = out_ref.shape
    copies = parts_ref.shape[0] // far
    rows = []
    for f in range(far):
        terms = jnp.sum(parts_ref[f * copies : (f + 1) * copies], axis=0)
        for c in range(width // far):
            rows.append(terms[:, near * c : near * (c + 1)])
    out_ref[...] = jnp.concatenate(rows, axis=0).T


def gate_kernel(far, terms_ref, routes_ref, gates_ref, out_ref):
    near, width = terms_ref.shape
    capacity = width // far
    named, present, before = ranks(routes_ref[...], far * near)
    matched = jnp.zeros(present.shape, F32)
    for c in range(capacity):
        columns = [
            terms_ref[:, f * capacity + c : f * capacity + c + 1] for f in range(far)
        ]
        here = jnp.logical_and(present, before == c)
        matched = jnp.where(here, jnp.concatenate(columns, axis=0), matched)
    total = [jnp.sum(jnp.where(n, matched, 0.0), axis=0, keepdims=True) for n in named]
    out_ref[...] = jnp.concatenate(total, axis=0) / gates_ref[...]


def whole():
    return pl.BlockSpec(memory_space=pltpu.VMEM)


def scalar():
    return pl.BlockSpec(memory_space=pltpu.SMEM)


def stays():
    return pl.BlockSpec(memory_space=pltpu.HBM)


def in_hbm(x):
    return pltpu.with_memory_space_constraint(x, pltpu.HBM)


def in_vmem(x):
    return pltpu.with_memory_space_constraint(x, pltpu.VMEM)


def limit(mib):
    return pltpu.CompilerParams(vmem_limit_bytes=mib * 2**20)


def cost(flops, moved):
    return pl.CostEstimate(flops=flops, bytes_accessed=moved, transcendentals=0)


def swap_all(x, axis):
    return lax.all_to_all(x, axis, split_axis=0, concat_axis=0, tiled=True)


def on_device(grad_out, routes, gates, hidden, w_down):
    near, far = lax.axis_size("near"), lax.axis_size("far")
    experts, rows_y = near * far, lax.axis_size("y")
    _, slots, units = hidden.shape
    width = w_down.shape[2]
    capacity = slots // experts
    share = grad_out.shape[1]
    mine = rows_y * share
    place = jnp.stack([lax.axis_index("x"), lax.axis_index("core")]).astype(jnp.int32)
    routes, gates = routes.T, gates.T
    bf16 = functools.partial(pltpu.HBM, dtype=BF16)
    f32 = functools.partial(pltpu.HBM, dtype=F32)

    def other(x, axis):
        return lax.ppermute(x, axis, [(0, 1), (1, 0)])

    packed = pl.pallas_call(
        pack_kernel,
        out_shape=jax.ShapeDtypeStruct((experts, 2, capacity * share // 2), BF16),
        in_specs=[whole()] * 3,
        out_specs=whole(),
        name="pack",
    )(grad_out, routes, gates)
    arrived = swap_all(packed, ("far", "near"))

    keep, to_far, to_far_later, order = pl.pallas_call(
        functools.partial(split_kernel, experts),
        out_shape=(
            pltpu.VMEM((units, 2 * mine + slots), BF16),
            bf16((units, mine)),
            bf16((units, mine + slots)),
            bf16((slots, slots)),
        ),
        in_specs=[scalar(), whole(), whole()],
        out_specs=(whole(),) * 4,
        cost_estimate=cost(2 * units * slots * slots, 2 * 2 * units * width),
        name="split",
    )(place, w_down[0], hidden[0])
    from_far = other(to_far, "x")
    arrived, from_far, to_far_later = lax.optimization_barrier(
        (arrived, from_far, to_far_later)
    )
    later = other(to_far_later, "x")

    copies = pl.pallas_call(
        unpack_kernel,
        out_shape=bf16((rows_y, share, slots)),
        in_specs=[whole()],
        out_specs=pl.BlockSpec(memory_space=pl.ANY),
        scratch_shapes=[
            pltpu.VMEM((share, slots), BF16),
            pltpu.SemaphoreType.DMA((rows_y,)),
        ],
        compiler_params=limit(8),
        name="unpack",
    )(arrived)
    dispatched, later = lax.optimization_barrier((swap_all(copies, "y"), later))
    from_core = other(dispatched, "core")
    dispatched = in_vmem(dispatched)

    keep, from_far, later = in_vmem(keep), in_hbm(from_far), in_vmem(later)
    flops = 2 * slots * units * width
    moved = slots * width + 2 * units * width
    back_own = pl.pallas_call(
        far_kernel,
        out_shape=bf16((units, mine)),
        in_specs=[whole()] * 2,
        out_specs=whole(),
        compiler_params=limit(16),
        cost_estimate=cost(flops // 4, moved // 4),
        name="far",
    )(dispatched, later)
    from_core, _ = lax.optimization_barrier((from_core, back_own))
    got_own = other(back_own, "x")

    mine_values, theirs, terms = pl.pallas_call(
        functools.partial(values_kernel, far, capacity),
        out_shape=(
            f32((units, slots)),
            f32((units, slots)),
            jax.ShapeDtypeStruct((far * 4 * rows_y, 1, capacity * near), F32),
        ),
        in_specs=[whole()] * 3 + [stays(), whole()],
        out_specs=(whole(),) * 3,
        scratch_shapes=[pltpu.VMEM((units, mine), BF16), pltpu.SemaphoreType.DMA],
        compiler_params=limit(16),
        cost_estimate=cost(flops, moved),
        name="values",
    )(dispatched, in_vmem(from_core), keep, from_far, later)
    parts = swap_all(terms, ("far", "x", "y", "core"))

    down_mine, back_other = pl.pallas_call(
        rest_kernel,
        out_shape=(bf16((units, 2 * mine)), bf16((units, mine + 2 * slots))),
        in_specs=[whole()] * 5,
        out_specs=(whole(),) * 2,
        compiler_params=limit(16),
        cost_estimate=cost(3 * flops // 4, moved // 2),
        name="rest",
    )(dispatched, in_vmem(from_core), keep, later, in_hbm(theirs))
    parts, back_other, got_own = lax.optimization_barrier((parts, back_other, got_own))
    got_other = other(back_other, "x")

    d_down, d_hidden = pl.pallas_call(
        finish_kernel,
        out_shape=(
            jax.ShapeDtypeStruct((units, width), BF16),
            jax.ShapeDtypeStruct((slots, units), BF16),
        ),
        in_specs=[scalar()] + [whole()] * 5,
        out_specs=(whole(),) * 2,
        compiler_params=limit(16),
        cost_estimate=cost(2 * units * slots * slots, 4 * units * width),
        name="finish",
    )(
        place,
        in_hbm(down_mine),
        in_vmem(got_own),
        in_vmem(got_other),
        in_hbm(mine_values),
        in_hbm(order),
    )

    sums = pl.pallas_call(
        functools.partial(sum_kernel, far),
        out_shape=jax.ShapeDtypeStruct((near, far * capacity), F32),
        in_specs=[whole()],
        out_specs=whole(),
        compiler_params=limit(4),
        name="sum",
    )(parts)
    returned = swap_all(sums, "near")
    returned, _ = lax.optimization_barrier((returned, d_hidden))
    d_gate = pl.pallas_call(
        functools.partial(gate_kernel, far),
        out_shape=jax.ShapeDtypeStruct(gates.shape, F32),
        in_specs=[whole()] * 3,
        out_specs=whole(),
        compiler_params=limit(4),
        name="match",
    )(returned, routes, gates)
    return (d_hidden[None], d_down[None], d_gate.T)


def solution(mesh):
    parts, experts = mesh.devices.shape
    devices = mesh.devices.reshape(2, parts // 4, 2, 2, experts // 2)
    finer = Mesh(devices, ("x", "y", "core", "far", "near"))
    dp, expert = ("x", "y", "core"), ("far", "near")
    in_specs = (
        P(expert, dp),
        P(expert, None),
        P(expert, None),
        P(expert, None, dp),
        P(expert, dp, None),
    )
    out_specs = (P(expert, None, dp), P(expert, dp, None), P(expert, None))
    return jax.shard_map(
        on_device, mesh=finer, in_specs=in_specs, out_specs=out_specs, check_vma=False
    )
```
